128 devices in a mesh: dp: 4 (over z_hi, core), expert: 32 (over y, x, z_lo).
Axes of the slice: x: 4, y: 4, z: 4 (z_hi: 2, z_lo: 2; z = z_hi * 2 + z_lo), core: 2. Of those that a mesh axis runs over, the one named last changes fastest.
Arguments:
- tokens: bfloat16 [256, 512, 1408], P(('dp', 'expert')), may hold values from -6 to 6
- slot_keys: bfloat16 [1408, 32], replicated, may hold values from -6 to 6
- logit_scale: float32 [1], replicated, may hold values from 20 to 40
- w_in: bfloat16 [32, 1408, 6144], P('expert', None, 'dp'), may hold values from -6 to 6
- w_out: bfloat16 [32, 6144, 1408], P('expert', 'dp'), may hold values from -0.078125 to 0.078125
- grad_out: bfloat16 [256, 512, 1408], P(('dp', 'expert')), may hold values from -6 to 6
Outputs:
- grad_tokens: bfloat16 [256, 512, 1408], P(('dp', 'expert'))
- grad_in: bfloat16 [32, 1408, 6144], P('expert', None, 'dp')
- grad_outw: bfloat16 [32, 6144, 1408], P('expert', 'dp')
- grad_keys: float32 [1408, 32], P(None, 'expert')
The draws below stay inside these ranges and needn't reach their ends.
All inputs are finite; a program needn't handle non-finite values.
Results may differ from the reference program's by a relative error of at most 0.011.
Values may be sent and summed in bfloat16 or wider, within the bound.
A program may use at most 128 MiB of HBM per device.

```python
import math
import jax
import jax.numpy as jnp
from jax import lax

D = 1408
HID = 6144
TOK = 512
EXPERTS = 32
IMAGES = 256


def steps_of(stream_key, dims, cuts, least, largest):
    loudness, own = 1.0, jax.random.fold_in(stream_key, 6)
    for dim, shards_of in cuts:
        draws = jnp.exp(jax.random.uniform(jax.random.fold_in(own, dim), (shards_of,), jnp.float32, least / len(cuts), largest / len(cuts)))
        loudness = loudness * jnp.repeat(draws, dims[dim] // shards_of).reshape([-1 if axis == dim else 1 for axis in range(len(dims))])
    return loudness


def bell_draw(rng, extent, spread, bound, split=(), dtype=jnp.bfloat16):
    drawn = spread * jax.random.normal(rng, extent, jnp.float32)
    if split:
        drawn = drawn * steps_of(rng, extent, split, -0.22, 0.18)
    return jnp.clip(drawn, -bound, bound).astype(dtype)


def setup_inputs(seed: int = 0) -> dict:
    arg_keys = jax.random.split(jax.random.key(seed), 7)
    tokens = bell_draw(arg_keys[0], (IMAGES, TOK, D), 1.0, 6.0, ((0, 128),))
    slot_keys = bell_draw(arg_keys[1], (D, EXPERTS), 1.0, 6.0)
    logit_scale = jnp.clip(jnp.exp(jax.random.uniform(arg_keys[2], (1,), jnp.float32, math.log(20.0), math.log(40.0))), 20.0, 40.0)
    w_in = bell_draw(arg_keys[3], (EXPERTS, D, HID), (0.5 * (2 * TOK) ** 0.5 * D ** -0.5), 6.0, ((0, 32), (2, 4)))
    w_out = bell_draw(arg_keys[4], (EXPERTS, HID, D), HID ** -0.5, 0.078125, ((0, 32), (1, 4)))
    grad_out = bell_draw(arg_keys[5], (IMAGES, TOK, D), 1.0, 6.0, ((0, 128),))
    return {"tokens": tokens, "slot_keys": slot_keys, "logit_scale": logit_scale, "w_in": w_in, "w_out": w_out, "grad_out": grad_out}


EPS = 1e-06

def normalize(v, axis):
    return v * lax.rsqrt(lax.optimization_barrier(jnp.sum(v * v, axis=axis, keepdims=True)) + EPS)

def gelu_exact(v):
    return 0.5 * v * (1.0 + lax.erf(v * 0.7071067811865476))

def gelu_slope(v):
    return 0.5 * (1.0 + lax.erf(v * 0.7071067811865476)) + v * jnp.exp(-0.5 * v * v) * 0.3989422804014327

def routing(image, keys, scale):
    normed = normalize(image.astype(jnp.float32), -1).astype(jnp.bfloat16)
    expo = jnp.exp(scale * jnp.dot(normed, keys, preferred_element_type=jnp.float32))
    dispatch = expo / lax.optimization_barrier(jnp.sum(expo, axis=0, keepdims=True))
    combine = expo / lax.optimization_barrier(jnp.sum(expo, axis=1, keepdims=True))
    return (normed, dispatch, combine)

def reference(tokens, slot_keys, logit_scale, w_in, w_out, grad_out):
    scale = logit_scale[0]
    key_float = slot_keys.astype(jnp.float32)
    keys = normalize(key_float, 0).astype(jnp.bfloat16)

    def forward_image(pair):
        image, cotan = pair
        normed, dispatch, combine = routing(image, keys, scale)
        slot_in = jnp.dot(dispatch.astype(jnp.bfloat16).T, image, preferred_element_type=jnp.float32)
        slot_grad = jnp.dot(combine.astype(jnp.bfloat16).T, cotan, preferred_element_type=jnp.float32)
        return (slot_in.astype(jnp.bfloat16), slot_grad.astype(jnp.bfloat16))
    slot_in, slot_grad = lax.map(forward_image, (tokens, grad_out))

    def expert_work(items):
        inputs, grads, first, second = items
        pre = jnp.dot(inputs, first, preferred_element_type=jnp.float32)
        act = gelu_exact(pre).astype(jnp.bfloat16)
        outputs = jnp.dot(act, second, preferred_element_type=jnp.float32).astype(jnp.bfloat16)
        hidden_grad = jnp.dot(grads, second.T, preferred_element_type=jnp.float32)
        pre_grad = (hidden_grad * gelu_slope(pre)).astype(jnp.bfloat16)
        second_grad = jnp.dot(act.T, grads, preferred_element_type=jnp.float32).astype(jnp.bfloat16)
        first_grad = jnp.dot(inputs.T, pre_grad, preferred_element_type=jnp.float32).astype(jnp.bfloat16)
        back = jnp.dot(pre_grad, first.T, preferred_element_type=jnp.float32).astype(jnp.bfloat16)
        return (outputs, back, first_grad, second_grad)
    slot_out, slot_back, grad_in, grad_outw = lax.map(expert_work, (jnp.swapaxes(slot_in, 0, 1), jnp.swapaxes(slot_grad, 0, 1), w_in, w_out))
    slot_out = jnp.swapaxes(slot_out, 0, 1)
    slot_back = jnp.swapaxes(slot_back, 0, 1)

    def backward_image(items):
        image, cotan, outputs, back = items
        normed, dispatch, combine = routing(image, keys, scale)
        comb_grad = jnp.dot(cotan, outputs.T, preferred_element_type=jnp.float32)
        disp_grad = jnp.dot(image, back.T, preferred_element_type=jnp.float32)
        direct = jnp.dot(dispatch.astype(jnp.bfloat16), back, preferred_element_type=jnp.float32)
        logit_grad = dispatch * (disp_grad - lax.optimization_barrier(jnp.sum(dispatch * disp_grad, axis=0, keepdims=True)))
        logit_grad = logit_grad + combine * (comb_grad - lax.optimization_barrier(jnp.sum(combine * comb_grad, axis=1, keepdims=True)))
        logit_grad = logit_grad.astype(jnp.bfloat16)
        normed_grad = scale * jnp.dot(logit_grad, keys.T, preferred_element_type=jnp.float32)
        keys_grad = scale * jnp.dot(normed.T, logit_grad, preferred_element_type=jnp.float32)
        _, pullback = jax.vjp(lambda v: normalize(v, -1), image.astype(jnp.float32))
        grad_image = direct + pullback(normed_grad)[0]
        return (grad_image.astype(jnp.bfloat16), keys_grad)
    grad_tokens, keys_parts = lax.map(backward_image, (tokens, grad_out, slot_out, slot_back))
    keys_grad = lax.optimization_barrier(jnp.sum(keys_parts, axis=0))
    _, key_pullback = jax.vjp(lambda v: normalize(v, 0), key_float)
    grad_keys = key_pullback(keys_grad)[0]
    return (grad_tokens, grad_in, grad_outw, grad_keys)
```

```python
import functools
import math

import jax
import jax.numpy as jnp
from jax import lax
from jax.experimental import pallas as pl
from jax.experimental.pallas import tpu as pltpu
from jax.sharding import PartitionSpec as P

EPS = 1e-06
MESH = pl.DeviceIdType.MESH
F32 = jnp.float32
BF16 = jnp.bfloat16
NN = (((1,), (0,)), ((), ()))
NT = (((1,), (1,)), ((), ()))
TN = (((0,), (0,)), ((), ()))


def dot(a, b, dims=NN):
    return lax.dot_general(a, b, dims, preferred_element_type=F32)


def selector(rows, cols, stride, offset):
    i = lax.broadcasted_iota(jnp.int32, (rows, cols), 0)
    j = lax.broadcasted_iota(jnp.int32, (rows, cols), 1)
    return jnp.where(i == j * stride + offset, 1.0, 0.0).astype(BF16)


def wait_for(ref, sem):
    pltpu.make_async_copy(ref, ref, sem).wait()


def slot_kernel(
    sizes,
    tok_h, cot_h, w1_h, w2_h, keys_ref, scale_ref,
    gt_o, gi_o, go_o, gk_o,
    tok, cot, w1, w2, at, mix_b, mix_c,
    kt, keysn, normed, rinv_s, logit_s, disp_s, comb_s, mix_in, mix_grad,
    send_in, send_grad, recv_in, recv_grad,
    x, gs, act, slope, pg, xt, actt,
    own_out, own_back, pair_out, pair_back, pair_out_r, pair_back_r,
    send_out, send_bk, recv_out, recv_bk, rows_out, rows_bk,
    key_send, key_recv, key_tot,
    load_sem, send_sem, recv_sem, in_sem, twin_sem, part_sem,
):
    images, tokens, width, experts, hidden, ny, nx, nz = sizes
    layer = 2 * nx * nz
    near = ny * layer
    half = near * images
    scale = scale_ref[0]
    dp = lax.axis_index("dp")
    ex = lax.axis_index("expert")
    zh, core = dp // 2, dp % 2
    px, py = (ex // nz) % nx, ex // (nz * nx)
    pz = zh * nz + ex % nz
    me = (py * nx + px) * 2 * nz + pz
    twin = {"dp": zh * 2 + 1 - core, "expert": ex}

    zs = [(pz + d) % (2 * nz) for d in range(2 * nz)]
    xs = [(px + d) % nx for d in range(nx)]
    ys = [(py + d) % ny * nx for d in range(ny)]
    z_dp = [z // nz * 2 + core for z in zs]
    z_ex = [z % nz for z in zs]

    def source(group):
        return ys[(ny - group) % ny] * 2 * nz

    def each_partner(body):
        for group in range(ny):
            for dx in range(nx):
                plane = ys[group] + xs[dx]
                for dz in range(2 * nz):
                    if group or dx or dz:
                        ee = plane * nz + z_ex[dz]
                        device = {"dp": z_dp[dz], "expert": ee}
                        body(group, plane * 2 * nz + zs[dz], ee, device)

    def load(index, src, dst):
        return pltpu.make_async_copy(src, dst, load_sem.at[index])

    loads = [load(b, tok_h.at[b], tok.at[pl.ds(b * tokens, tokens)]) for b in range(images)]
    loads += [
        load(images + b, cot_h.at[b], cot.at[pl.ds(b * tokens, tokens)]) for b in range(images)
    ]
    loads += [load(2 * images, w1_h.at[0], w1), load(2 * images + 1, w2_h.at[0], w2)]
    for one in loads[: 2 * images]:
        one.start()

    barrier = pltpu.get_barrier_semaphore()

    def greet(group, index, ee, device):
        pl.semaphore_signal(barrier, inc=1, device_id=device, device_id_type=MESH)

    each_partner(greet)
    for far in (zh, 1 - zh):
        pl.semaphore_signal(
            barrier, inc=1, device_id={"dp": far * 2 + 1 - core, "expert": ex}, device_id_type=MESH
        )

    key_rows = keys_ref[...].astype(F32)
    kt[...] = key_rows
    keysn[...] = (
        key_rows * lax.rsqrt(jnp.sum(key_rows * key_rows, axis=1, keepdims=True) + EPS)
    ).astype(BF16)

    for b in range(images):
        loads[b].wait()
        if b == 0:
            loads[2 * images].start()
            loads[2 * images + 1].start()
        rows = pl.ds(b * tokens, tokens)
        for i in range(tokens // 128):
            part = tok[b * tokens + i * 128 : b * tokens + (i + 1) * 128, :].astype(F32)
            square = part * part
            acc = square[:, :128]
            for j in range(1, width // 128):
                acc = acc + square[:, j * 128 : (j + 1) * 128]
            rinv_s[b, :, i * 128 : (i + 1) * 128] = lax.rsqrt(
                jnp.sum(acc.T, axis=0, keepdims=True) + EPS
            )
            down = lax.rsqrt(jnp.sum(acc, axis=1, keepdims=True) + EPS)
            normed[i * 128 : (i + 1) * 128, :] = (part * down).astype(BF16)
        logits = dot(keysn[...], normed[...], NT) * scale
        expo = jnp.exp(logits)
        disp = expo / jnp.sum(expo, axis=1, keepdims=True)
        comb = expo / jnp.sum(expo, axis=0, keepdims=True)
        logit_s[b] = logits
        disp_s[b] = disp
        comb_s[b] = comb
        disp_b = disp.astype(BF16)
        at[b, experts:, :] = disp_b
        spread = selector(images * experts, experts, images, b)
        mix_in[:, rows] = dot(spread, disp_b).astype(BF16)
        mix_grad[:, rows] = dot(spread, comb.astype(BF16)).astype(BF16)

    def remote(src, dst, send, recv, device):
        return pltpu.make_async_remote_copy(
            src_ref=src, dst_ref=dst, send_sem=send, recv_sem=recv,
            device_id=device, device_id_type=MESH,
        )

    def pack(rows_ref, start, blocks_ref, first, count):
        for i in range(count):
            rows_ref[start + i * images : start + (i + 1) * images, :] = blocks_ref[first + i]

    def out_of_experts(kind, out_ref, in_ref):
        def one(group, index, ee, device):
            remote(
                out_ref.at[ee], in_ref.at[me], send_sem.at[kind], in_sem.at[kind, group], device
            ).start()

        each_partner(one)
        in_ref[me] = out_ref[ex]

    def unpack(blocks_ref, value):
        for i in range(experts):
            blocks_ref[i] = value[i * images : (i + 1) * images, :]

    unpack(send_in, dot(mix_in[...], tok[...]).astype(BF16))
    pl.semaphore_wait(barrier, near + 1)
    out_of_experts(0, send_in, recv_in)
    for b in range(images):
        loads[images + b].wait()
    unpack(send_grad, dot(mix_grad[...], cot[...]).astype(BF16))
    out_of_experts(1, send_grad, recv_grad)

    def arrive(kind, in_ref, rows_ref):
        copies = []
        for group in range(ny):
            count = layer if group else layer - 1
            wait_for(in_ref.at[pl.ds(0, count)], in_sem.at[kind, group])
            pack(rows_ref, group * layer * images, in_ref, source(group), layer)
            mine = pl.ds(group * layer * images, layer * images)
            theirs = pl.ds(half + group * layer * images, layer * images)
            copies.append(
                remote(
                    rows_ref.at[mine], rows_ref.at[theirs],
                    part_sem.at[kind, group], twin_sem.at[kind, group], twin,
                )
            )
            copies[-1].start()
        return copies

    copies_in = arrive(0, recv_in, x)
    loads[2 * images].wait()
    loads[2 * images + 1].wait()
    for one in copies_in:
        one.wait_recv()

    step = min(256, hidden)

    def first(j, carry):
        cols = pl.ds(pl.multiple_of(j * step, step), step)
        pre = dot(x[...], w1[:, cols])
        cdf = 0.5 * (1.0 + lax.erf(pre * 0.7071067811865476))
        act[:, cols] = (pre * cdf).astype(BF16)
        slope[:, cols] = cdf + pre * jnp.exp(-0.5 * pre * pre) * 0.3989422804014327
        return carry

    lax.fori_loop(0, hidden // step, first, 0, unroll=2)

    wide = min(256, width)
    parts = -(-width // wide)

    def columns(j):
        return pl.ds(pl.multiple_of(jnp.minimum(j * wide, width - wide), 128), wide)

    def pair_copy(kind, j, src, dst):
        return remote(src.at[j], dst.at[j], send_sem.at[4 + kind], recv_sem.at[4 + kind], twin)

    def second(j, carry):
        res = dot(act[...], w2[:, columns(j)])
        pair_out[j] = res[half:].astype(BF16)
        pair_copy(0, j, pair_out, pair_out_r).start()
        own_out[j] = res[:half]
        return carry

    lax.fori_loop(0, parts, second, 0)

    copies_grad = arrive(1, recv_grad, gs)
    for one in copies_grad:
        one.wait_recv()

    def third(j, carry):
        cols = pl.ds(pl.multiple_of(j * step, step), step)
        pg[:, cols] = (dot(gs[...], w2[cols, :], NT) * slope[:, cols]).astype(BF16)
        return carry

    def chip_sums(kind, own, pair_r, rows_ref, out_ref, in_ref):
        wait_for(pair_r, recv_sem.at[4 + kind])
        for j in range(parts):
            start = min(j * wide, width - wide)
            rows_ref[:, start : start + wide] = (own[j] + pair_r[j].astype(F32)).astype(BF16)
        for group in range(ny):
            for i in range(layer):
                row = (group * layer + i) * images
                out_ref[source(group) + i] = rows_ref[row : row + images, :]

        def one(group, index, ee, device):
            remote(
                out_ref.at[index], in_ref.at[me], send_sem.at[2 + kind], in_sem.at[2 + kind, group],
                device,
            ).start()

        each_partner(one)
        in_ref[me] = out_ref[me]

    chip_sums(0, own_out, pair_out_r, rows_out, send_out, recv_out)
    lax.fori_loop(0, hidden // step, third, 0, unroll=2)

    def fourth(j, carry):
        res = dot(pg[...], w1[columns(j), :], NT)
        pair_back[j] = res[half:].astype(BF16)
        pair_copy(1, j, pair_back, pair_back_r).start()
        own_back[j] = res[:half]
        return carry

    lax.fori_loop(0, parts, fourth, 0)
    chip_sums(1, own_back, pair_back_r, rows_bk, send_bk, recv_bk)

    def turn(src, dst, size):
        same = selector(wide, wide, 1, 0)

        def one(j, carry):
            cols = pl.ds(pl.multiple_of(jnp.minimum(j * wide, size - wide), 128), wide)
            dst[cols, :] = dot(same, src[:, cols], NT).astype(BF16)
            return carry

        lax.fori_loop(0, -(-size // wide), one, 0)

    def product(left, right, out, size):
        def one(j, carry):
            rows = pl.ds(pl.multiple_of(j * size, 16), size)
            out[0, rows, :] = dot(left[rows, :], right[...]).astype(BF16)
            return carry

        lax.fori_loop(0, left.shape[0] // size, one, 0)

    turn(act, actt, hidden)
    product(actt, gs, go_o, hidden // 4)
    turn(x, xt, width)
    product(xt, pg, gi_o, width // 4)

    def collect(kind, in_ref, rows_ref):
        for group in range(ny):
            count = layer if group else layer - 1
            wait_for(in_ref.at[pl.ds(0, count)], in_sem.at[2 + kind, group])
            pack(rows_ref, group * layer * images, in_ref, source(group), layer)

    def gathered(rows_ref, b):
        i = lax.broadcasted_iota(jnp.int32, (experts, half), 0)
        j = lax.broadcasted_iota(jnp.int32, (experts, half), 1)
        slot = j // images
        group = slot // layer
        plane = (py + ny - group) % ny * nx + slot % layer // (2 * nz)
        wanted = (j % images == b) & (plane * nz + slot % nz == i)
        return dot(jnp.where(wanted, 1.0, 0.0).astype(BF16), rows_ref[...]).astype(BF16)

    collect(0, recv_out, rows_out)
    parts_lg = []
    for b in range(images):
        rows = pl.ds(b * tokens, tokens)
        comb_grad = dot(gathered(rows_out, b), cot[rows, :], NT)
        comb = comb_s[b]
        parts_lg.append(comb * (comb_grad - jnp.sum(comb * comb_grad, axis=0, keepdims=True)))

    collect(1, recv_bk, rows_bk)
    keys_grad = None
    for b in range(images):
        rows = pl.ds(b * tokens, tokens)
        back = gathered(rows_bk, b)
        mix_b[b, :experts, :] = keysn[...]
        mix_b[b, experts:, :] = back
        disp_grad = dot(back, tok[rows, :], NT)
        disp = disp_s[b]
        lg = parts_lg[b] + disp * (disp_grad - jnp.sum(disp * disp_grad, axis=1, keepdims=True))
        rinv = rinv_s[b]
        scaled = (lg * (scale * rinv)).astype(BF16)
        at[b, :experts, :] = scaled
        mix_c[b] = rinv * rinv * jnp.sum(lg * logit_s[b], axis=0, keepdims=True)
        term = dot(scaled, tok[rows, :])
        keys_grad = term if keys_grad is None else keys_grad + term

    for e in range(experts):
        key_send[e] = keys_grad[e : e + 1, :]

    for dy in range(ny):
        for dx in range(nx):
            for dz in range(nz):
                if dy or dx or dz:
                    ee = (ys[dy] + xs[dx]) * nz + z_ex[dz]
                    remote(
                        key_send.at[ee], key_recv.at[ex], send_sem.at[6], recv_sem.at[6],
                        {"dp": dp, "expert": ee},
                    ).start()
    key_recv[ex] = key_send[ex]
    most = pl.ds(0, experts - 1)

    per = min(256, tokens)
    for b in range(images):

        def one(j, carry, b=b):
            cut = pl.ds(pl.multiple_of(j * per, per), per)
            rows = pl.ds(pl.multiple_of(b * tokens + j * per, per), per)
            res = dot(at[b, :, cut], mix_b[b], TN)
            col = jnp.broadcast_to(mix_c[b, :, cut], (128, per)).T
            for k in range(width // 128):
                cols = slice(k * 128, (k + 1) * 128)
                gt_o[b, cut, cols] = (res[:, cols] - tok[rows, cols].astype(F32) * col).astype(BF16)
            return carry

        lax.fori_loop(0, tokens // per, one, 0)

    wait_for(key_recv.at[most], recv_sem.at[6])
    total = key_recv[0]
    for e in range(1, experts):
        total = total + key_recv[e]
    key_tot[dp] = total
    for k in range(1, 4):
        remote(
            key_tot.at[dp], key_tot.at[dp], send_sem.at[7], recv_sem.at[7],
            {"dp": (dp + k) % 4, "expert": ex},
        ).start()
    wait_for(key_tot.at[pl.ds(0, 3)], recv_sem.at[7])
    grad = (key_tot[0] + key_tot[1]) + (key_tot[2] + key_tot[3])
    own = kt[pl.ds(ex, 1), :]
    r = lax.rsqrt(jnp.sum(own * own, axis=1, keepdims=True) + EPS)
    gk_o[...] = grad * r - own * (r * r * r * jnp.sum(grad * own, axis=1, keepdims=True))

    some = pl.ds(0, near - 1)
    for kind, ref in enumerate((recv_in, recv_grad, recv_out, recv_bk)):
        wait_for(ref.at[some], send_sem.at[kind])
    wait_for(pair_out, send_sem.at[4])
    wait_for(pair_back, send_sem.at[5])
    for one in copies_in + copies_grad:
        one.wait_send()
    wait_for(key_recv.at[most], send_sem.at[6])
    wait_for(key_tot.at[pl.ds(0, 3)], send_sem.at[7])


def slots(sizes, tokens, cotangents, w_in, w_out, keys, scale):
    images, toks, width, experts, hidden, ny, nx, nz = sizes
    near = 2 * experts
    rows = near * images * 2
    half = near * images
    wide = min(256, width)
    parts = -(-width // wide)
    vmem = pltpu.VMEM
    dma = pltpu.SemaphoreType.DMA
    any_space = pl.BlockSpec(memory_space=pl.ANY)
    local = pl.BlockSpec(memory_space=pltpu.VMEM)
    flops = 2 * rows * width * hidden * 4
    return pl.pallas_call(
        functools.partial(slot_kernel, sizes),
        out_shape=(
            vmem((images, toks, width), BF16),
            vmem((1, width, hidden), BF16),
            vmem((1, hidden, width), BF16),
            vmem((1, width), F32),
        ),
        in_specs=[any_space] * 4 + [local, pl.BlockSpec(memory_space=pltpu.SMEM)],
        out_specs=(local,) * 4,
        scratch_shapes=[
            vmem((images * toks, width), BF16),
            vmem((images * toks, width), BF16),
            vmem((width, hidden), BF16),
            vmem((hidden, width), BF16),
            vmem((images, 2 * experts, toks), BF16),
            vmem((images, 2 * experts, width), BF16),
            vmem((images, 1, toks), F32),
            vmem((experts, width), F32),
            vmem((experts, width), BF16),
            vmem((toks, width), BF16),
            vmem((images, 1, toks), F32),
            vmem((images, experts, toks), F32),
            vmem((images, experts, toks), F32),
            vmem((images, experts, toks), F32),
            vmem((images * experts, images * toks), BF16),
            vmem((images * experts, images * toks), BF16),
            vmem((experts, images, width), BF16),
            vmem((experts, images, width), BF16),
            vmem((near, images, width), BF16),
            vmem((near, images, width), BF16),
            vmem((rows, width), BF16),
            vmem((rows, width), BF16),
            vmem((rows, hidden), BF16),
            vmem((rows, hidden), F32),
            vmem((rows, hidden), BF16),
            vmem((width, rows), BF16),
            vmem((hidden, rows), BF16),
            vmem((parts, half, wide), F32),
            vmem((parts, half, wide), F32),
            vmem((parts, half, wide), BF16),
            vmem((parts, half, wide), BF16),
            vmem((parts, half, wide), BF16),
            vmem((parts, half, wide), BF16),
            vmem((near, images, width), BF16),
            vmem((near, images, width), BF16),
            vmem((near, images, width), BF16),
            vmem((near, images, width), BF16),
            vmem((half, width), BF16),
            vmem((half, width), BF16),
            vmem((experts, 1, width), F32),
            vmem((experts, 1, width), F32),
            vmem((4, 1, width), F32),
            dma((2 * images + 2,)),
            dma((8,)),
            dma((8,)),
            dma((4, ny)),
            dma((2, ny)),
            dma((2, ny)),
        ],
        compiler_params=pltpu.CompilerParams(
            collective_id=0, has_side_effects=True, vmem_limit_bytes=44 * 1024 * 1024
        ),
        cost_estimate=pl.CostEstimate(
            flops=flops, bytes_accessed=4 * images * toks * width * 2, transcendentals=0
        ),
        name="slots",
    )(tokens, cotangents, w_in, w_out, keys, scale)


def store_kernel(gt, gi, go, gk, gt_h, gi_h, go_h, gk_h, sem):
    copies = []
    for src, dst in ((gi, gi_h), (go, go_h), (gt, gt_h), (gk, gk_h)):
        if len(src.shape) == 2:
            cuts = [(slice(None),)]
        elif src.shape[0] == 1:
            size = src.shape[1] // 4
            cuts = [(0, pl.ds(k * size, size)) for k in range(4)]
        else:
            cuts = [(k,) for k in range(src.shape[0])]
        for cut in cuts:
            copies.append(pltpu.make_async_copy(src.at[cut], dst.at[cut], sem.at[len(copies)]))
            copies[-1].start()
    for one in copies:
        one.wait()


def stored(*arrays):
    shape = jax.ShapeDtypeStruct
    return pl.pallas_call(
        store_kernel,
        out_shape=tuple(shape(one.shape, one.dtype) for one in arrays),
        in_specs=[pl.BlockSpec(memory_space=pltpu.VMEM)] * 4,
        out_specs=(pl.BlockSpec(memory_space=pl.ANY),) * 4,
        scratch_shapes=[pltpu.SemaphoreType.DMA((9 + arrays[0].shape[0],))],
        compiler_params=pltpu.CompilerParams(vmem_limit_bytes=4 * 1024 * 1024),
        cost_estimate=pl.CostEstimate(
            flops=0, bytes_accessed=2 * sum(one.size for one in arrays), transcendentals=0
        ),
        name="stored",
    )(*arrays)


def body(grid, tokens, slot_keys, logit_scale, w_in, w_out, grad_out):
    images, toks, width = tokens.shape
    sizes = (images, toks, width, slot_keys.shape[1], w_in.shape[2], *grid)
    gt, gi, go, gk = slots(sizes, tokens, grad_out, w_in, w_out, slot_keys.T, logit_scale)
    gt, gi, go, gk = stored(gt, gi, go, gk)
    return gt, gi, go, gk.reshape(width, 1)


def solution(mesh):
    experts = mesh.shape["expert"]
    nz = 2
    side = math.isqrt(experts // nz)
    grid = (experts // nz // side, side, nz)
    in_specs = (
        P(("dp", "expert"), None, None),
        P(),
        P(),
        P("expert", None, "dp"),
        P("expert", "dp", None),
        P(("dp", "expert"), None, None),
    )
    out_specs = (
        P(("dp", "expert"), None, None),
        P("expert", None, "dp"),
        P("expert", "dp", None),
        P(None, "expert"),
    )
    return jax.shard_map(
        functools.partial(body, grid),
        mesh=mesh,
        in_specs=in_specs,
        out_specs=out_specs,
        check_vma=False,
    )
```

```python
import functools
import math

import jax
import jax.numpy as jnp
from jax import lax
from jax.experimental import pallas as pl
from jax.experimental.pallas import tpu as pltpu
from jax.sharding import PartitionSpec as P

EPS = 1e-06
MESH = pl.DeviceIdType.MESH
F32 = jnp.float32
BF16 = jnp.bfloat16
NN = (((1,), (0,)), ((), ()))
NT = (((1,), (1,)), ((), ()))
TN = (((0,), (0,)), ((), ()))


def dot(a, b, dims=NN):
    return lax.dot_general(a, b, dims, preferred_element_type=F32)


def selector(rows, cols, stride, offset):
    i = lax.broadcasted_iota(jnp.int32, (rows, cols), 0)
    j = lax.broadcasted_iota(jnp.int32, (rows, cols), 1)
    return jnp.where(i == j * stride + offset, 1.0, 0.0).astype(BF16)


def wait_for(ref, sem):
    pltpu.make_async_copy(ref, ref, sem).wait()


def slot_kernel(
    sizes,
    tok_h, cot_h, w1_h, w2_h, keys_ref, scale_ref,
    gt_o, gi_o, go_o, gk_o,
    tok, cot, w1, w2, at, mix_b, mix_c,
    kt, keysn, normed, rinv_s, logit_s, disp_s, comb_s, mix_in, mix_grad,
    rows_first, send_in, send_grad, recv_in, recv_grad,
    x, gs, act, slope, pg, xt, actt,
    own_out, own_back, pair_out, pair_back, pair_out_r, pair_back_r,
    send_out, send_bk, recv_out, recv_bk, rows_out, rows_bk,
    key_send, key_recv, key_tot,
    load_sem, send_sem, recv_sem, in_sem, twin_sem, part_sem,
):
    images, tokens, width, experts, hidden, ny, nx, nz = sizes
    layer = 2 * nx * nz
    near = ny * layer
    half = near * images
    scale = scale_ref[0]
    dp = lax.axis_index("dp")
    ex = lax.axis_index("expert")
    zh, core = dp // 2, dp % 2
    px, py = (ex // nz) % nx, ex // (nz * nx)
    pz = zh * nz + ex % nz
    me = (py * nx + px) * 2 * nz + pz
    twin = {"dp": zh * 2 + 1 - core, "expert": ex}

    zs = [(pz + d) % (2 * nz) for d in range(2 * nz)]
    xs = [(px + d) % nx for d in range(nx)]
    ys = [(py + d) % ny * nx for d in range(ny)]
    z_dp = [z // nz * 2 + core for z in zs]
    z_ex = [z % nz for z in zs]

    def source(group):
        return ys[(ny - group) % ny] * 2 * nz

    def each_partner(body):
        for group in range(ny):
            for dx in range(nx):
                plane = ys[group] + xs[dx]
                for dz in range(2 * nz):
                    if group or dx or dz:
                        ee = plane * nz + z_ex[dz]
                        device = {"dp": z_dp[dz], "expert": ee}
                        body(group, plane * 2 * nz + zs[dz], ee, device)

    def load(index, src, dst):
        return pltpu.make_async_copy(src, dst, load_sem.at[index])

    pieces = 2
    piece = tokens // pieces
    tok_loads = [
        load(
            b * pieces + p, tok_h.at[b, pl.ds(p * piece, piece)],
            tok.at[pl.ds(b * tokens + p * piece, piece)],
        )
        for b in range(images)
        for p in range(pieces)
    ]
    done = images * pieces
    cot_loads = [
        load(done + b, cot_h.at[b], cot.at[pl.ds(b * tokens, tokens)]) for b in range(images)
    ]
    done += images
    weight_loads = [load(done, w1_h.at[0], w1), load(done + 1, w2_h.at[0], w2)]
    for one in tok_loads:
        one.start()

    barrier = pltpu.get_barrier_semaphore()

    def greet(group, index, ee, device):
        pl.semaphore_signal(barrier, inc=1, device_id=device, device_id_type=MESH)

    each_partner(greet)
    for far in (zh, 1 - zh):
        pl.semaphore_signal(
            barrier, inc=1, device_id={"dp": far * 2 + 1 - core, "expert": ex}, device_id_type=MESH
        )

    key_rows = keys_ref[...].astype(F32)
    kt[...] = key_rows
    keysn[...] = (
        key_rows * lax.rsqrt(jnp.sum(key_rows * key_rows, axis=1, keepdims=True) + EPS)
    ).astype(BF16)

    for b in range(images):
        rows = pl.ds(b * tokens, tokens)
        for p in range(pieces):
            tok_loads[b * pieces + p].wait()
            if b == 0 and p == 0:
                for one in (*cot_loads, *weight_loads):
                    one.start()
            for i in range(p * piece // 128, (p + 1) * piece // 128):
                accs = []
                for r in range(i * 128, (i + 1) * 128, 32):
                    part = tok[b * tokens + r : b * tokens + r + 32, :].astype(F32)
                    square = part * part
                    acc = square[:, :128]
                    for j in range(1, width // 128):
                        acc = acc + square[:, j * 128 : (j + 1) * 128]
                    accs.append(acc)
                    down = lax.rsqrt(jnp.sum(acc, axis=1, keepdims=True) + EPS)
                    normed[r : r + 32, :] = (part * down).astype(BF16)
                acc = jnp.concatenate(accs, axis=0)
                rinv_s[b, :, i * 128 : (i + 1) * 128] = lax.rsqrt(
                    jnp.sum(acc.T, axis=0, keepdims=True) + EPS
                )
        logits = dot(keysn[...], normed[...], NT) * scale
        expo = jnp.exp(logits)
        disp = expo / jnp.sum(expo, axis=1, keepdims=True)
        comb = expo / jnp.sum(expo, axis=0, keepdims=True)
        logit_s[b] = logits
        disp_s[b] = disp
        comb_s[b] = comb
        disp_b = disp.astype(BF16)
        at[experts:, rows] = disp_b
        spread = selector(images * experts, experts, images, b)
        mix_in[:, rows] = dot(spread, disp_b).astype(BF16)
        mix_grad[:, rows] = dot(spread, comb.astype(BF16)).astype(BF16)

    def remote(src, dst, send, recv, device):
        return pltpu.make_async_remote_copy(
            src_ref=src, dst_ref=dst, send_sem=send, recv_sem=recv,
            device_id=device, device_id_type=MESH,
        )

    def pack(rows_ref, start, blocks_ref, first, count):
        for i in range(count):
            rows_ref[start + i * images : start + (i + 1) * images, :] = blocks_ref[first + i]

    def by_group(send):
        todo = [[] for _ in range(ny)]
        each_partner(lambda group, *rest: todo[group].append(rest))
        for group in range(ny):
            send(group, todo[group])

    def out_of_experts(kind, value, out_ref, in_ref):
        each = nx * nz
        rows_first[...] = value

        def send(group, devices):
            part = rows_first[pl.ds(pl.multiple_of(ys[group] * nz * images, 16), each * images), :]
            for i in range(each):
                out_ref[ys[group] * nz + i] = part[i * images : (i + 1) * images, :]
            for index, ee, device in devices:
                remote(
                    out_ref.at[ee], in_ref.at[me], send_sem.at[kind], in_sem.at[kind, group], device
                ).start()

        by_group(send)
        in_ref[me] = out_ref[ex]

    pl.semaphore_wait(barrier, near + 1)
    out_of_experts(0, dot(mix_in[...], tok[...]).astype(BF16), send_in, recv_in)
    for one in cot_loads:
        one.wait()
    out_of_experts(1, dot(mix_grad[...], cot[...]).astype(BF16), send_grad, recv_grad)

    def arrive(kind, in_ref, rows_ref):
        copies = []
        for group in range(ny):
            count = layer if group else layer - 1
            wait_for(in_ref.at[pl.ds(0, count)], in_sem.at[kind, group])
            pack(rows_ref, group * layer * images, in_ref, source(group), layer)
            mine = pl.ds(group * layer * images, layer * images)
            theirs = pl.ds(half + group * layer * images, layer * images)
            copies.append(
                remote(
                    rows_ref.at[mine], rows_ref.at[theirs],
                    part_sem.at[kind, group], twin_sem.at[kind, group], twin,
                )
            )
            copies[-1].start()
        return copies

    copies_in = arrive(0, recv_in, x)
    for one in weight_loads:
        one.wait()
    for one in copies_in:
        one.wait_recv()

    step = min(256, hidden)

    def first(j, carry):
        cols = pl.ds(pl.multiple_of(j * step, step), step)
        pre = dot(x[...], w1[:, cols])
        cdf = 0.5 * (1.0 + lax.erf(pre * 0.7071067811865476))
        act[:, cols] = (pre * cdf).astype(BF16)
        slope[:, cols] = cdf + pre * jnp.exp(-0.5 * pre * pre) * 0.3989422804014327
        return carry

    lax.fori_loop(0, hidden // step, first, 0, unroll=2)

    wide = min(256, width)
    parts = -(-width // wide)

    def columns(j):
        return pl.ds(pl.multiple_of(jnp.minimum(j * wide, width - wide), 128), wide)

    def pair_copy(kind, j, src, dst):
        return remote(src.at[j], dst.at[j], send_sem.at[4 + kind], recv_sem.at[4 + kind], twin)

    def second(j, carry):
        res = dot(act[...], w2[:, columns(j)])
        pair_out[j] = res[half:].astype(BF16)
        pair_copy(0, j, pair_out, pair_out_r).start()
        own_out[j] = res[:half]
        return carry

    lax.fori_loop(0, parts, second, 0)

    copies_grad = arrive(1, recv_grad, gs)

    def third(j, carry):
        cols = pl.ds(pl.multiple_of(j * step, step), step)
        pg[:, cols] = (dot(gs[...], w2[cols, :], NT) * slope[:, cols]).astype(BF16)
        return carry

    def chip_sums(kind, own, pair_r, rows_ref, out_ref, in_ref):
        wait_for(pair_r, recv_sem.at[4 + kind])
        for j in range(parts):
            start = min(j * wide, width - wide)
            rows_ref[:, start : start + wide] = (own[j] + pair_r[j].astype(F32)).astype(BF16)

        def send(group, devices):
            other = (ny - group) % ny
            for i in range(layer):
                row = (other * layer + i) * images
                out_ref[source(other) + i] = rows_ref[row : row + images, :]
            for index, ee, device in devices:
                remote(
                    out_ref.at[index], in_ref.at[me], send_sem.at[2 + kind],
                    in_sem.at[2 + kind, group], device,
                ).start()

        by_group(send)
        in_ref[me] = out_ref[me]

    chip_sums(0, own_out, pair_out_r, rows_out, send_out, recv_out)
    for one in copies_grad:
        one.wait_recv()
    lax.fori_loop(0, hidden // step, third, 0, unroll=2)

    def fourth(j, carry):
        res = dot(pg[...], w1[columns(j), :], NT)
        pair_back[j] = res[half:].astype(BF16)
        pair_copy(1, j, pair_back, pair_back_r).start()
        own_back[j] = res[:half]
        return carry

    lax.fori_loop(0, parts, fourth, 0)
    def turn(src, dst, size):
        same = selector(wide, wide, 1, 0)

        def one(j, carry):
            cols = pl.ds(pl.multiple_of(jnp.minimum(j * wide, size - wide), 128), wide)
            dst[cols, :] = dot(same, src[:, cols], NT).astype(BF16)
            return carry

        lax.fori_loop(0, -(-size // wide), one, 0)

    def product(left, right, out, size):
        def one(j, carry):
            rows = pl.ds(pl.multiple_of(j * size, 16), size)
            out[0, rows, :] = dot(left[rows, :], right[...]).astype(BF16)
            return carry

        lax.fori_loop(0, left.shape[0] // size, one, 0)

    turn(act, actt, hidden)
    turn(x, xt, width)
    chip_sums(1, own_back, pair_back_r, rows_bk, send_bk, recv_bk)
    product(actt, gs, go_o, hidden // 4)
    product(xt, pg, gi_o, width // 4)

    def collect(kind, in_ref, rows_ref):
        for group in range(ny):
            count = layer if group else layer - 1
            wait_for(in_ref.at[pl.ds(0, count)], in_sem.at[2 + kind, group])
            pack(rows_ref, group * layer * images, in_ref, source(group), layer)

    def gathered(rows_ref):
        i = lax.broadcasted_iota(jnp.int32, (images * experts, half), 0)
        j = lax.broadcasted_iota(jnp.int32, (images * experts, half), 1)
        slot = j // images
        group = slot // layer
        plane = (py + ny - group) % ny * nx + slot % layer // (2 * nz)
        wanted = i == j % images * experts + plane * nz + slot % nz
        return dot(jnp.where(wanted, 1.0, 0.0).astype(BF16), rows_ref[...]).astype(BF16)

    collect(0, recv_out, rows_out)
    slot_out = gathered(rows_out)
    parts_lg = []
    for b in range(images):
        rows = pl.ds(b * tokens, tokens)
        comb_grad = dot(slot_out[b * experts : (b + 1) * experts], cot[rows, :], NT)
        comb = comb_s[b]
        parts_lg.append(comb * (comb_grad - jnp.sum(comb * comb_grad, axis=0, keepdims=True)))

    collect(1, recv_bk, rows_bk)
    slot_back = gathered(rows_bk)
    for b in range(images):
        rows = pl.ds(b * tokens, tokens)
        back = slot_back[b * experts : (b + 1) * experts]
        mix_b[b, :experts, :] = keysn[...]
        mix_b[b, experts:, :] = back
        disp_grad = dot(back, tok[rows, :], NT)
        disp = disp_s[b]
        lg = parts_lg[b] + disp * (disp_grad - jnp.sum(disp * disp_grad, axis=1, keepdims=True))
        rinv = rinv_s[b]
        scaled = (lg * (scale * rinv)).astype(BF16)
        at[:experts, rows] = scaled
        mix_c[b] = rinv * rinv * jnp.sum(lg * logit_s[b], axis=0, keepdims=True)
    keys_grad = dot(at[:experts, :], tok[...])

    for e in range(experts):
        key_send[e] = keys_grad[e : e + 1, :]

    for dy in range(ny):
        for dx in range(nx):
            for dz in range(nz):
                if dy or dx or dz:
                    ee = (ys[dy] + xs[dx]) * nz + z_ex[dz]
                    remote(
                        key_send.at[ee], key_recv.at[ex], send_sem.at[6], recv_sem.at[6],
                        {"dp": dp, "expert": ee},
                    ).start()
    key_recv[ex] = key_send[ex]
    most = pl.ds(0, experts - 1)

    per = min(256, tokens)

    def token_grads(b):
        def one(j, carry):
            cut = pl.ds(pl.multiple_of(j * per, per), per)
            rows = pl.ds(pl.multiple_of(b * tokens + j * per, per), per)
            res = dot(at[:, rows], mix_b[b], TN)
            col = jnp.broadcast_to(mix_c[b, :, cut], (128, per)).T
            for k in range(width // 128):
                cols = slice(k * 128, (k + 1) * 128)
                gt_o[b, cut, cols] = (res[:, cols] - tok[rows, cols].astype(F32) * col).astype(BF16)
            return carry

        lax.fori_loop(0, tokens // per, one, 0)

    for b in range(images // 2):
        token_grads(b)
    wait_for(key_recv.at[most], recv_sem.at[6])
    total = key_recv[0]
    for e in range(1, experts):
        total = total + key_recv[e]
    key_tot[dp] = total
    for k in range(1, 4):
        remote(
            key_tot.at[dp], key_tot.at[dp], send_sem.at[7], recv_sem.at[7],
            {"dp": (dp + k) % 4, "expert": ex},
        ).start()
    for b in range(images // 2, images):
        token_grads(b)
    wait_for(key_tot.at[pl.ds(0, 3)], recv_sem.at[7])
    grad = (key_tot[0] + key_tot[1]) + (key_tot[2] + key_tot[3])
    own = kt[pl.ds(ex, 1), :]
    r = lax.rsqrt(jnp.sum(own * own, axis=1, keepdims=True) + EPS)
    gk_o[...] = grad * r - own * (r * r * r * jnp.sum(grad * own, axis=1, keepdims=True))

    some = pl.ds(0, near - 1)
    for kind, ref in enumerate((recv_in, recv_grad, recv_out, recv_bk)):
        wait_for(ref.at[some], send_sem.at[kind])
    wait_for(pair_out, send_sem.at[4])
    wait_for(pair_back, send_sem.at[5])
    for one in copies_in + copies_grad:
        one.wait_send()
    wait_for(key_recv.at[most], send_sem.at[6])
    wait_for(key_tot.at[pl.ds(0, 3)], send_sem.at[7])


def slots(sizes, tokens, cotangents, w_in, w_out, keys, scale):
    images, toks, width, experts, hidden, ny, nx, nz = sizes
    near = 2 * experts
    rows = near * images * 2
    half = near * images
    wide = min(256, width)
    parts = -(-width // wide)
    vmem = pltpu.VMEM
    dma = pltpu.SemaphoreType.DMA
    any_space = pl.BlockSpec(memory_space=pl.ANY)
    local = pl.BlockSpec(memory_space=pltpu.VMEM)
    flops = 2 * rows * width * hidden * 4
    return pl.pallas_call(
        functools.partial(slot_kernel, sizes),
        out_shape=(
            vmem((images, toks, width), BF16),
            vmem((1, width, hidden), BF16),
            vmem((1, hidden, width), BF16),
            vmem((1, width), F32),
        ),
        in_specs=[any_space] * 4 + [local, pl.BlockSpec(memory_space=pltpu.SMEM)],
        out_specs=(local,) * 4,
        scratch_shapes=[
            vmem((images * toks, width), BF16),
            vmem((images * toks, width), BF16),
            vmem((width, hidden), BF16),
            vmem((hidden, width), BF16),
            vmem((2 * experts, images * toks), BF16),
            vmem((images, 2 * experts, width), BF16),
            vmem((images, 1, toks), F32),
            vmem((experts, width), F32),
            vmem((experts, width), BF16),
            vmem((toks, width), BF16),
            vmem((images, 1, toks), F32),
            vmem((images, experts, toks), F32),
            vmem((images, experts, toks), F32),
            vmem((images, experts, toks), F32),
            vmem((images * experts, images * toks), BF16),
            vmem((images * experts, images * toks), BF16),
            vmem((images * experts, width), BF16),
            vmem((experts, images, width), BF16),
            vmem((experts, images, width), BF16),
            vmem((near, images, width), BF16),
            vmem((near, images, width), BF16),
            vmem((rows, width), BF16),
            vmem((rows, width), BF16),
            vmem((rows, hidden), BF16),
            vmem((rows, hidden), F32),
            vmem((rows, hidden), BF16),
            vmem((width, rows), BF16),
            vmem((hidden, rows), BF16),
            vmem((parts, half, wide), F32),
            vmem((parts, half, wide), F32),
            vmem((parts, half, wide), BF16),
            vmem((parts, half, wide), BF16),
            vmem((parts, half, wide), BF16),
            vmem((parts, half, wide), BF16),
            vmem((near, images, width), BF16),
            vmem((near, images, width), BF16),
            vmem((near, images, width), BF16),
            vmem((near, images, width), BF16),
            vmem((half, width), BF16),
            vmem((half, width), BF16),
            vmem((experts, 1, width), F32),
            vmem((experts, 1, width), F32),
            vmem((4, 1, width), F32),
            dma((3 * images + 2,)),
            dma((8,)),
            dma((8,)),
            dma((4, ny)),
            dma((2, ny)),
            dma((2, ny)),
        ],
        compiler_params=pltpu.CompilerParams(
            collective_id=0, has_side_effects=True, vmem_limit_bytes=44 * 1024 * 1024
        ),
        cost_estimate=pl.CostEstimate(
            flops=flops, bytes_accessed=4 * images * toks * width * 2, transcendentals=0
        ),
        name="slots",
    )(tokens, cotangents, w_in, w_out, keys, scale)


def store_kernel(gt, gi, go, gk, gt_h, gi_h, go_h, gk_h, sem):
    copies = []
    for src, dst in ((gi, gi_h), (go, go_h), (gt, gt_h), (gk, gk_h)):
        if len(src.shape) == 2:
            cuts = [(slice(None),)]
        elif src.shape[0] == 1:
            size = src.shape[1] // 8
            cuts = [(0, pl.ds(k * size, size)) for k in range(8)]
        else:
            size = src.shape[1] // 2
            cuts = [(k, pl.ds(j * size, size)) for k in range(src.shape[0]) for j in range(2)]
        for cut in cuts:
            copies.append(pltpu.make_async_copy(src.at[cut], dst.at[cut], sem.at[len(copies)]))
            copies[-1].start()
    for one in copies:
        one.wait()


def stored(*arrays):
    shape = jax.ShapeDtypeStruct
    return pl.pallas_call(
        store_kernel,
        out_shape=tuple(shape(one.shape, one.dtype) for one in arrays),
        in_specs=[pl.BlockSpec(memory_space=pltpu.VMEM)] * 4,
        out_specs=(pl.BlockSpec(memory_space=pl.ANY),) * 4,
        scratch_shapes=[pltpu.SemaphoreType.DMA((17 + 2 * arrays[0].shape[0],))],
        compiler_params=pltpu.CompilerParams(vmem_limit_bytes=4 * 1024 * 1024),
        cost_estimate=pl.CostEstimate(
            flops=0, bytes_accessed=2 * sum(one.size for one in arrays), transcendentals=0
        ),
        name="stored",
    )(*arrays)


def body(grid, tokens, slot_keys, logit_scale, w_in, w_out, grad_out):
    images, toks, width = tokens.shape
    sizes = (images, toks, width, slot_keys.shape[1], w_in.shape[2], *grid)
    gt, gi, go, gk = slots(sizes, tokens, grad_out, w_in, w_out, slot_keys.T, logit_scale)
    gt, gi, go, gk = stored(gt, gi, go, gk)
    return gt, gi, go, gk.reshape(width, 1)


def solution(mesh):
    experts = mesh.shape["expert"]
    nz = 2
    side = math.isqrt(experts // nz)
    grid = (experts // nz // side, side, nz)
    in_specs = (
        P(("dp", "expert"), None, None),
        P(),
        P(),
        P("expert", None, "dp"),
        P("expert", "dp", None),
        P(("dp", "expert"), None, None),
    )
    out_specs = (
        P(("dp", "expert"), None, None),
        P("expert", None, "dp"),
        P("expert", "dp", None),
        P(None, "expert"),
    )
    return jax.shard_map(
        functools.partial(body, grid),
        mesh=mesh,
        in_specs=in_specs,
        out_specs=out_specs,
        check_vma=False,
    )
```

```python
import functools
import math

import jax
import jax.numpy as jnp
from jax import lax
from jax.experimental import pallas as pl
from jax.experimental.pallas import tpu as pltpu
from jax.sharding import PartitionSpec as P

EPS = 1e-06
MESH = pl.DeviceIdType.MESH
F32 = jnp.float32
BF16 = jnp.bfloat16
NN = (((1,), (0,)), ((), ()))
NT = (((1,), (1,)), ((), ()))
TN = (((0,), (0,)), ((), ()))


def dot(a, b, dims=NN):
    return lax.dot_general(a, b, dims, preferred_element_type=F32)


def selector(rows, cols, stride, offset):
    i = lax.broadcasted_iota(jnp.int32, (rows, cols), 0)
    j = lax.broadcasted_iota(jnp.int32, (rows, cols), 1)
    return jnp.where(i == j * stride + offset, 1.0, 0.0).astype(BF16)


def wait_for(ref, sem):
    pltpu.make_async_copy(ref, ref, sem).wait()


def spread_offsets(dims):
    left = [
        (a, b, c) for a in range(dims[0]) for b in range(dims[1]) for c in range(dims[2])
    ][1:]
    share = {}
    for one in left:
        for kind in enumerate(one):
            share[kind] = share.get(kind, 0) + 1
    order, used, total = [(0, 0, 0)], dict.fromkeys(share, 0), len(left)
    while left:
        at = len(order)

        def uneven(one):
            taken = set(enumerate(one))
            return sum(
                (used[k] + (k in taken) - share[k] * at / total) ** 2 * (2 if k[1] else 1)
                for k in share
            )

        best = min(left, key=lambda one: (round(uneven(one), 9), one))
        left.remove(best)
        order.append(best)
        for kind in enumerate(best):
            used[kind] += 1
    return order


def slot_kernel(
    sizes,
    tok_h, cot_h, w1_h, w2_h, keys_ref, scale_ref,
    gt_o, gi_o, go_o, gk_o,
    tok, cot, w1, w2, at, mix_b, mix_c,
    kt, keysn, normed, rinv_s, logit_s, disp_s, comb_s, mix_in, mix_grad,
    send_in, send_grad, recv_in, recv_grad,
    x, gs, act, slope, pg, xt, actt,
    own_out, own_back, pair_out, pair_back, pair_out_r, pair_back_r,
    send_out, send_bk, recv_out, recv_bk, rows_out, rows_bk,
    key_send, key_recv, key_tot,
    load_sem, send_sem, recv_sem, in_sem, twin_sem, part_sem,
):
    images, tokens, width, experts, hidden, ny, nx, nz = sizes
    layer = 2 * nx * nz
    near = ny * layer
    half = near * images
    scale = scale_ref[0]
    dp = lax.axis_index("dp")
    ex = lax.axis_index("expert")
    zh, core = dp // 2, dp % 2
    px, py = (ex // nz) % nx, ex // (nz * nx)
    pz = zh * nz + ex % nz
    twin = {"dp": zh * 2 + 1 - core, "expert": ex}

    zs = [(pz + d) % (2 * nz) for d in range(2 * nz)]
    xs = [(px + d) % nx for d in range(nx)]
    ys = [(py + d) % ny * nx for d in range(ny)]
    z_dp = [z // nz * 2 + core for z in zs]
    z_ex = [z % nz for z in zs]

    offsets = spread_offsets((ny, nx, 2 * nz))

    def device_at(dy, dx, dz):
        dz = dz % (2 * nz)
        ee = (ys[dy % ny] + xs[dx % nx]) * nz + z_ex[dz]
        return ee, {"dp": z_dp[dz], "expert": ee}

    def each_partner(body, sign=1):
        for p, (dy, dx, dz) in enumerate(offsets):
            if p:
                body(p, *device_at(sign * dy, sign * dx, sign * dz))

    def load(index, src, dst):
        return pltpu.make_async_copy(src, dst, load_sem.at[index])

    loads = [load(b, tok_h.at[b], tok.at[pl.ds(b * tokens, tokens)]) for b in range(images)]
    loads += [
        load(images + b, cot_h.at[b], cot.at[pl.ds(b * tokens, tokens)]) for b in range(images)
    ]
    loads += [load(2 * images, w1_h.at[0], w1), load(2 * images + 1, w2_h.at[0], w2)]
    for one in loads[: 2 * images]:
        one.start()

    barrier = pltpu.get_barrier_semaphore()

    def greet(p, ee, device):
        pl.semaphore_signal(barrier, inc=1, device_id=device, device_id_type=MESH)

    each_partner(greet)
    for far in (zh, 1 - zh):
        pl.semaphore_signal(
            barrier, inc=1, device_id={"dp": far * 2 + 1 - core, "expert": ex}, device_id_type=MESH
        )

    key_rows = keys_ref[...].astype(F32)
    kt[...] = key_rows
    keysn[...] = (
        key_rows * lax.rsqrt(jnp.sum(key_rows * key_rows, axis=1, keepdims=True) + EPS)
    ).astype(BF16)

    for b in range(images):
        loads[b].wait()
        if b == 0:
            loads[2 * images].start()
            loads[2 * images + 1].start()
        rows = pl.ds(b * tokens, tokens)
        for i in range(tokens // 128):
            part = tok[b * tokens + i * 128 : b * tokens + (i + 1) * 128, :].astype(F32)
            square = part * part
            acc = square[:, :128]
            for j in range(1, width // 128):
                acc = acc + square[:, j * 128 : (j + 1) * 128]
            rinv_s[b, :, i * 128 : (i + 1) * 128] = lax.rsqrt(
                jnp.sum(acc.T, axis=0, keepdims=True) + EPS
            )
            down = lax.rsqrt(jnp.sum(acc, axis=1, keepdims=True) + EPS)
            normed[i * 128 : (i + 1) * 128, :] = (part * down).astype(BF16)
        logits = dot(keysn[...], normed[...], NT) * scale
        expo = jnp.exp(logits)
        disp = expo / jnp.sum(expo, axis=1, keepdims=True)
        comb = expo / jnp.sum(expo, axis=0, keepdims=True)
        logit_s[b] = logits
        disp_s[b] = disp
        comb_s[b] = comb
        disp_b = disp.astype(BF16)
        at[b, experts:, :] = disp_b
        spread = selector(images * experts, experts, images, b)
        mix_in[:, rows] = dot(spread, disp_b).astype(BF16)
        mix_grad[:, rows] = dot(spread, comb.astype(BF16)).astype(BF16)

    def remote(src, dst, send, recv, device):
        return pltpu.make_async_remote_copy(
            src_ref=src, dst_ref=dst, send_sem=send, recv_sem=recv,
            device_id=device, device_id_type=MESH,
        )

    def pack(rows_ref, start, blocks_ref, first, count):
        for i in range(count):
            rows_ref[start + i * images : start + (i + 1) * images, :] = blocks_ref[first + i]

    def out_of_experts(kind, out_ref, in_ref):
        def one(p, ee, device):
            remote(
                out_ref.at[ee], in_ref.at[p], send_sem.at[kind], in_sem.at[kind, p // layer], device
            ).start()

        each_partner(one)
        in_ref[0] = out_ref[ex]

    def unpack(blocks_ref, value):
        for i in range(experts):
            blocks_ref[i] = value[i * images : (i + 1) * images, :]

    unpack(send_in, dot(mix_in[...], tok[...]).astype(BF16))
    pl.semaphore_wait(barrier, near + 1)
    out_of_experts(0, send_in, recv_in)
    for b in range(images):
        loads[images + b].wait()
    unpack(send_grad, dot(mix_grad[...], cot[...]).astype(BF16))
    out_of_experts(1, send_grad, recv_grad)

    def arrive(kind, in_ref, rows_ref):
        copies = []
        for group in range(ny):
            count = layer if group else layer - 1
            wait_for(in_ref.at[pl.ds(0, count)], in_sem.at[kind, group])
            pack(rows_ref, group * layer * images, in_ref, group * layer, layer)
            mine = pl.ds(group * layer * images, layer * images)
            theirs = pl.ds(half + group * layer * images, layer * images)
            copies.append(
                remote(
                    rows_ref.at[mine], rows_ref.at[theirs],
                    part_sem.at[kind, group], twin_sem.at[kind, group], twin,
                )
            )
            copies[-1].start()
        return copies

    copies_in = arrive(0, recv_in, x)
    loads[2 * images].wait()
    loads[2 * images + 1].wait()
    for one in copies_in:
        one.wait_recv()

    step = min(256, hidden)

    def first(j, carry):
        cols = pl.ds(pl.multiple_of(j * step, step), step)
        pre = dot(x[...], w1[:, cols])
        cdf = 0.5 * (1.0 + lax.erf(pre * 0.7071067811865476))
        act[:, cols] = (pre * cdf).astype(BF16)
        slope[:, cols] = cdf + pre * jnp.exp(-0.5 * pre * pre) * 0.3989422804014327
        return carry

    lax.fori_loop(0, hidden // step, first, 0, unroll=2)

    wide = min(256, width)
    parts = -(-width // wide)

    def columns(j):
        return pl.ds(pl.multiple_of(jnp.minimum(j * wide, width - wide), 128), wide)

    def pair_copy(kind, j, src, dst):
        return remote(src.at[j], dst.at[j], send_sem.at[4 + kind], recv_sem.at[4 + kind], twin)

    def second(j, carry):
        res = dot(act[...], w2[:, columns(j)])
        pair_out[j] = res[half:].astype(BF16)
        pair_copy(0, j, pair_out, pair_out_r).start()
        own_out[j] = res[:half]
        return carry

    lax.fori_loop(0, parts, second, 0)

    copies_grad = arrive(1, recv_grad, gs)
    for one in copies_grad:
        one.wait_recv()

    def third(j, carry):
        cols = pl.ds(pl.multiple_of(j * step, step), step)
        pg[:, cols] = (dot(gs[...], w2[cols, :], NT) * slope[:, cols]).astype(BF16)
        return carry

    def chip_sums(kind, own, pair_r, rows_ref, out_ref, in_ref):
        wait_for(pair_r, recv_sem.at[4 + kind])
        for j in range(parts):
            start = min(j * wide, width - wide)
            rows_ref[:, start : start + wide] = (own[j] + pair_r[j].astype(F32)).astype(BF16)
        for p in range(near):
            out_ref[p] = rows_ref[p * images : (p + 1) * images, :]

        def one(p, ee, device):
            remote(
                out_ref.at[p], in_ref.at[p], send_sem.at[2 + kind], in_sem.at[2 + kind, p // layer],
                device,
            ).start()

        each_partner(one, -1)
        in_ref[0] = out_ref[0]

    chip_sums(0, own_out, pair_out_r, rows_out, send_out, recv_out)
    lax.fori_loop(0, hidden // step, third, 0, unroll=2)

    def fourth(j, carry):
        res = dot(pg[...], w1[columns(j), :], NT)
        pair_back[j] = res[half:].astype(BF16)
        pair_copy(1, j, pair_back, pair_back_r).start()
        own_back[j] = res[:half]
        return carry

    lax.fori_loop(0, parts, fourth, 0)
    chip_sums(1, own_back, pair_back_r, rows_bk, send_bk, recv_bk)

    def turn(src, dst, size):
        same = selector(wide, wide, 1, 0)

        def one(j, carry):
            cols = pl.ds(pl.multiple_of(jnp.minimum(j * wide, size - wide), 128), wide)
            dst[cols, :] = dot(same, src[:, cols], NT).astype(BF16)
            return carry

        lax.fori_loop(0, -(-size // wide), one, 0)

    def product(left, right, out, size):
        def one(j, carry):
            rows = pl.ds(pl.multiple_of(j * size, 16), size)
            out[0, rows, :] = dot(left[rows, :], right[...]).astype(BF16)
            return carry

        lax.fori_loop(0, left.shape[0] // size, one, 0)

    turn(act, actt, hidden)
    product(actt, gs, go_o, hidden // 4)
    turn(x, xt, width)
    product(xt, pg, gi_o, width // 4)

    def collect(kind, in_ref, rows_ref):
        for group in range(ny):
            count = layer if group else layer - 1
            wait_for(in_ref.at[pl.ds(0, count)], in_sem.at[2 + kind, group])
            pack(rows_ref, group * layer * images, in_ref, group * layer, layer)

    i = lax.broadcasted_iota(jnp.int32, (images * experts, half), 0)
    j = lax.broadcasted_iota(jnp.int32, (1, half), 1)
    place = jnp.full((1, half), ex, jnp.int32)
    for p, offset in enumerate(offsets):
        place = jnp.where(j // images == p, device_at(*offset)[0], place)
    wanted = i == place + j % images * experts
    gather = jnp.where(wanted, 1.0, 0.0).astype(BF16)

    def gathered(rows_ref):
        return dot(gather, rows_ref[...]).astype(BF16)

    collect(0, recv_out, rows_out)
    slot_out = gathered(rows_out)
    parts_lg = []
    for b in range(images):
        rows = pl.ds(b * tokens, tokens)
        comb_grad = dot(slot_out[b * experts : (b + 1) * experts], cot[rows, :], NT)
        comb = comb_s[b]
        parts_lg.append(comb * (comb_grad - jnp.sum(comb * comb_grad, axis=0, keepdims=True)))

    collect(1, recv_bk, rows_bk)
    slot_back = gathered(rows_bk)
    keys_grad = None
    for b in range(images):
        rows = pl.ds(b * tokens, tokens)
        back = slot_back[b * experts : (b + 1) * experts]
        mix_b[b, :experts, :] = keysn[...]
        mix_b[b, experts:, :] = back
        disp_grad = dot(back, tok[rows, :], NT)
        disp = disp_s[b]
        lg = parts_lg[b] + disp * (disp_grad - jnp.sum(disp * disp_grad, axis=1, keepdims=True))
        rinv = rinv_s[b]
        scaled = (lg * (scale * rinv)).astype(BF16)
        at[b, :experts, :] = scaled
        mix_c[b] = rinv * rinv * jnp.sum(lg * logit_s[b], axis=0, keepdims=True)
        term = dot(scaled, tok[rows, :])
        keys_grad = term if keys_grad is None else keys_grad + term

    for e in range(experts):
        key_send[e] = keys_grad[e : e + 1, :]

    for dy, dx, dz in spread_offsets((ny, nx, nz))[1:]:
        ee = (ys[dy] + xs[dx]) * nz + z_ex[dz]
        remote(
            key_send.at[ee], key_recv.at[ex], send_sem.at[6], recv_sem.at[6],
            {"dp": dp, "expert": ee},
        ).start()
    key_recv[ex] = key_send[ex]
    most = pl.ds(0, experts - 1)

    per = min(256, tokens)
    for b in range(images):

        def one(j, carry, b=b):
            cut = pl.ds(pl.multiple_of(j * per, per), per)
            rows = pl.ds(pl.multiple_of(b * tokens + j * per, per), per)
            res = dot(at[b, :, cut], mix_b[b], TN)
            col = jnp.broadcast_to(mix_c[b, :, cut], (128, per)).T
            for k in range(width // 128):
                cols = slice(k * 128, (k + 1) * 128)
                gt_o[b, cut, cols] = (res[:, cols] - tok[rows, cols].astype(F32) * col).astype(BF16)
            return carry

        lax.fori_loop(0, tokens // per, one, 0)

    wait_for(key_recv.at[most], recv_sem.at[6])
    total = key_recv[0]
    for e in range(1, experts):
        total = total + key_recv[e]
    key_tot[dp] = total
    for k in range(1, 4):
        remote(
            key_tot.at[dp], key_tot.at[dp], send_sem.at[7], recv_sem.at[7],
            {"dp": (dp + k) % 4, "expert": ex},
        ).start()
    wait_for(key_tot.at[pl.ds(0, 3)], recv_sem.at[7])
    grad = (key_tot[0] + key_tot[1]) + (key_tot[2] + key_tot[3])
    own = kt[pl.ds(ex, 1), :]
    r = lax.rsqrt(jnp.sum(own * own, axis=1, keepdims=True) + EPS)
    gk_o[...] = grad * r - own * (r * r * r * jnp.sum(grad * own, axis=1, keepdims=True))

    some = pl.ds(0, near - 1)
    for kind, ref in enumerate((recv_in, recv_grad, recv_out, recv_bk)):
        wait_for(ref.at[some], send_sem.at[kind])
    wait_for(pair_out, send_sem.at[4])
    wait_for(pair_back, send_sem.at[5])
    for one in copies_in + copies_grad:
        one.wait_send()
    wait_for(key_recv.at[most], send_sem.at[6])
    wait_for(key_tot.at[pl.ds(0, 3)], send_sem.at[7])


def slots(sizes, tokens, cotangents, w_in, w_out, keys, scale):
    images, toks, width, experts, hidden, ny, nx, nz = sizes
    near = 2 * experts
    rows = near * images * 2
    half = near * images
    wide = min(256, width)
    parts = -(-width // wide)
    vmem = pltpu.VMEM
    dma = pltpu.SemaphoreType.DMA
    any_space = pl.BlockSpec(memory_space=pl.ANY)
    local = pl.BlockSpec(memory_space=pltpu.VMEM)
    flops = 2 * rows * width * hidden * 4
    return pl.pallas_call(
        functools.partial(slot_kernel, sizes),
        out_shape=(
            vmem((images, toks, width), BF16),
            vmem((1, width, hidden), BF16),
            vmem((1, hidden, width), BF16),
            vmem((1, width), F32),
        ),
        in_specs=[any_space] * 4 + [local, pl.BlockSpec(memory_space=pltpu.SMEM)],
        out_specs=(local,) * 4,
        scratch_shapes=[
            vmem((images * toks, width), BF16),
            vmem((images * toks, width), BF16),
            vmem((width, hidden), BF16),
            vmem((hidden, width), BF16),
            vmem((images, 2 * experts, toks), BF16),
            vmem((images, 2 * experts, width), BF16),
            vmem((images, 1, toks), F32),
            vmem((experts, width), F32),
            vmem((experts, width), BF16),
            vmem((toks, width), BF16),
            vmem((images, 1, toks), F32),
            vmem((images, experts, toks), F32),
            vmem((images, experts, toks), F32),
            vmem((images, experts, toks), F32),
            vmem((images * experts, images * toks), BF16),
            vmem((images * experts, images * toks), BF16),
            vmem((experts, images, width), BF16),
            vmem((experts, images, width), BF16),
            vmem((near, images, width), BF16),
            vmem((near, images, width), BF16),
            vmem((rows, width), BF16),
            vmem((rows, width), BF16),
            vmem((rows, hidden), BF16),
            vmem((rows, hidden), F32),
            vmem((rows, hidden), BF16),
            vmem((width, rows), BF16),
            vmem((hidden, rows), BF16),
            vmem((parts, half, wide), F32),
            vmem((parts, half, wide), F32),
            vmem((parts, half, wide), BF16),
            vmem((parts, half, wide), BF16),
            vmem((parts, half, wide), BF16),
            vmem((parts, half, wide), BF16),
            vmem((near, images, width), BF16),
            vmem((near, images, width), BF16),
            vmem((near, images, width), BF16),
            vmem((near, images, width), BF16),
            vmem((half, width), BF16),
            vmem((half, width), BF16),
            vmem((experts, 1, width), F32),
            vmem((experts, 1, width), F32),
            vmem((4, 1, width), F32),
            dma((2 * images + 2,)),
            dma((8,)),
            dma((8,)),
            dma((4, ny)),
            dma((2, ny)),
            dma((2, ny)),
        ],
        compiler_params=pltpu.CompilerParams(
            collective_id=0, has_side_effects=True, vmem_limit_bytes=44 * 1024 * 1024
        ),
        cost_estimate=pl.CostEstimate(
            flops=flops, bytes_accessed=4 * images * toks * width * 2, transcendentals=0
        ),
        name="slots",
    )(tokens, cotangents, w_in, w_out, keys, scale)


def store_kernel(gt, gi, go, gk, gt_h, gi_h, go_h, gk_h, sem):
    copies = []
    for src, dst in ((gi, gi_h), (go, go_h), (gt, gt_h), (gk, gk_h)):
        if len(src.shape) == 2:
            cuts = [(slice(None),)]
        elif src.shape[0] == 1:
            size = src.shape[1] // 4
            cuts = [(0, pl.ds(k * size, size)) for k in range(4)]
        else:
            cuts = [(k,) for k in range(src.shape[0])]
        for cut in cuts:
            copies.append(pltpu.make_async_copy(src.at[cut], dst.at[cut], sem.at[len(copies)]))
            copies[-1].start()
    for one in copies:
        one.wait()


def stored(*arrays):
    shape = jax.ShapeDtypeStruct
    return pl.pallas_call(
        store_kernel,
        out_shape=tuple(shape(one.shape, one.dtype) for one in arrays),
        in_specs=[pl.BlockSpec(memory_space=pltpu.VMEM)] * 4,
        out_specs=(pl.BlockSpec(memory_space=pl.ANY),) * 4,
        scratch_shapes=[pltpu.SemaphoreType.DMA((9 + arrays[0].shape[0],))],
        compiler_params=pltpu.CompilerParams(vmem_limit_bytes=4 * 1024 * 1024),
        cost_estimate=pl.CostEstimate(
            flops=0, bytes_accessed=2 * sum(one.size for one in arrays), transcendentals=0
        ),
        name="stored",
    )(*arrays)


def body(grid, tokens, slot_keys, logit_scale, w_in, w_out, grad_out):
    images, toks, width = tokens.shape
    sizes = (images, toks, width, slot_keys.shape[1], w_in.shape[2], *grid)
    gt, gi, go, gk = slots(sizes, tokens, grad_out, w_in, w_out, slot_keys.T, logit_scale)
    gt, gi, go, gk = stored(gt, gi, go, gk)
    return gt, gi, go, gk.reshape(width, 1)


def solution(mesh):
    experts = mesh.shape["expert"]
    nz = 2
    side = math.isqrt(experts // nz)
    grid = (experts // nz // side, side, nz)
    in_specs = (
        P(("dp", "expert"), None, None),
        P(),
        P(),
        P("expert", None, "dp"),
        P("expert", "dp", None),
        P(("dp", "expert"), None, None),
    )
    out_specs = (
        P(("dp", "expert"), None, None),
        P("expert", None, "dp"),
        P("expert", "dp", None),
        P(None, "expert"),
    )
    return jax.shard_map(
        functools.partial(body, grid),
        mesh=mesh,
        in_specs=in_specs,
        out_specs=out_specs,
        check_vma=False,
    )
```

```python
import functools
import math

import jax
import jax.numpy as jnp
from jax import lax
from jax.experimental import pallas as pl
from jax.experimental.pallas import tpu as pltpu
from jax.sharding import PartitionSpec as P

EPS = 1e-06
MESH = pl.DeviceIdType.MESH
F32 = jnp.float32
BF16 = jnp.bfloat16
NN = (((1,), (0,)), ((), ()))
NT = (((1,), (1,)), ((), ()))
TN = (((0,), (0,)), ((), ()))


def dot(a, b, dims=NN):
    return lax.dot_general(a, b, dims, preferred_element_type=F32)


def selector(rows, cols, stride, offset):
    i = lax.broadcasted_iota(jnp.int32, (rows, cols), 0)
    j = lax.broadcasted_iota(jnp.int32, (rows, cols), 1)
    return jnp.where(i == j * stride + offset, 1.0, 0.0).astype(BF16)


def wait_for(ref, sem):
    pltpu.make_async_copy(ref, ref, sem).wait()


def spread_offsets(dims):
    left = [
        (a, b, c) for a in range(dims[0]) for b in range(dims[1]) for c in range(dims[2])
    ][1:]
    share = {}
    for one in left:
        for kind in enumerate(one):
            share[kind] = share.get(kind, 0) + 1
    order, used, total = [(0, 0, 0)], dict.fromkeys(share, 0), len(left)
    while left:
        at = len(order)

        def uneven(one):
            taken = set(enumerate(one))
            return sum(
                (used[k] + (k in taken) - share[k] * at / total) ** 2 * (2 if k[1] else 1)
                for k in share
            )

        best = min(left, key=lambda one: (round(uneven(one), 9), one))
        left.remove(best)
        order.append(best)
        for kind in enumerate(best):
            used[kind] += 1
    return order


def slot_kernel(
    sizes,
    tok_h, cot_h, w1_h, w2_h, keys_ref, scale_ref,
    gt_o, gi_o, go_o, gk_o,
    tok, cot, w1, w2, at, mix_b, mix_c,
    kt, keysn, normed, rinv_s, logit_s, disp_s, comb_s, mix_in, mix_grad,
    send_in, send_grad, recv_in, recv_grad,
    x, gs, act, slope, pg, xt, actt,
    own_out, own_back, pair_out, pair_back, pair_out_r, pair_back_r,
    send_out, send_bk, recv_out, recv_bk, rows_out, rows_bk,
    key_send, key_recv, key_tot,
    load_sem, send_sem, recv_sem, in_sem, twin_sem, part_sem,
):
    images, tokens, width, experts, hidden, ny, nx, nz = sizes
    layer = 2 * nx * nz
    near = ny * layer
    half = near * images
    scale = scale_ref[0]
    dp = lax.axis_index("dp")
    ex = lax.axis_index("expert")
    zh, core = dp // 2, dp % 2
    px, py = (ex // nz) % nx, ex // (nz * nx)
    pz = zh * nz + ex % nz
    twin = {"dp": zh * 2 + 1 - core, "expert": ex}

    zs = [(pz + d) % (2 * nz) for d in range(2 * nz)]
    xs = [(px + d) % nx for d in range(nx)]
    ys = [(py + d) % ny * nx for d in range(ny)]
    z_dp = [z // nz * 2 + core for z in zs]
    z_ex = [z % nz for z in zs]

    offsets = spread_offsets((ny, nx, 2 * nz))

    def device_at(dy, dx, dz):
        dz = dz % (2 * nz)
        ee = (ys[dy % ny] + xs[dx % nx]) * nz + z_ex[dz]
        return ee, {"dp": z_dp[dz], "expert": ee}

    def each_partner(body, sign=1):
        for p, (dy, dx, dz) in enumerate(offsets):
            if p:
                body(p, *device_at(sign * dy, sign * dx, sign * dz))

    def load(index, src, dst):
        return pltpu.make_async_copy(src, dst, load_sem.at[index])

    pieces = 2
    piece = tokens // pieces
    tok_loads = [
        load(
            b * pieces + p, tok_h.at[b, pl.ds(p * piece, piece)],
            tok.at[pl.ds(b * tokens + p * piece, piece)],
        )
        for b in range(images)
        for p in range(pieces)
    ]
    done = images * pieces
    cot_loads = [
        load(done + b, cot_h.at[b], cot.at[pl.ds(b * tokens, tokens)]) for b in range(images)
    ]
    done += images
    weight_loads = [load(done, w1_h.at[0], w1), load(done + 1, w2_h.at[0], w2)]
    for one in tok_loads:
        one.start()

    barrier = pltpu.get_barrier_semaphore()

    def greet(p, ee, device):
        pl.semaphore_signal(barrier, inc=1, device_id=device, device_id_type=MESH)

    each_partner(greet)
    for far in (zh, 1 - zh):
        pl.semaphore_signal(
            barrier, inc=1, device_id={"dp": far * 2 + 1 - core, "expert": ex}, device_id_type=MESH
        )

    key_rows = keys_ref[...].astype(F32)
    kt[...] = key_rows
    keysn[...] = (
        key_rows * lax.rsqrt(jnp.sum(key_rows * key_rows, axis=1, keepdims=True) + EPS)
    ).astype(BF16)

    for b in range(images):
        rows = pl.ds(b * tokens, tokens)
        for p in range(pieces):
            tok_loads[b * pieces + p].wait()
            if b == 0 and p == 0:
                for one in (*cot_loads, *weight_loads):
                    one.start()
            for i in range(p * piece // 128, (p + 1) * piece // 128):
                accs = []
                for r in range(i * 128, (i + 1) * 128, 32):
                    part = tok[b * tokens + r : b * tokens + r + 32, :].astype(F32)
                    square = part * part
                    acc = square[:, :128]
                    for j in range(1, width // 128):
                        acc = acc + square[:, j * 128 : (j + 1) * 128]
                    accs.append(acc)
                    down = lax.rsqrt(jnp.sum(acc, axis=1, keepdims=True) + EPS)
                    normed[r : r + 32, :] = (part * down).astype(BF16)
                acc = jnp.concatenate(accs, axis=0)
                rinv_s[b, :, i * 128 : (i + 1) * 128] = lax.rsqrt(
                    jnp.sum(acc.T, axis=0, keepdims=True) + EPS
                )
        logits = dot(keysn[...], normed[...], NT) * scale
        expo = jnp.exp(logits)
        disp = expo / jnp.sum(expo, axis=1, keepdims=True)
        comb = expo / jnp.sum(expo, axis=0, keepdims=True)
        logit_s[b] = logits
        disp_s[b] = disp
        comb_s[b] = comb
        disp_b = disp.astype(BF16)
        at[b, experts:, :] = disp_b
        spread = selector(images * experts, experts, images, b)
        mix_in[:, rows] = dot(spread, disp_b).astype(BF16)
        mix_grad[:, rows] = dot(spread, comb.astype(BF16)).astype(BF16)

    def remote(src, dst, send, recv, device):
        return pltpu.make_async_remote_copy(
            src_ref=src, dst_ref=dst, send_sem=send, recv_sem=recv,
            device_id=device, device_id_type=MESH,
        )

    def pack(rows_ref, start, blocks_ref, first, count):
        for i in range(count):
            rows_ref[start + i * images : start + (i + 1) * images, :] = blocks_ref[first + i]

    def out_of_experts(kind, out_ref, in_ref):
        def one(p, ee, device):
            remote(
                out_ref.at[ee], in_ref.at[p], send_sem.at[kind], in_sem.at[kind, p // layer], device
            ).start()

        each_partner(one)
        in_ref[0] = out_ref[ex]

    def unpack(blocks_ref, value):
        for i in range(experts):
            blocks_ref[i] = value[i * images : (i + 1) * images, :]

    unpack(send_in, dot(mix_in[...], tok[...]).astype(BF16))
    pl.semaphore_wait(barrier, near + 1)
    out_of_experts(0, send_in, recv_in)
    for one in cot_loads:
        one.wait()
    unpack(send_grad, dot(mix_grad[...], cot[...]).astype(BF16))
    out_of_experts(1, send_grad, recv_grad)

    def arrive(kind, in_ref, rows_ref):
        copies = []
        for group in range(ny):
            count = layer if group else layer - 1
            wait_for(in_ref.at[pl.ds(0, count)], in_sem.at[kind, group])
            pack(rows_ref, group * layer * images, in_ref, group * layer, layer)
            mine = pl.ds(group * layer * images, layer * images)
            theirs = pl.ds(half + group * layer * images, layer * images)
            copies.append(
                remote(
                    rows_ref.at[mine], rows_ref.at[theirs],
                    part_sem.at[kind, group], twin_sem.at[kind, group], twin,
                )
            )
            copies[-1].start()
        return copies

    copies_in = arrive(0, recv_in, x)
    for one in weight_loads:
        one.wait()
    for one in copies_in:
        one.wait_recv()

    step = min(256, hidden)

    def first(j, carry):
        cols = pl.ds(pl.multiple_of(j * step, step), step)
        pre = dot(x[...], w1[:, cols])
        cdf = 0.5 * (1.0 + lax.erf(pre * 0.7071067811865476))
        act[:, cols] = (pre * cdf).astype(BF16)
        slope[:, cols] = cdf + pre * jnp.exp(-0.5 * pre * pre) * 0.3989422804014327
        return carry

    lax.fori_loop(0, hidden // step, first, 0, unroll=2)

    wide = min(256, width)
    parts = -(-width // wide)

    def columns(j):
        return pl.ds(pl.multiple_of(jnp.minimum(j * wide, width - wide), 128), wide)

    def pair_copy(kind, j, src, dst):
        return remote(src.at[j], dst.at[j], send_sem.at[4 + kind], recv_sem.at[4 + kind], twin)

    def second(j, carry):
        res = dot(act[...], w2[:, columns(j)])
        pair_out[j] = res[half:].astype(BF16)
        pair_copy(0, j, pair_out, pair_out_r).start()
        own_out[j] = res[:half]
        return carry

    lax.fori_loop(0, parts, second, 0)

    copies_grad = arrive(1, recv_grad, gs)

    def third(j, carry):
        cols = pl.ds(pl.multiple_of(j * step, step), step)
        pg[:, cols] = (dot(gs[...], w2[cols, :], NT) * slope[:, cols]).astype(BF16)
        return carry

    def chip_sums(kind, own, pair_r, rows_ref, out_ref, in_ref):
        wait_for(pair_r, recv_sem.at[4 + kind])
        for j in range(parts):
            start = min(j * wide, width - wide)
            rows_ref[:, start : start + wide] = (own[j] + pair_r[j].astype(F32)).astype(BF16)
        for p in range(near):
            out_ref[p] = rows_ref[p * images : (p + 1) * images, :]

        def one(p, ee, device):
            remote(
                out_ref.at[p], in_ref.at[p], send_sem.at[2 + kind], in_sem.at[2 + kind, p // layer],
                device,
            ).start()

        each_partner(one, -1)
        in_ref[0] = out_ref[0]

    chip_sums(0, own_out, pair_out_r, rows_out, send_out, recv_out)
    for one in copies_grad:
        one.wait_recv()
    lax.fori_loop(0, hidden // step, third, 0, unroll=2)

    def fourth(j, carry):
        res = dot(pg[...], w1[columns(j), :], NT)
        pair_back[j] = res[half:].astype(BF16)
        pair_copy(1, j, pair_back, pair_back_r).start()
        own_back[j] = res[:half]
        return carry

    lax.fori_loop(0, parts, fourth, 0)
    chip_sums(1, own_back, pair_back_r, rows_bk, send_bk, recv_bk)

    def turn(src, dst, size):
        same = selector(wide, wide, 1, 0)

        def one(j, carry):
            cols = pl.ds(pl.multiple_of(jnp.minimum(j * wide, size - wide), 128), wide)
            dst[cols, :] = dot(same, src[:, cols], NT).astype(BF16)
            return carry

        lax.fori_loop(0, -(-size // wide), one, 0)

    def product(left, right, out, size):
        def one(j, carry):
            rows = pl.ds(pl.multiple_of(j * size, 16), size)
            out[0, rows, :] = dot(left[rows, :], right[...]).astype(BF16)
            return carry

        lax.fori_loop(0, left.shape[0] // size, one, 0)

    turn(act, actt, hidden)
    product(actt, gs, go_o, hidden // 4)
    turn(x, xt, width)
    product(xt, pg, gi_o, width // 4)

    def collect(kind, in_ref, rows_ref):
        for group in range(ny):
            count = layer if group else layer - 1
            wait_for(in_ref.at[pl.ds(0, count)], in_sem.at[2 + kind, group])
            pack(rows_ref, group * layer * images, in_ref, group * layer, layer)

    i = lax.broadcasted_iota(jnp.int32, (images * experts, half), 0)
    j = lax.broadcasted_iota(jnp.int32, (1, half), 1)
    place = jnp.full((1, half), ex, jnp.int32)
    for p, offset in enumerate(offsets):
        place = jnp.where(j // images == p, device_at(*offset)[0], place)
    wanted = i == place + j % images * experts
    gather = jnp.where(wanted, 1.0, 0.0).astype(BF16)

    def gathered(rows_ref):
        return dot(gather, rows_ref[...]).astype(BF16)

    collect(0, recv_out, rows_out)
    slot_out = gathered(rows_out)
    parts_lg = []
    for b in range(images):
        rows = pl.ds(b * tokens, tokens)
        comb_grad = dot(slot_out[b * experts : (b + 1) * experts], cot[rows, :], NT)
        comb = comb_s[b]
        parts_lg.append(comb * (comb_grad - jnp.sum(comb * comb_grad, axis=0, keepdims=True)))

    collect(1, recv_bk, rows_bk)
    slot_back = gathered(rows_bk)
    keys_grad = None
    for b in range(images):
        rows = pl.ds(b * tokens, tokens)
        back = slot_back[b * experts : (b + 1) * experts]
        mix_b[b, :experts, :] = keysn[...]
        mix_b[b, experts:, :] = back
        disp_grad = dot(back, tok[rows, :], NT)
        disp = disp_s[b]
        lg = parts_lg[b] + disp * (disp_grad - jnp.sum(disp * disp_grad, axis=1, keepdims=True))
        rinv = rinv_s[b]
        scaled = (lg * (scale * rinv)).astype(BF16)
        at[b, :experts, :] = scaled
        mix_c[b] = rinv * rinv * jnp.sum(lg * logit_s[b], axis=0, keepdims=True)
        term = dot(scaled, tok[rows, :])
        keys_grad = term if keys_grad is None else keys_grad + term

    for e in range(experts):
        key_send[e] = keys_grad[e : e + 1, :]

    for dy, dx, dz in spread_offsets((ny, nx, nz))[1:]:
        ee = (ys[dy] + xs[dx]) * nz + z_ex[dz]
        remote(
            key_send.at[ee], key_recv.at[ex], send_sem.at[6], recv_sem.at[6],
            {"dp": dp, "expert": ee},
        ).start()
    key_recv[ex] = key_send[ex]
    most = pl.ds(0, experts - 1)

    per = min(256, tokens)

    def token_grads(b):
        def one(j, carry):
            cut = pl.ds(pl.multiple_of(j * per, per), per)
            rows = pl.ds(pl.multiple_of(b * tokens + j * per, per), per)
            res = dot(at[b, :, cut], mix_b[b], TN)
            col = jnp.broadcast_to(mix_c[b, :, cut], (128, per)).T
            for k in range(width // 128):
                cols = slice(k * 128, (k + 1) * 128)
                gt_o[b, cut, cols] = (res[:, cols] - tok[rows, cols].astype(F32) * col).astype(BF16)
            return carry

        lax.fori_loop(0, tokens // per, one, 0)

    for b in range(images // 2):
        token_grads(b)
    wait_for(key_recv.at[most], recv_sem.at[6])
    total = key_recv[0]
    for e in range(1, experts):
        total = total + key_recv[e]
    key_tot[dp] = total
    for k in range(1, 4):
        remote(
            key_tot.at[dp], key_tot.at[dp], send_sem.at[7], recv_sem.at[7],
            {"dp": (dp + k) % 4, "expert": ex},
        ).start()
    for b in range(images // 2, images):
        token_grads(b)
    wait_for(key_tot.at[pl.ds(0, 3)], recv_sem.at[7])
    grad = (key_tot[0] + key_tot[1]) + (key_tot[2] + key_tot[3])
    own = kt[pl.ds(ex, 1), :]
    r = lax.rsqrt(jnp.sum(own * own, axis=1, keepdims=True) + EPS)
    gk_o[...] = grad * r - own * (r * r * r * jnp.sum(grad * own, axis=1, keepdims=True))

    some = pl.ds(0, near - 1)
    for kind, ref in enumerate((recv_in, recv_grad, recv_out, recv_bk)):
        wait_for(ref.at[some], send_sem.at[kind])
    wait_for(pair_out, send_sem.at[4])
    wait_for(pair_back, send_sem.at[5])
    for one in copies_in + copies_grad:
        one.wait_send()
    wait_for(key_recv.at[most], send_sem.at[6])
    wait_for(key_tot.at[pl.ds(0, 3)], send_sem.at[7])


def slots(sizes, tokens, cotangents, w_in, w_out, keys, scale):
    images, toks, width, experts, hidden, ny, nx, nz = sizes
    near = 2 * experts
    rows = near * images * 2
    half = near * images
    wide = min(256, width)
    parts = -(-width // wide)
    vmem = pltpu.VMEM
    dma = pltpu.SemaphoreType.DMA
    any_space = pl.BlockSpec(memory_space=pl.ANY)
    local = pl.BlockSpec(memory_space=pltpu.VMEM)
    flops = 2 * rows * width * hidden * 4
    return pl.pallas_call(
        functools.partial(slot_kernel, sizes),
        out_shape=(
            vmem((images, toks, width), BF16),
            vmem((1, width, hidden), BF16),
            vmem((1, hidden, width), BF16),
            vmem((1, width), F32),
        ),
        in_specs=[any_space] * 4 + [local, pl.BlockSpec(memory_space=pltpu.SMEM)],
        out_specs=(local,) * 4,
        scratch_shapes=[
            vmem((images * toks, width), BF16),
            vmem((images * toks, width), BF16),
            vmem((width, hidden), BF16),
            vmem((hidden, width), BF16),
            vmem((images, 2 * experts, toks), BF16),
            vmem((images, 2 * experts, width), BF16),
            vmem((images, 1, toks), F32),
            vmem((experts, width), F32),
            vmem((experts, width), BF16),
            vmem((toks, width), BF16),
            vmem((images, 1, toks), F32),
            vmem((images, experts, toks), F32),
            vmem((images, experts, toks), F32),
            vmem((images, experts, toks), F32),
            vmem((images * experts, images * toks), BF16),
            vmem((images * experts, images * toks), BF16),
            vmem((experts, images, width), BF16),
            vmem((experts, images, width), BF16),
            vmem((near, images, width), BF16),
            vmem((near, images, width), BF16),
            vmem((rows, width), BF16),
            vmem((rows, width), BF16),
            vmem((rows, hidden), BF16),
            vmem((rows, hidden), F32),
            vmem((rows, hidden), BF16),
            vmem((width, rows), BF16),
            vmem((hidden, rows), BF16),
            vmem((parts, half, wide), F32),
            vmem((parts, half, wide), F32),
            vmem((parts, half, wide), BF16),
            vmem((parts, half, wide), BF16),
            vmem((parts, half, wide), BF16),
            vmem((parts, half, wide), BF16),
            vmem((near, images, width), BF16),
            vmem((near, images, width), BF16),
            vmem((near, images, width), BF16),
            vmem((near, images, width), BF16),
            vmem((half, width), BF16),
            vmem((half, width), BF16),
            vmem((experts, 1, width), F32),
            vmem((experts, 1, width), F32),
            vmem((4, 1, width), F32),
            dma((3 * images + 2,)),
            dma((8,)),
            dma((8,)),
            dma((4, ny)),
            dma((2, ny)),
            dma((2, ny)),
        ],
        compiler_params=pltpu.CompilerParams(
            collective_id=0, has_side_effects=True, vmem_limit_bytes=44 * 1024 * 1024
        ),
        cost_estimate=pl.CostEstimate(
            flops=flops, bytes_accessed=4 * images * toks * width * 2, transcendentals=0
        ),
        name="slots",
    )(tokens, cotangents, w_in, w_out, keys, scale)


def store_kernel(gt, gi, go, gk, gt_h, gi_h, go_h, gk_h, sem):
    copies = []
    for src, dst in ((gi, gi_h), (go, go_h), (gt, gt_h), (gk, gk_h)):
        if len(src.shape) == 2:
            cuts = [(slice(None),)]
        elif src.shape[0] == 1:
            size = src.shape[1] // 4
            cuts = [(0, pl.ds(k * size, size)) for k in range(4)]
        else:
            cuts = [(k,) for k in range(src.shape[0])]
        for cut in cuts:
            copies.append(pltpu.make_async_copy(src.at[cut], dst.at[cut], sem.at[len(copies)]))
            copies[-1].start()
    for one in copies:
        one.wait()


def stored(*arrays):
    shape = jax.ShapeDtypeStruct
    return pl.pallas_call(
        store_kernel,
        out_shape=tuple(shape(one.shape, one.dtype) for one in arrays),
        in_specs=[pl.BlockSpec(memory_space=pltpu.VMEM)] * 4,
        out_specs=(pl.BlockSpec(memory_space=pl.ANY),) * 4,
        scratch_shapes=[pltpu.SemaphoreType.DMA((9 + arrays[0].shape[0],))],
        compiler_params=pltpu.CompilerParams(vmem_limit_bytes=4 * 1024 * 1024),
        cost_estimate=pl.CostEstimate(
            flops=0, bytes_accessed=2 * sum(one.size for one in arrays), transcendentals=0
        ),
        name="stored",
    )(*arrays)


def body(grid, tokens, slot_keys, logit_scale, w_in, w_out, grad_out):
    images, toks, width = tokens.shape
    sizes = (images, toks, width, slot_keys.shape[1], w_in.shape[2], *grid)
    gt, gi, go, gk = slots(sizes, tokens, grad_out, w_in, w_out, slot_keys.T, logit_scale)
    gt, gi, go, gk = stored(gt, gi, go, gk)
    return gt, gi, go, gk.reshape(width, 1)


def solution(mesh):
    experts = mesh.shape["expert"]
    nz = 2
    side = math.isqrt(experts // nz)
    grid = (experts // nz // side, side, nz)
    in_specs = (
        P(("dp", "expert"), None, None),
        P(),
        P(),
        P("expert", None, "dp"),
        P("expert", "dp", None),
        P(("dp", "expert"), None, None),
    )
    out_specs = (
        P(("dp", "expert"), None, None),
        P("expert", None, "dp"),
        P("expert", "dp", None),
        P(None, "expert"),
    )
    return jax.shard_map(
        functools.partial(body, grid),
        mesh=mesh,
        in_specs=in_specs,
        out_specs=out_specs,
        check_vma=False,
    )
```

```python
import functools
import math

import jax
import jax.numpy as jnp
from jax import lax
from jax.experimental import pallas as pl
from jax.experimental.pallas import tpu as pltpu
from jax.sharding import PartitionSpec as P

EPS = 1e-06
MESH = pl.DeviceIdType.MESH
F32 = jnp.float32
BF16 = jnp.bfloat16
NN = (((1,), (0,)), ((), ()))
NT = (((1,), (1,)), ((), ()))
TN = (((0,), (0,)), ((), ()))


def dot(a, b, dims=NN):
    return lax.dot_general(a, b, dims, preferred_element_type=F32)


def selector(rows, cols, stride, offset):
    i = lax.broadcasted_iota(jnp.int32, (rows, cols), 0)
    j = lax.broadcasted_iota(jnp.int32, (rows, cols), 1)
    return jnp.where(i == j * stride + offset, 1.0, 0.0).astype(BF16)


def wait_for(ref, sem):
    pltpu.make_async_copy(ref, ref, sem).wait()


def spread_offsets(dims):
    left = [
        (a, b, c) for a in range(dims[0]) for b in range(dims[1]) for c in range(dims[2])
    ][1:]
    share = {}
    for one in left:
        for kind in enumerate(one):
            share[kind] = share.get(kind, 0) + 1
    order, used, total = [(0, 0, 0)], dict.fromkeys(share, 0), len(left)
    while left:
        at = len(order)

        def uneven(one):
            taken = set(enumerate(one))
            return sum(
                (used[k] + (k in taken) - share[k] * at / total) ** 2 * (2 if k[1] else 1)
                for k in share
            )

        best = min(left, key=lambda one: (round(uneven(one), 9), one))
        left.remove(best)
        order.append(best)
        for kind in enumerate(best):
            used[kind] += 1
    return order


def slot_kernel(
    sizes,
    tok_h, cot_h, w1_h, w2_h, keys_ref, scale_ref,
    gt_o, gi_o, go_o, gk_o,
    tok, cot, w1, w2, at, mix_b, mix_c,
    kt, keysn, normed, rinv_s, logit_s, disp_s, comb_s, mix_in, mix_grad,
    send_in, send_grad, recv_in, recv_grad,
    x, gs, act, slope, pg, xt, actt,
    own_out, own_back, pair_out, pair_back, pair_out_r, pair_back_r,
    send_out, send_bk, recv_out, recv_bk, rows_out, rows_bk,
    key_send, key_recv, key_tot,
    load_sem, send_sem, recv_sem, in_sem, twin_sem, part_sem,
):
    images, tokens, width, experts, hidden, ny, nx, nz = sizes
    layer = 2 * nx * nz
    near = ny * layer
    half = near * images
    scale = scale_ref[0]
    dp = lax.axis_index("dp")
    ex = lax.axis_index("expert")
    zh, core = dp // 2, dp % 2
    px, py = (ex // nz) % nx, ex // (nz * nx)
    pz = zh * nz + ex % nz
    twin = {"dp": zh * 2 + 1 - core, "expert": ex}

    zs = [(pz + d) % (2 * nz) for d in range(2 * nz)]
    xs = [(px + d) % nx for d in range(nx)]
    ys = [(py + d) % ny * nx for d in range(ny)]
    z_dp = [z // nz * 2 + core for z in zs]
    z_ex = [z % nz for z in zs]

    offsets = spread_offsets((ny, nx, 2 * nz))

    def device_at(dy, dx, dz):
        dz = dz % (2 * nz)
        ee = (ys[dy % ny] + xs[dx % nx]) * nz + z_ex[dz]
        return ee, {"dp": z_dp[dz], "expert": ee}

    def each_partner(body, sign=1):
        for p, (dy, dx, dz) in enumerate(offsets):
            if p:
                body(p, *device_at(sign * dy, sign * dx, sign * dz))

    def load(index, src, dst):
        return pltpu.make_async_copy(src, dst, load_sem.at[index])

    pieces = 2
    piece = tokens // pieces
    tok_loads = [
        load(
            b * pieces + p, tok_h.at[b, pl.ds(p * piece, piece)],
            tok.at[pl.ds(b * tokens + p * piece, piece)],
        )
        for b in range(images)
        for p in range(pieces)
    ]
    done = images * pieces
    cot_loads = [
        load(done + b, cot_h.at[b], cot.at[pl.ds(b * tokens, tokens)]) for b in range(images)
    ]
    done += images
    weight_loads = [load(done, w1_h.at[0], w1), load(done + 1, w2_h.at[0], w2)]
    for one in tok_loads:
        one.start()

    barrier = pltpu.get_barrier_semaphore()

    def greet(p, ee, device):
        pl.semaphore_signal(barrier, inc=1, device_id=device, device_id_type=MESH)

    each_partner(greet)
    for far in (zh, 1 - zh):
        pl.semaphore_signal(
            barrier, inc=1, device_id={"dp": far * 2 + 1 - core, "expert": ex}, device_id_type=MESH
        )

    key_rows = keys_ref[...].astype(F32)
    kt[...] = key_rows
    keysn[...] = (
        key_rows * lax.rsqrt(jnp.sum(key_rows * key_rows, axis=1, keepdims=True) + EPS)
    ).astype(BF16)

    for b in range(images):
        rows = pl.ds(b * tokens, tokens)
        for p in range(pieces):
            tok_loads[b * pieces + p].wait()
            if b == 0 and p == 0:
                for one in (*cot_loads, *weight_loads):
                    one.start()
            for i in range(p * piece // 128, (p + 1) * piece // 128):
                accs = []
                for r in range(i * 128, (i + 1) * 128, 32):
                    part = tok[b * tokens + r : b * tokens + r + 32, :].astype(F32)
                    square = part * part
                    acc = square[:, :128]
                    for j in range(1, width // 128):
                        acc = acc + square[:, j * 128 : (j + 1) * 128]
                    accs.append(acc)
                    down = lax.rsqrt(jnp.sum(acc, axis=1, keepdims=True) + EPS)
                    normed[r : r + 32, :] = (part * down).astype(BF16)
                acc = jnp.concatenate(accs, axis=0)
                rinv_s[b, :, i * 128 : (i + 1) * 128] = lax.rsqrt(
                    jnp.sum(acc.T, axis=0, keepdims=True) + EPS
                )
        logits = dot(keysn[...], normed[...], NT) * scale
        expo = jnp.exp(logits)
        disp = expo / jnp.sum(expo, axis=1, keepdims=True)
        comb = expo / jnp.sum(expo, axis=0, keepdims=True)
        logit_s[b] = logits
        disp_s[b] = disp
        comb_s[b] = comb
        disp_b = disp.astype(BF16)
        at[b, experts:, :] = disp_b
        spread = selector(images * experts, experts, images, b)
        mix_in[:, rows] = dot(spread, disp_b).astype(BF16)
        mix_grad[:, rows] = dot(spread, comb.astype(BF16)).astype(BF16)

    def remote(src, dst, send, recv, device):
        return pltpu.make_async_remote_copy(
            src_ref=src, dst_ref=dst, send_sem=send, recv_sem=recv,
            device_id=device, device_id_type=MESH,
        )

    def pack(rows_ref, start, blocks_ref, first, count):
        for i in range(count):
            rows_ref[start + i * images : start + (i + 1) * images, :] = blocks_ref[first + i]

    def out_of_experts(kind, out_ref, in_ref):
        def one(p, ee, device):
            remote(
                out_ref.at[ee], in_ref.at[p], send_sem.at[kind], in_sem.at[kind, p // layer], device
            ).start()

        each_partner(one)
        in_ref[0] = out_ref[ex]

    def unpack(blocks_ref, value):
        for i in range(experts):
            blocks_ref[i] = value[i * images : (i + 1) * images, :]

    unpack(send_in, dot(mix_in[...], tok[...]).astype(BF16))
    pl.semaphore_wait(barrier, near + 1)
    out_of_experts(0, send_in, recv_in)
    for one in cot_loads:
        one.wait()
    unpack(send_grad, dot(mix_grad[...], cot[...]).astype(BF16))
    out_of_experts(1, send_grad, recv_grad)

    def arrive(kind, in_ref, rows_ref):
        copies = []
        for group in range(ny):
            count = layer if group else layer - 1
            wait_for(in_ref.at[pl.ds(0, count)], in_sem.at[kind, group])
            pack(rows_ref, group * layer * images, in_ref, group * layer, layer)
            mine = pl.ds(group * layer * images, layer * images)
            theirs = pl.ds(half + group * layer * images, layer * images)
            copies.append(
                remote(
                    rows_ref.at[mine], rows_ref.at[theirs],
                    part_sem.at[kind, group], twin_sem.at[kind, group], twin,
                )
            )
            copies[-1].start()
        return copies

    copies_in = arrive(0, recv_in, x)
    for one in weight_loads:
        one.wait()
    for one in copies_in:
        one.wait_recv()

    step = min(256, hidden)

    def first(j, carry):
        cols = pl.ds(pl.multiple_of(j * step, step), step)
        pre = dot(x[...], w1[:, cols])
        cdf = 0.5 * (1.0 + lax.erf(pre * 0.7071067811865476))
        act[:, cols] = (pre * cdf).astype(BF16)
        slope[:, cols] = cdf + pre * jnp.exp(-0.5 * pre * pre) * 0.3989422804014327
        return carry

    lax.fori_loop(0, hidden // step, first, 0, unroll=2)

    wide = min(256, width)
    parts = -(-width // wide)

    def columns(j):
        return pl.ds(pl.multiple_of(jnp.minimum(j * wide, width - wide), 128), wide)

    def pair_copy(kind, j, src, dst):
        return remote(src.at[j], dst.at[j], send_sem.at[4 + kind], recv_sem.at[4 + kind], twin)

    def second(j, carry):
        res = dot(act[...], w2[:, columns(j)])
        pair_out[j] = res[half:].astype(BF16)
        pair_copy(0, j, pair_out, pair_out_r).start()
        own_out[j] = res[:half]
        return carry

    lax.fori_loop(0, parts, second, 0)

    copies_grad = arrive(1, recv_grad, gs)

    def third(j, carry):
        cols = pl.ds(pl.multiple_of(j * step, step), step)
        pg[:, cols] = (dot(gs[...], w2[cols, :], NT) * slope[:, cols]).astype(BF16)
        return carry

    def chip_sums(kind, own, pair_r, rows_ref, out_ref, in_ref):
        wait_for(pair_r, recv_sem.at[4 + kind])
        for j in range(parts):
            start = min(j * wide, width - wide)
            rows_ref[:, start : start + wide] = (own[j] + pair_r[j].astype(F32)).astype(BF16)
        for p in range(near):
            out_ref[p] = rows_ref[p * images : (p + 1) * images, :]

        def one(p, ee, device):
            remote(
                out_ref.at[p], in_ref.at[p], send_sem.at[2 + kind], in_sem.at[2 + kind, p // layer],
                device,
            ).start()

        each_partner(one, -1)
        in_ref[0] = out_ref[0]

    chip_sums(0, own_out, pair_out_r, rows_out, send_out, recv_out)
    for one in copies_grad:
        one.wait_recv()
    lax.fori_loop(0, hidden // step, third, 0, unroll=2)

    def fourth(j, carry):
        res = dot(pg[...], w1[columns(j), :], NT)
        pair_back[j] = res[half:].astype(BF16)
        pair_copy(1, j, pair_back, pair_back_r).start()
        own_back[j] = res[:half]
        return carry

    lax.fori_loop(0, parts, fourth, 0)
    chip_sums(1, own_back, pair_back_r, rows_bk, send_bk, recv_bk)

    def turn(src, dst, size):
        same = selector(wide, wide, 1, 0)

        def one(j, carry):
            cols = pl.ds(pl.multiple_of(jnp.minimum(j * wide, size - wide), 128), wide)
            dst[cols, :] = dot(same, src[:, cols], NT).astype(BF16)
            return carry

        lax.fori_loop(0, -(-size // wide), one, 0)

    def product(left, right, out, size):
        def one(j, carry):
            rows = pl.ds(pl.multiple_of(j * size, 16), size)
            out[0, rows, :] = dot(left[rows, :], right[...]).astype(BF16)
            return carry

        lax.fori_loop(0, left.shape[0] // size, one, 0)

    turn(act, actt, hidden)
    product(actt, gs, go_o, hidden // 4)
    def collect(kind, in_ref, rows_ref):
        for group in range(ny):
            count = layer if group else layer - 1
            wait_for(in_ref.at[pl.ds(0, count)], in_sem.at[2 + kind, group])
            pack(rows_ref, group * layer * images, in_ref, group * layer, layer)

    i = lax.broadcasted_iota(jnp.int32, (images * experts, half), 0)
    j = lax.broadcasted_iota(jnp.int32, (1, half), 1)
    place = jnp.full((1, half), ex, jnp.int32)
    for p, offset in enumerate(offsets):
        place = jnp.where(j // images == p, device_at(*offset)[0], place)
    wanted = i == place + j % images * experts
    gather = jnp.where(wanted, 1.0, 0.0).astype(BF16)

    def gathered(rows_ref):
        return dot(gather, rows_ref[...]).astype(BF16)

    collect(0, recv_out, rows_out)
    slot_out = gathered(rows_out)
    parts_lg = []
    for b in range(images):
        rows = pl.ds(b * tokens, tokens)
        comb_grad = dot(slot_out[b * experts : (b + 1) * experts], cot[rows, :], NT)
        comb = comb_s[b]
        parts_lg.append(comb * (comb_grad - jnp.sum(comb * comb_grad, axis=0, keepdims=True)))

    collect(1, recv_bk, rows_bk)
    slot_back = gathered(rows_bk)
    keys_grad = None
    for b in range(images):
        rows = pl.ds(b * tokens, tokens)
        back = slot_back[b * experts : (b + 1) * experts]
        mix_b[b, :experts, :] = keysn[...]
        mix_b[b, experts:, :] = back
        disp_grad = dot(back, tok[rows, :], NT)
        disp = disp_s[b]
        lg = parts_lg[b] + disp * (disp_grad - jnp.sum(disp * disp_grad, axis=1, keepdims=True))
        rinv = rinv_s[b]
        scaled = (lg * (scale * rinv)).astype(BF16)
        at[b, :experts, :] = scaled
        mix_c[b] = rinv * rinv * jnp.sum(lg * logit_s[b], axis=0, keepdims=True)
        term = dot(scaled, tok[rows, :])
        keys_grad = term if keys_grad is None else keys_grad + term

    for e in range(experts):
        key_send[e] = keys_grad[e : e + 1, :]

    for dy, dx, dz in spread_offsets((ny, nx, nz))[1:]:
        ee = (ys[dy] + xs[dx]) * nz + z_ex[dz]
        remote(
            key_send.at[ee], key_recv.at[ex], send_sem.at[6], recv_sem.at[6],
            {"dp": dp, "expert": ee},
        ).start()
    key_recv[ex] = key_send[ex]
    most = pl.ds(0, experts - 1)

    per = min(256, tokens)

    def token_grads(b):
        def one(j, carry):
            cut = pl.ds(pl.multiple_of(j * per, per), per)
            rows = pl.ds(pl.multiple_of(b * tokens + j * per, per), per)
            res = dot(at[b, :, cut], mix_b[b], TN)
            col = jnp.broadcast_to(mix_c[b, :, cut], (128, per)).T
            for k in range(width // 128):
                cols = slice(k * 128, (k + 1) * 128)
                gt_o[b, cut, cols] = (res[:, cols] - tok[rows, cols].astype(F32) * col).astype(BF16)
            return carry

        lax.fori_loop(0, tokens // per, one, 0)

    turn(x, xt, width)
    product(xt, pg, gi_o, width // 4)
    for b in range(images // 2):
        token_grads(b)
    wait_for(key_recv.at[most], recv_sem.at[6])
    total = key_recv[0]
    for e in range(1, experts):
        total = total + key_recv[e]
    key_tot[dp] = total
    for k in range(1, 4):
        remote(
            key_tot.at[dp], key_tot.at[dp], send_sem.at[7], recv_sem.at[7],
            {"dp": (dp + k) % 4, "expert": ex},
        ).start()
    for b in range(images // 2, images):
        token_grads(b)
    wait_for(key_tot.at[pl.ds(0, 3)], recv_sem.at[7])
    grad = (key_tot[0] + key_tot[1]) + (key_tot[2] + key_tot[3])
    own = kt[pl.ds(ex, 1), :]
    r = lax.rsqrt(jnp.sum(own * own, axis=1, keepdims=True) + EPS)
    gk_o[...] = grad * r - own * (r * r * r * jnp.sum(grad * own, axis=1, keepdims=True))

    some = pl.ds(0, near - 1)
    for kind, ref in enumerate((recv_in, recv_grad, recv_out, recv_bk)):
        wait_for(ref.at[some], send_sem.at[kind])
    wait_for(pair_out, send_sem.at[4])
    wait_for(pair_back, send_sem.at[5])
    for one in copies_in + copies_grad:
        one.wait_send()
    wait_for(key_recv.at[most], send_sem.at[6])
    wait_for(key_tot.at[pl.ds(0, 3)], send_sem.at[7])


def slots(sizes, tokens, cotangents, w_in, w_out, keys, scale):
    images, toks, width, experts, hidden, ny, nx, nz = sizes
    near = 2 * experts
    rows = near * images * 2
    half = near * images
    wide = min(256, width)
    parts = -(-width // wide)
    vmem = pltpu.VMEM
    dma = pltpu.SemaphoreType.DMA
    any_space = pl.BlockSpec(memory_space=pl.ANY)
    local = pl.BlockSpec(memory_space=pltpu.VMEM)
    flops = 2 * rows * width * hidden * 4
    return pl.pallas_call(
        functools.partial(slot_kernel, sizes),
        out_shape=(
            vmem((images, toks, width), BF16),
            vmem((1, width, hidden), BF16),
            vmem((1, hidden, width), BF16),
            vmem((1, width), F32),
        ),
        in_specs=[any_space] * 4 + [local, pl.BlockSpec(memory_space=pltpu.SMEM)],
        out_specs=(local,) * 4,
        scratch_shapes=[
            vmem((images * toks, width), BF16),
            vmem((images * toks, width), BF16),
            vmem((width, hidden), BF16),
            vmem((hidden, width), BF16),
            vmem((images, 2 * experts, toks), BF16),
            vmem((images, 2 * experts, width), BF16),
            vmem((images, 1, toks), F32),
            vmem((experts, width), F32),
            vmem((experts, width), BF16),
            vmem((toks, width), BF16),
            vmem((images, 1, toks), F32),
            vmem((images, experts, toks), F32),
            vmem((images, experts, toks), F32),
            vmem((images, experts, toks), F32),
            vmem((images * experts, images * toks), BF16),
            vmem((images * experts, images * toks), BF16),
            vmem((experts, images, width), BF16),
            vmem((experts, images, width), BF16),
            vmem((near, images, width), BF16),
            vmem((near, images, width), BF16),
            vmem((rows, width), BF16),
            vmem((rows, width), BF16),
            vmem((rows, hidden), BF16),
            vmem((rows, hidden), F32),
            vmem((rows, hidden), BF16),
            vmem((width, rows), BF16),
            vmem((hidden, rows), BF16),
            vmem((parts, half, wide), F32),
            vmem((parts, half, wide), F32),
            vmem((parts, half, wide), BF16),
            vmem((parts, half, wide), BF16),
            vmem((parts, half, wide), BF16),
            vmem((parts, half, wide), BF16),
            vmem((near, images, width), BF16),
            vmem((near, images, width), BF16),
            vmem((near, images, width), BF16),
            vmem((near, images, width), BF16),
            vmem((half, width), BF16),
            vmem((half, width), BF16),
            vmem((experts, 1, width), F32),
            vmem((experts, 1, width), F32),
            vmem((4, 1, width), F32),
            dma((3 * images + 2,)),
            dma((8,)),
            dma((8,)),
            dma((4, ny)),
            dma((2, ny)),
            dma((2, ny)),
        ],
        compiler_params=pltpu.CompilerParams(
            collective_id=0, has_side_effects=True, vmem_limit_bytes=44 * 1024 * 1024
        ),
        cost_estimate=pl.CostEstimate(
            flops=flops, bytes_accessed=4 * images * toks * width * 2, transcendentals=0
        ),
        name="slots",
    )(tokens, cotangents, w_in, w_out, keys, scale)


def store_kernel(gt, gi, go, gk, gt_h, gi_h, go_h, gk_h, sem):
    copies = []
    for src, dst in ((gi, gi_h), (go, go_h), (gt, gt_h), (gk, gk_h)):
        if len(src.shape) == 2:
            cuts = [(slice(None),)]
        elif src.shape[0] == 1:
            size = src.shape[1] // 4
            cuts = [(0, pl.ds(k * size, size)) for k in range(4)]
        else:
            cuts = [(k,) for k in range(src.shape[0])]
        for cut in cuts:
            copies.append(pltpu.make_async_copy(src.at[cut], dst.at[cut], sem.at[len(copies)]))
            copies[-1].start()
    for one in copies:
        one.wait()


def stored(*arrays):
    shape = jax.ShapeDtypeStruct
    return pl.pallas_call(
        store_kernel,
        out_shape=tuple(shape(one.shape, one.dtype) for one in arrays),
        in_specs=[pl.BlockSpec(memory_space=pltpu.VMEM)] * 4,
        out_specs=(pl.BlockSpec(memory_space=pl.ANY),) * 4,
        scratch_shapes=[pltpu.SemaphoreType.DMA((9 + arrays[0].shape[0],))],
        compiler_params=pltpu.CompilerParams(vmem_limit_bytes=4 * 1024 * 1024),
        cost_estimate=pl.CostEstimate(
            flops=0, bytes_accessed=2 * sum(one.size for one in arrays), transcendentals=0
        ),
        name="stored",
    )(*arrays)


def body(grid, tokens, slot_keys, logit_scale, w_in, w_out, grad_out):
    images, toks, width = tokens.shape
    sizes = (images, toks, width, slot_keys.shape[1], w_in.shape[2], *grid)
    gt, gi, go, gk = slots(sizes, tokens, grad_out, w_in, w_out, slot_keys.T, logit_scale)
    gt, gi, go, gk = stored(gt, gi, go, gk)
    return gt, gi, go, gk.reshape(width, 1)


def solution(mesh):
    experts = mesh.shape["expert"]
    nz = 2
    side = math.isqrt(experts // nz)
    grid = (experts // nz // side, side, nz)
    in_specs = (
        P(("dp", "expert"), None, None),
        P(),
        P(),
        P("expert", None, "dp"),
        P("expert", "dp", None),
        P(("dp", "expert"), None, None),
    )
    out_specs = (
        P(("dp", "expert"), None, None),
        P("expert", None, "dp"),
        P("expert", "dp", None),
        P(None, "expert"),
    )
    return jax.shard_map(
        functools.partial(body, grid),
        mesh=mesh,
        in_specs=in_specs,
        out_specs=out_specs,
        check_vma=False,
    )
```

```python
import functools
import math

import jax
import jax.numpy as jnp
from jax import lax
from jax.experimental import pallas as pl
from jax.experimental.pallas import tpu as pltpu
from jax.sharding import PartitionSpec as P

EPS = 1e-06
MESH = pl.DeviceIdType.MESH
F32 = jnp.float32
BF16 = jnp.bfloat16
NN = (((1,), (0,)), ((), ()))
NT = (((1,), (1,)), ((), ()))
TN = (((0,), (0,)), ((), ()))


def dot(a, b, dims=NN):
    return lax.dot_general(a, b, dims, preferred_element_type=F32)


def selector(rows, cols, stride, offset):
    i = lax.broadcasted_iota(jnp.int32, (rows, cols), 0)
    j = lax.broadcasted_iota(jnp.int32, (rows, cols), 1)
    return jnp.where(i == j * stride + offset, 1.0, 0.0).astype(BF16)


def wait_for(ref, sem):
    pltpu.make_async_copy(ref, ref, sem).wait()


def spread_offsets(dims):
    left = [
        (a, b, c) for a in range(dims[0]) for b in range(dims[1]) for c in range(dims[2])
    ][1:]
    share = {}
    for one in left:
        for kind in enumerate(one):
            share[kind] = share.get(kind, 0) + 1
    order, used, total = [(0, 0, 0)], dict.fromkeys(share, 0), len(left)
    while left:
        at = len(order)

        def uneven(one):
            taken = set(enumerate(one))
            return sum(
                (used[k] + (k in taken) - share[k] * at / total) ** 2 * (2 if k[1] else 1)
                for k in share
            )

        best = min(left, key=lambda one: (round(uneven(one), 9), one))
        left.remove(best)
        order.append(best)
        for kind in enumerate(best):
            used[kind] += 1
    near = lambda one: sum(min(d, n - d) for d, n in zip(one, dims))
    return order[:1] + sorted(order[1:], key=near, reverse=True)


def slot_kernel(
    sizes,
    tok_h, cot_h, w1_h, w2_h, keys_ref, scale_ref,
    gt_o, gi_o, go_o, gk_o,
    tok, cot, w1, w2, at, mix_b, mix_c,
    kt, keysn, normed, rinv_s, logit_s, disp_s, comb_s, mix_in, mix_grad,
    send_in, send_grad, recv_in, recv_grad,
    x, gs, act, slope, pg, xt, actt,
    own_out, own_back, pair_out, pair_back, pair_out_r, pair_back_r,
    send_out, send_bk, recv_out, recv_bk, rows_out, rows_bk,
    key_send, key_recv, key_tot,
    load_sem, send_sem, recv_sem, in_sem, twin_sem, part_sem,
):
    images, tokens, width, experts, hidden, ny, nx, nz = sizes
    layer = 2 * nx * nz
    near = ny * layer
    half = near * images
    scale = scale_ref[0]
    dp = lax.axis_index("dp")
    ex = lax.axis_index("expert")
    zh, core = dp // 2, dp % 2
    px, py = (ex // nz) % nx, ex // (nz * nx)
    pz = zh * nz + ex % nz
    twin = {"dp": zh * 2 + 1 - core, "expert": ex}

    zs = [(pz + d) % (2 * nz) for d in range(2 * nz)]
    xs = [(px + d) % nx for d in range(nx)]
    ys = [(py + d) % ny * nx for d in range(ny)]
    z_dp = [z // nz * 2 + core for z in zs]
    z_ex = [z % nz for z in zs]

    offsets = spread_offsets((ny, nx, 2 * nz))

    def device_at(dy, dx, dz):
        dz = dz % (2 * nz)
        ee = (ys[dy % ny] + xs[dx % nx]) * nz + z_ex[dz]
        return ee, {"dp": z_dp[dz], "expert": ee}

    def each_partner(body, sign=1):
        for p, (dy, dx, dz) in enumerate(offsets):
            if p:
                body(p, *device_at(sign * dy, sign * dx, sign * dz))

    def load(index, src, dst):
        return pltpu.make_async_copy(src, dst, load_sem.at[index])

    pieces = 2
    piece = tokens // pieces
    tok_loads = [
        load(
            b * pieces + p, tok_h.at[b, pl.ds(p * piece, piece)],
            tok.at[pl.ds(b * tokens + p * piece, piece)],
        )
        for b in range(images)
        for p in range(pieces)
    ]
    done = images * pieces
    cot_loads = [
        load(done + b, cot_h.at[b], cot.at[pl.ds(b * tokens, tokens)]) for b in range(images)
    ]
    done += images
    weight_loads = [load(done, w1_h.at[0], w1), load(done + 1, w2_h.at[0], w2)]
    barrier = pltpu.get_barrier_semaphore()

    def greet(p, ee, device):
        pl.semaphore_signal(barrier, inc=1, device_id=device, device_id_type=MESH)

    each_partner(greet)
    for far in (zh, 1 - zh):
        pl.semaphore_signal(
            barrier, inc=1, device_id={"dp": far * 2 + 1 - core, "expert": ex}, device_id_type=MESH
        )

    for one in tok_loads:
        one.start()

    key_rows = keys_ref[...].astype(F32)
    kt[...] = key_rows
    keysn[...] = (
        key_rows * lax.rsqrt(jnp.sum(key_rows * key_rows, axis=1, keepdims=True) + EPS)
    ).astype(BF16)

    for b in range(images):
        rows = pl.ds(b * tokens, tokens)
        for p in range(pieces):
            tok_loads[b * pieces + p].wait()
            if b == 0 and p == 0:
                for one in (*cot_loads, *weight_loads):
                    one.start()
            for i in range(p * piece // 128, (p + 1) * piece // 128):
                accs = []
                for r in range(i * 128, (i + 1) * 128, 32):
                    part = tok[b * tokens + r : b * tokens + r + 32, :].astype(F32)
                    square = part * part
                    acc = square[:, :128]
                    for j in range(1, width // 128):
                        acc = acc + square[:, j * 128 : (j + 1) * 128]
                    accs.append(acc)
                    down = lax.rsqrt(jnp.sum(acc, axis=1, keepdims=True) + EPS)
                    normed[r : r + 32, :] = (part * down).astype(BF16)
                acc = jnp.concatenate(accs, axis=0)
                rinv_s[b, :, i * 128 : (i + 1) * 128] = lax.rsqrt(
                    jnp.sum(acc.T, axis=0, keepdims=True) + EPS
                )
        logits = dot(keysn[...], normed[...], NT) * scale
        expo = jnp.exp(logits)
        disp = expo / jnp.sum(expo, axis=1, keepdims=True)
        comb = expo / jnp.sum(expo, axis=0, keepdims=True)
        logit_s[b] = logits
        disp_s[b] = disp
        comb_s[b] = comb
        disp_b = disp.astype(BF16)
        at[b, experts:, :] = disp_b
        spread = selector(images * experts, experts, images, b)
        mix_in[:, rows] = dot(spread, disp_b).astype(BF16)
        mix_grad[:, rows] = dot(spread, comb.astype(BF16)).astype(BF16)

    def remote(src, dst, send, recv, device):
        return pltpu.make_async_remote_copy(
            src_ref=src, dst_ref=dst, send_sem=send, recv_sem=recv,
            device_id=device, device_id_type=MESH,
        )

    def pack(rows_ref, start, blocks_ref, first, count):
        for i in range(count):
            rows_ref[start + i * images : start + (i + 1) * images, :] = blocks_ref[first + i]

    def out_of_experts(kind, out_ref, in_ref):
        def one(p, ee, device):
            remote(
                out_ref.at[ee], in_ref.at[p], send_sem.at[kind], in_sem.at[kind, p // layer], device
            ).start()

        each_partner(one)
        in_ref[0] = out_ref[ex]

    def unpack(blocks_ref, value):
        for i in range(experts):
            blocks_ref[i] = value[i * images : (i + 1) * images, :]

    unpack(send_in, dot(mix_in[...], tok[...]).astype(BF16))
    pl.semaphore_wait(barrier, near + 1)
    out_of_experts(0, send_in, recv_in)
    for one in cot_loads:
        one.wait()
    unpack(send_grad, dot(mix_grad[...], cot[...]).astype(BF16))
    out_of_experts(1, send_grad, recv_grad)

    def arrive(kind, in_ref, rows_ref):
        copies = []
        for group in range(ny):
            count = layer if group else layer - 1
            wait_for(in_ref.at[pl.ds(0, count)], in_sem.at[kind, group])
            pack(rows_ref, group * layer * images, in_ref, group * layer, layer)
            mine = pl.ds(group * layer * images, layer * images)
            theirs = pl.ds(half + group * layer * images, layer * images)
            copies.append(
                remote(
                    rows_ref.at[mine], rows_ref.at[theirs],
                    part_sem.at[kind, group], twin_sem.at[kind, group], twin,
                )
            )
            copies[-1].start()
        return copies

    copies_in = arrive(0, recv_in, x)
    for one in weight_loads:
        one.wait()
    for one in copies_in:
        one.wait_recv()

    step = min(256, hidden)

    def first(j, carry):
        cols = pl.ds(pl.multiple_of(j * step, step), step)
        pre = dot(x[...], w1[:, cols])
        cdf = 0.5 * (1.0 + lax.erf(pre * 0.7071067811865476))
        act[:, cols] = (pre * cdf).astype(BF16)
        slope[:, cols] = cdf + pre * jnp.exp(-0.5 * pre * pre) * 0.3989422804014327
        return carry

    lax.fori_loop(0, hidden // step, first, 0, unroll=2)

    wide = min(256, width)
    parts = -(-width // wide)

    def columns(j):
        return pl.ds(pl.multiple_of(jnp.minimum(j * wide, width - wide), 128), wide)

    def pair_copy(kind, j, src, dst):
        return remote(src.at[j], dst.at[j], send_sem.at[4 + kind], recv_sem.at[4 + kind], twin)

    def second(j, carry):
        res = dot(act[...], w2[:, columns(j)])
        pair_out[j] = res[half:].astype(BF16)
        pair_copy(0, j, pair_out, pair_out_r).start()
        own_out[j] = res[:half]
        return carry

    lax.fori_loop(0, parts, second, 0)

    copies_grad = arrive(1, recv_grad, gs)

    def third(j, carry):
        cols = pl.ds(pl.multiple_of(j * step, step), step)
        pg[:, cols] = (dot(gs[...], w2[cols, :], NT) * slope[:, cols]).astype(BF16)
        return carry

    def chip_sums(kind, own, pair_r, rows_ref, out_ref, in_ref):
        wait_for(pair_r, recv_sem.at[4 + kind])
        for j in range(parts):
            start = min(j * wide, width - wide)
            rows_ref[:, start : start + wide] = (own[j] + pair_r[j].astype(F32)).astype(BF16)
        for p in range(near):
            out_ref[p] = rows_ref[p * images : (p + 1) * images, :]

        def one(p, ee, device):
            remote(
                out_ref.at[p], in_ref.at[p], send_sem.at[2 + kind], in_sem.at[2 + kind, p // layer],
                device,
            ).start()

        each_partner(one, -1)
        in_ref[0] = out_ref[0]

    chip_sums(0, own_out, pair_out_r, rows_out, send_out, recv_out)
    for one in copies_grad:
        one.wait_recv()
    lax.fori_loop(0, hidden // step, third, 0, unroll=2)

    def fourth(j, carry):
        res = dot(pg[...], w1[columns(j), :], NT)
        pair_back[j] = res[half:].astype(BF16)
        pair_copy(1, j, pair_back, pair_back_r).start()
        own_back[j] = res[:half]
        return carry

    lax.fori_loop(0, parts, fourth, 0)
    chip_sums(1, own_back, pair_back_r, rows_bk, send_bk, recv_bk)

    def turn(src, dst, size):
        same = selector(wide, wide, 1, 0)

        def one(j, carry):
            cols = pl.ds(pl.multiple_of(jnp.minimum(j * wide, size - wide), 128), wide)
            dst[cols, :] = dot(same, src[:, cols], NT).astype(BF16)
            return carry

        lax.fori_loop(0, -(-size // wide), one, 0)

    def product(left, right, out, size):
        def one(j, carry):
            rows = pl.ds(pl.multiple_of(j * size, 16), size)
            out[0, rows, :] = dot(left[rows, :], right[...]).astype(BF16)
            return carry

        lax.fori_loop(0, left.shape[0] // size, one, 0)

    turn(act, actt, hidden)
    product(actt, gs, go_o, hidden // 4)
    def collect(kind, in_ref, rows_ref):
        for group in range(ny):
            count = layer if group else layer - 1
            wait_for(in_ref.at[pl.ds(0, count)], in_sem.at[2 + kind, group])
            pack(rows_ref, group * layer * images, in_ref, group * layer, layer)

    i = lax.broadcasted_iota(jnp.int32, (images * experts, half), 0)
    j = lax.broadcasted_iota(jnp.int32, (1, half), 1)
    place = jnp.full((1, half), ex, jnp.int32)
    for p, offset in enumerate(offsets):
        place = jnp.where(j // images == p, device_at(*offset)[0], place)
    wanted = i == place + j % images * experts
    gather = jnp.where(wanted, 1.0, 0.0).astype(BF16)

    def gathered(rows_ref):
        return dot(gather, rows_ref[...]).astype(BF16)

    collect(0, recv_out, rows_out)
    slot_out = gathered(rows_out)
    parts_lg = []
    for b in range(images):
        rows = pl.ds(b * tokens, tokens)
        comb_grad = dot(slot_out[b * experts : (b + 1) * experts], cot[rows, :], NT)
        comb = comb_s[b]
        parts_lg.append(comb * (comb_grad - jnp.sum(comb * comb_grad, axis=0, keepdims=True)))

    collect(1, recv_bk, rows_bk)
    slot_back = gathered(rows_bk)
    keys_grad = None
    for b in range(images):
        rows = pl.ds(b * tokens, tokens)
        back = slot_back[b * experts : (b + 1) * experts]
        mix_b[b, :experts, :] = keysn[...]
        mix_b[b, experts:, :] = back
        disp_grad = dot(back, tok[rows, :], NT)
        disp = disp_s[b]
        lg = parts_lg[b] + disp * (disp_grad - jnp.sum(disp * disp_grad, axis=1, keepdims=True))
        rinv = rinv_s[b]
        scaled = (lg * (scale * rinv)).astype(BF16)
        at[b, :experts, :] = scaled
        mix_c[b] = rinv * rinv * jnp.sum(lg * logit_s[b], axis=0, keepdims=True)
        term = dot(scaled, tok[rows, :])
        keys_grad = term if keys_grad is None else keys_grad + term

    for e in range(experts):
        key_send[e] = keys_grad[e : e + 1, :]

    for dy, dx, dz in spread_offsets((ny, nx, nz))[1:]:
        ee = (ys[dy] + xs[dx]) * nz + z_ex[dz]
        remote(
            key_send.at[ee], key_recv.at[ex], send_sem.at[6], recv_sem.at[6],
            {"dp": dp, "expert": ee},
        ).start()
    key_recv[ex] = key_send[ex]
    most = pl.ds(0, experts - 1)

    per = min(256, tokens)

    def token_grads(b):
        def one(j, carry):
            cut = pl.ds(pl.multiple_of(j * per, per), per)
            rows = pl.ds(pl.multiple_of(b * tokens + j * per, per), per)
            res = dot(at[b, :, cut], mix_b[b], TN)
            col = jnp.broadcast_to(mix_c[b, :, cut], (128, per)).T
            for k in range(width // 128):
                cols = slice(k * 128, (k + 1) * 128)
                gt_o[b, cut, cols] = (res[:, cols] - tok[rows, cols].astype(F32) * col).astype(BF16)
            return carry

        lax.fori_loop(0, tokens // per, one, 0)

    turn(x, xt, width)
    product(xt, pg, gi_o, width // 4)
    for b in range(images // 2):
        token_grads(b)
    wait_for(key_recv.at[most], recv_sem.at[6])
    total = key_recv[0]
    for e in range(1, experts):
        total = total + key_recv[e]
    key_tot[dp] = total
    for k in range(1, 4):
        remote(
            key_tot.at[dp], key_tot.at[dp], send_sem.at[7], recv_sem.at[7],
            {"dp": (dp + k) % 4, "expert": ex},
        ).start()
    for b in range(images // 2, images):
        token_grads(b)
    wait_for(key_tot.at[pl.ds(0, 3)], recv_sem.at[7])
    grad = (key_tot[0] + key_tot[1]) + (key_tot[2] + key_tot[3])
    own = kt[pl.ds(ex, 1), :]
    r = lax.rsqrt(jnp.sum(own * own, axis=1, keepdims=True) + EPS)
    gk_o[...] = grad * r - own * (r * r * r * jnp.sum(grad * own, axis=1, keepdims=True))

    some = pl.ds(0, near - 1)
    for kind, ref in enumerate((recv_in, recv_grad, recv_out, recv_bk)):
        wait_for(ref.at[some], send_sem.at[kind])
    wait_for(pair_out, send_sem.at[4])
    wait_for(pair_back, send_sem.at[5])
    for one in copies_in + copies_grad:
        one.wait_send()
    wait_for(key_recv.at[most], send_sem.at[6])
    wait_for(key_tot.at[pl.ds(0, 3)], send_sem.at[7])


def slots(sizes, tokens, cotangents, w_in, w_out, keys, scale):
    images, toks, width, experts, hidden, ny, nx, nz = sizes
    near = 2 * experts
    rows = near * images * 2
    half = near * images
    wide = min(256, width)
    parts = -(-width // wide)
    vmem = pltpu.VMEM
    dma = pltpu.SemaphoreType.DMA
    any_space = pl.BlockSpec(memory_space=pl.ANY)
    local = pl.BlockSpec(memory_space=pltpu.VMEM)
    flops = 2 * rows * width * hidden * 4
    return pl.pallas_call(
        functools.partial(slot_kernel, sizes),
        out_shape=(
            vmem((images, toks, width), BF16),
            vmem((1, width, hidden), BF16),
            vmem((1, hidden, width), BF16),
            vmem((1, width), F32),
        ),
        in_specs=[any_space] * 4 + [local, pl.BlockSpec(memory_space=pltpu.SMEM)],
        out_specs=(local,) * 4,
        scratch_shapes=[
            vmem((images * toks, width), BF16),
            vmem((images * toks, width), BF16),
            vmem((width, hidden), BF16),
            vmem((hidden, width), BF16),
            vmem((images, 2 * experts, toks), BF16),
            vmem((images, 2 * experts, width), BF16),
            vmem((images, 1, toks), F32),
            vmem((experts, width), F32),
            vmem((experts, width), BF16),
            vmem((toks, width), BF16),
            vmem((images, 1, toks), F32),
            vmem((images, experts, toks), F32),
            vmem((images, experts, toks), F32),
            vmem((images, experts, toks), F32),
            vmem((images * experts, images * toks), BF16),
            vmem((images * experts, images * toks), BF16),
            vmem((experts, images, width), BF16),
            vmem((experts, images, width), BF16),
            vmem((near, images, width), BF16),
            vmem((near, images, width), BF16),
            vmem((rows, width), BF16),
            vmem((rows, width), BF16),
            vmem((rows, hidden), BF16),
            vmem((rows, hidden), F32),
            vmem((rows, hidden), BF16),
            vmem((width, rows), BF16),
            vmem((hidden, rows), BF16),
            vmem((parts, half, wide), F32),
            vmem((parts, half, wide), F32),
            vmem((parts, half, wide), BF16),
            vmem((parts, half, wide), BF16),
            vmem((parts, half, wide), BF16),
            vmem((parts, half, wide), BF16),
            vmem((near, images, width), BF16),
            vmem((near, images, width), BF16),
            vmem((near, images, width), BF16),
            vmem((near, images, width), BF16),
            vmem((half, width), BF16),
            vmem((half, width), BF16),
            vmem((experts, 1, width), F32),
            vmem((experts, 1, width), F32),
            vmem((4, 1, width), F32),
            dma((3 * images + 2,)),
            dma((8,)),
            dma((8,)),
            dma((4, ny)),
            dma((2, ny)),
            dma((2, ny)),
        ],
        compiler_params=pltpu.CompilerParams(
            collective_id=0, has_side_effects=True, vmem_limit_bytes=44 * 1024 * 1024
        ),
        cost_estimate=pl.CostEstimate(
            flops=flops, bytes_accessed=4 * images * toks * width * 2, transcendentals=0
        ),
        name="slots",
    )(tokens, cotangents, w_in, w_out, keys, scale)


def store_kernel(gt, gi, go, gk, gt_h, gi_h, go_h, gk_h, sem):
    copies = []
    for src, dst in ((gi, gi_h), (go, go_h), (gt, gt_h), (gk, gk_h)):
        if len(src.shape) == 2:
            cuts = [(slice(None),)]
        elif src.shape[0] == 1:
            size = src.shape[1] // 4
            cuts = [(0, pl.ds(k * size, size)) for k in range(4)]
        else:
            cuts = [(k,) for k in range(src.shape[0])]
        for cut in cuts:
            copies.append(pltpu.make_async_copy(src.at[cut], dst.at[cut], sem.at[len(copies)]))
            copies[-1].start()
    for one in copies:
        one.wait()


def stored(*arrays):
    shape = jax.ShapeDtypeStruct
    return pl.pallas_call(
        store_kernel,
        out_shape=tuple(shape(one.shape, one.dtype) for one in arrays),
        in_specs=[pl.BlockSpec(memory_space=pltpu.VMEM)] * 4,
        out_specs=(pl.BlockSpec(memory_space=pl.ANY),) * 4,
        scratch_shapes=[pltpu.SemaphoreType.DMA((9 + arrays[0].shape[0],))],
        compiler_params=pltpu.CompilerParams(vmem_limit_bytes=4 * 1024 * 1024),
        cost_estimate=pl.CostEstimate(
            flops=0, bytes_accessed=2 * sum(one.size for one in arrays), transcendentals=0
        ),
        name="stored",
    )(*arrays)


def body(grid, tokens, slot_keys, logit_scale, w_in, w_out, grad_out):
    images, toks, width = tokens.shape
    sizes = (images, toks, width, slot_keys.shape[1], w_in.shape[2], *grid)
    gt, gi, go, gk = slots(sizes, tokens, grad_out, w_in, w_out, slot_keys.T, logit_scale)
    gt, gi, go, gk = stored(gt, gi, go, gk)
    return gt, gi, go, gk.reshape(width, 1)


def solution(mesh):
    experts = mesh.shape["expert"]
    nz = 2
    side = math.isqrt(experts // nz)
    grid = (experts // nz // side, side, nz)
    in_specs = (
        P(("dp", "expert"), None, None),
        P(),
        P(),
        P("expert", None, "dp"),
        P("expert", "dp", None),
        P(("dp", "expert"), None, None),
    )
    out_specs = (
        P(("dp", "expert"), None, None),
        P("expert", None, "dp"),
        P("expert", "dp", None),
        P(None, "expert"),
    )
    return jax.shard_map(
        functools.partial(body, grid),
        mesh=mesh,
        in_specs=in_specs,
        out_specs=out_specs,
        check_vma=False,
    )
```

```python
import functools
import math

import jax
import jax.numpy as jnp
from jax import lax
from jax.experimental import pallas as pl
from jax.experimental.pallas import tpu as pltpu
from jax.sharding import PartitionSpec as P

EPS = 1e-06
MESH = pl.DeviceIdType.MESH
F32 = jnp.float32
BF16 = jnp.bfloat16
NN = (((1,), (0,)), ((), ()))
NT = (((1,), (1,)), ((), ()))
TN = (((0,), (0,)), ((), ()))


def dot(a, b, dims=NN):
    return lax.dot_general(a, b, dims, preferred_element_type=F32)


def selector(rows, cols, stride, offset):
    i = lax.broadcasted_iota(jnp.int32, (rows, cols), 0)
    j = lax.broadcasted_iota(jnp.int32, (rows, cols), 1)
    return jnp.where(i == j * stride + offset, 1.0, 0.0).astype(BF16)


def wait_for(ref, sem):
    pltpu.make_async_copy(ref, ref, sem).wait()


def spread_offsets(dims):
    left = [
        (a, b, c) for a in range(dims[0]) for b in range(dims[1]) for c in range(dims[2])
    ][1:]
    share = {}
    for one in left:
        for kind in enumerate(one):
            share[kind] = share.get(kind, 0) + 1
    order, used, total = [(0, 0, 0)], dict.fromkeys(share, 0), len(left)
    while left:
        at = len(order)

        def uneven(one):
            taken = set(enumerate(one))
            return sum(
                (used[k] + (k in taken) - share[k] * at / total) ** 2 * (2 if k[1] else 1)
                for k in share
            )

        best = min(left, key=lambda one: (round(uneven(one), 9), one))
        left.remove(best)
        order.append(best)
        for kind in enumerate(best):
            used[kind] += 1
    near = lambda one: sum(min(d, n - d) for d, n in zip(one, dims))
    return order[:1] + sorted(order[1:], key=near, reverse=True)


def slot_kernel(
    sizes,
    tok_h, cot_h, w1_h, w2_h, keys_ref, scale_ref,
    gt_o, gi_o, go_o, gk_o,
    tok, cot, w1, w2, at, mix_b, mix_c,
    kt, keysn, normed, rinv_s, logit_s, disp_s, comb_s, mix_in, mix_grad,
    send_in, send_grad, recv_in, recv_grad,
    x, gs, act, slope, pg, xt, actt,
    own_out, own_back, pair_out, pair_back, pair_out_r, pair_back_r,
    send_out, send_bk, recv_out, recv_bk, rows_out, rows_bk,
    key_send, key_recv, key_tot,
    load_sem, send_sem, recv_sem, in_sem, twin_sem, part_sem,
):
    images, tokens, width, experts, hidden, ny, nx, nz = sizes
    layer = 2 * nx * nz
    near = ny * layer
    half = near * images
    scale = scale_ref[0]
    dp = lax.axis_index("dp")
    ex = lax.axis_index("expert")
    zh, core = dp // 2, dp % 2
    px, py = (ex // nz) % nx, ex // (nz * nx)
    pz = zh * nz + ex % nz
    twin = {"dp": zh * 2 + 1 - core, "expert": ex}

    zs = [(pz + d) % (2 * nz) for d in range(2 * nz)]
    xs = [(px + d) % nx for d in range(nx)]
    ys = [(py + d) % ny * nx for d in range(ny)]
    z_dp = [z // nz * 2 + core for z in zs]
    z_ex = [z % nz for z in zs]

    offsets = spread_offsets((ny, nx, 2 * nz))

    def device_at(dy, dx, dz):
        dz = dz % (2 * nz)
        ee = (ys[dy % ny] + xs[dx % nx]) * nz + z_ex[dz]
        return ee, {"dp": z_dp[dz], "expert": ee}

    def each_partner(body, sign=1):
        for p, (dy, dx, dz) in enumerate(offsets):
            if p:
                body(p, *device_at(sign * dy, sign * dx, sign * dz))

    def load(index, src, dst):
        return pltpu.make_async_copy(src, dst, load_sem.at[index])

    pieces = 2
    piece = tokens // pieces
    tok_loads = [
        load(
            b * pieces + p, tok_h.at[b, pl.ds(p * piece, piece)],
            tok.at[pl.ds(b * tokens + p * piece, piece)],
        )
        for b in range(images)
        for p in range(pieces)
    ]
    done = images * pieces
    cot_loads = [
        load(done + b, cot_h.at[b], cot.at[pl.ds(b * tokens, tokens)]) for b in range(images)
    ]
    done += images
    weight_loads = [load(done, w1_h.at[0], w1), load(done + 1, w2_h.at[0], w2)]
    barrier = pltpu.get_barrier_semaphore()

    def greet(p, ee, device):
        pl.semaphore_signal(barrier, inc=1, device_id=device, device_id_type=MESH)

    each_partner(greet)
    for far in (zh, 1 - zh):
        pl.semaphore_signal(
            barrier, inc=1, device_id={"dp": far * 2 + 1 - core, "expert": ex}, device_id_type=MESH
        )

    for one in tok_loads:
        one.start()

    key_rows = keys_ref[...].astype(F32)
    kt[...] = key_rows
    keysn[...] = (
        key_rows * lax.rsqrt(jnp.sum(key_rows * key_rows, axis=1, keepdims=True) + EPS)
    ).astype(BF16)

    for b in range(images):
        rows = pl.ds(b * tokens, tokens)
        for p in range(pieces):
            tok_loads[b * pieces + p].wait()
            if b == 0 and p == 0:
                for one in (*cot_loads, *weight_loads):
                    one.start()
            for i in range(p * piece // 128, (p + 1) * piece // 128):
                accs = []
                for r in range(i * 128, (i + 1) * 128, 32):
                    part = tok[b * tokens + r : b * tokens + r + 32, :].astype(F32)
                    square = part * part
                    acc = square[:, :128]
                    for j in range(1, width // 128):
                        acc = acc + square[:, j * 128 : (j + 1) * 128]
                    accs.append(acc)
                    down = lax.rsqrt(jnp.sum(acc, axis=1, keepdims=True) + EPS)
                    normed[r : r + 32, :] = (part * down).astype(BF16)
                acc = jnp.concatenate(accs, axis=0)
                rinv_s[b, :, i * 128 : (i + 1) * 128] = lax.rsqrt(
                    jnp.sum(acc.T, axis=0, keepdims=True) + EPS
                )
        logits = dot(keysn[...], normed[...], NT) * scale
        expo = jnp.exp(logits)
        disp = expo / jnp.sum(expo, axis=1, keepdims=True)
        comb = expo / jnp.sum(expo, axis=0, keepdims=True)
        logit_s[b] = logits
        disp_s[b] = disp
        comb_s[b] = comb
        disp_b = disp.astype(BF16)
        at[b, experts:, :] = disp_b
        spread = selector(images * experts, experts, images, b)
        mix_in[:, rows] = dot(spread, disp_b).astype(BF16)
        mix_grad[:, rows] = dot(spread, comb.astype(BF16)).astype(BF16)

    def remote(src, dst, send, recv, device):
        return pltpu.make_async_remote_copy(
            src_ref=src, dst_ref=dst, send_sem=send, recv_sem=recv,
            device_id=device, device_id_type=MESH,
        )

    def pack(rows_ref, start, blocks_ref, first, count):
        for i in range(count):
            rows_ref[start + i * images : start + (i + 1) * images, :] = blocks_ref[first + i]

    def out_of_experts(kind, out_ref, in_ref):
        def one(p, ee, device):
            remote(
                out_ref.at[ee], in_ref.at[p], send_sem.at[kind], in_sem.at[kind, p // layer], device
            ).start()

        each_partner(one)
        in_ref[0] = out_ref[ex]

    def unpack(blocks_ref, value):
        for i in range(experts):
            blocks_ref[i] = value[i * images : (i + 1) * images, :]

    unpack(send_in, dot(mix_in[...], tok[...]).astype(BF16))
    pl.semaphore_wait(barrier, near + 1)
    out_of_experts(0, send_in, recv_in)
    for one in cot_loads:
        one.wait()
    unpack(send_grad, dot(mix_grad[...], cot[...]).astype(BF16))
    out_of_experts(1, send_grad, recv_grad)

    def arrive(kind, in_ref, rows_ref):
        copies = []
        for group in range(ny):
            count = layer if group else layer - 1
            wait_for(in_ref.at[pl.ds(0, count)], in_sem.at[kind, group])
            pack(rows_ref, group * layer * images, in_ref, group * layer, layer)
            mine = pl.ds(group * layer * images, layer * images)
            theirs = pl.ds(half + group * layer * images, layer * images)
            copies.append(
                remote(
                    rows_ref.at[mine], rows_ref.at[theirs],
                    part_sem.at[kind, group], twin_sem.at[kind, group], twin,
                )
            )
            copies[-1].start()
        return copies

    copies_in = arrive(0, recv_in, x)
    for one in weight_loads:
        one.wait()
    for one in copies_in:
        one.wait_recv()

    step = min(256, hidden)

    def first(j, carry):
        cols = pl.ds(pl.multiple_of(j * step, step), step)
        pre = dot(x[...], w1[:, cols])
        cdf = 0.5 * (1.0 + lax.erf(pre * 0.7071067811865476))
        act[:, cols] = (pre * cdf).astype(BF16)
        slope[:, cols] = cdf + pre * jnp.exp(-0.5 * pre * pre) * 0.3989422804014327
        return carry

    lax.fori_loop(0, hidden // step, first, 0, unroll=2)

    wide = min(256, width)
    parts = -(-width // wide)

    def columns(j):
        return pl.ds(pl.multiple_of(jnp.minimum(j * wide, width - wide), 128), wide)

    def pair_copy(kind, j, src, dst):
        return remote(src.at[j], dst.at[j], send_sem.at[4 + kind], recv_sem.at[4 + kind], twin)

    def second(j, carry):
        res = dot(act[...], w2[:, columns(j)])
        pair_out[j] = res[half:].astype(BF16)
        pair_copy(0, j, pair_out, pair_out_r).start()
        own_out[j] = res[:half]
        return carry

    lax.fori_loop(0, parts, second, 0)

    copies_grad = arrive(1, recv_grad, gs)

    def third(j, carry):
        cols = pl.ds(pl.multiple_of(j * step, step), step)
        pg[:, cols] = (dot(gs[...], w2[cols, :], NT) * slope[:, cols]).astype(BF16)
        return carry

    def chip_sums(kind, own, pair_r, rows_ref, out_ref, in_ref):
        wait_for(pair_r, recv_sem.at[4 + kind])
        for j in range(parts):
            start = min(j * wide, width - wide)
            rows_ref[:, start : start + wide] = (own[j] + pair_r[j].astype(F32)).astype(BF16)
        def one(p, ee, device):
            if p % layer == 1:
                for i in range(p, min(p + layer, near)):
                    out_ref[i] = rows_ref[i * images : (i + 1) * images, :]
            remote(
                out_ref.at[p], in_ref.at[p], send_sem.at[2 + kind], in_sem.at[2 + kind, p // layer],
                device,
            ).start()

        each_partner(one, -1)
        in_ref[0] = rows_ref[:images, :]

    chip_sums(0, own_out, pair_out_r, rows_out, send_out, recv_out)
    for one in copies_grad:
        one.wait_recv()
    lax.fori_loop(0, hidden // step, third, 0, unroll=2)

    def fourth(j, carry):
        res = dot(pg[...], w1[columns(j), :], NT)
        pair_back[j] = res[half:].astype(BF16)
        pair_copy(1, j, pair_back, pair_back_r).start()
        own_back[j] = res[:half]
        return carry

    lax.fori_loop(0, parts, fourth, 0)
    chip_sums(1, own_back, pair_back_r, rows_bk, send_bk, recv_bk)

    def turn(src, dst, size):
        same = selector(wide, wide, 1, 0)

        def one(j, carry):
            cols = pl.ds(pl.multiple_of(jnp.minimum(j * wide, size - wide), 128), wide)
            dst[cols, :] = dot(same, src[:, cols], NT).astype(BF16)
            return carry

        lax.fori_loop(0, -(-size // wide), one, 0)

    def product(left, right, out, size):
        def one(j, carry):
            rows = pl.ds(pl.multiple_of(j * size, 16), size)
            out[0, rows, :] = dot(left[rows, :], right[...]).astype(BF16)
            return carry

        lax.fori_loop(0, left.shape[0] // size, one, 0)

    turn(act, actt, hidden)
    product(actt, gs, go_o, hidden // 4)
    def collect(kind, in_ref, rows_ref):
        for group in range(ny):
            count = layer if group else layer - 1
            wait_for(in_ref.at[pl.ds(0, count)], in_sem.at[2 + kind, group])
            pack(rows_ref, group * layer * images, in_ref, group * layer, layer)

    i = lax.broadcasted_iota(jnp.int32, (images * experts, half), 0)
    j = lax.broadcasted_iota(jnp.int32, (1, half), 1)
    place = jnp.full((1, half), ex, jnp.int32)
    for p, offset in enumerate(offsets):
        place = jnp.where(j // images == p, device_at(*offset)[0], place)
    wanted = i == place + j % images * experts
    gather = jnp.where(wanted, 1.0, 0.0).astype(BF16)

    def gathered(rows_ref):
        return dot(gather, rows_ref[...]).astype(BF16)

    collect(0, recv_out, rows_out)
    slot_out = gathered(rows_out)
    parts_lg = []
    for b in range(images):
        rows = pl.ds(b * tokens, tokens)
        comb_grad = dot(slot_out[b * experts : (b + 1) * experts], cot[rows, :], NT)
        comb = comb_s[b]
        parts_lg.append(comb * (comb_grad - jnp.sum(comb * comb_grad, axis=0, keepdims=True)))

    collect(1, recv_bk, rows_bk)
    slot_back = gathered(rows_bk)
    keys_grad = None
    for b in range(images):
        rows = pl.ds(b * tokens, tokens)
        back = slot_back[b * experts : (b + 1) * experts]
        mix_b[b, :experts, :] = keysn[...]
        mix_b[b, experts:, :] = back
        disp_grad = dot(back, tok[rows, :], NT)
        disp = disp_s[b]
        lg = parts_lg[b] + disp * (disp_grad - jnp.sum(disp * disp_grad, axis=1, keepdims=True))
        rinv = rinv_s[b]
        scaled = (lg * (scale * rinv)).astype(BF16)
        at[b, :experts, :] = scaled
        mix_c[b] = rinv * rinv * jnp.sum(lg * logit_s[b], axis=0, keepdims=True)
        term = dot(scaled, tok[rows, :])
        keys_grad = term if keys_grad is None else keys_grad + term

    for e in range(experts):
        key_send[e] = keys_grad[e : e + 1, :]

    for dy, dx, dz in spread_offsets((ny, nx, nz))[1:]:
        ee = (ys[dy] + xs[dx]) * nz + z_ex[dz]
        remote(
            key_send.at[ee], key_recv.at[ex], send_sem.at[6], recv_sem.at[6],
            {"dp": dp, "expert": ee},
        ).start()
    key_recv[ex] = key_send[ex]
    most = pl.ds(0, experts - 1)

    per = min(256, tokens)

    def token_grads(b):
        def one(j, carry):
            cut = pl.ds(pl.multiple_of(j * per, per), per)
            rows = pl.ds(pl.multiple_of(b * tokens + j * per, per), per)
            res = dot(at[b, :, cut], mix_b[b], TN)
            col = jnp.broadcast_to(mix_c[b, :, cut], (128, per)).T
            for k in range(width // 128):
                cols = slice(k * 128, (k + 1) * 128)
                gt_o[b, cut, cols] = (res[:, cols] - tok[rows, cols].astype(F32) * col).astype(BF16)
            return carry

        lax.fori_loop(0, tokens // per, one, 0)

    turn(x, xt, width)
    product(xt, pg, gi_o, width // 4)
    for b in range(images // 2):
        token_grads(b)
    wait_for(key_recv.at[most], recv_sem.at[6])
    total = key_recv[0]
    for e in range(1, experts):
        total = total + key_recv[e]
    key_tot[dp] = total
    for k in range(1, 4):
        remote(
            key_tot.at[dp], key_tot.at[dp], send_sem.at[7], recv_sem.at[7],
            {"dp": (dp + k) % 4, "expert": ex},
        ).start()
    for b in range(images // 2, images):
        token_grads(b)
    wait_for(key_tot.at[pl.ds(0, 3)], recv_sem.at[7])
    grad = (key_tot[0] + key_tot[1]) + (key_tot[2] + key_tot[3])
    own = kt[pl.ds(ex, 1), :]
    r = lax.rsqrt(jnp.sum(own * own, axis=1, keepdims=True) + EPS)
    gk_o[...] = grad * r - own * (r * r * r * jnp.sum(grad * own, axis=1, keepdims=True))

    some = pl.ds(0, near - 1)
    for kind, ref in enumerate((recv_in, recv_grad, recv_out, recv_bk)):
        wait_for(ref.at[some], send_sem.at[kind])
    wait_for(pair_out, send_sem.at[4])
    wait_for(pair_back, send_sem.at[5])
    for one in copies_in + copies_grad:
        one.wait_send()
    wait_for(key_recv.at[most], send_sem.at[6])
    wait_for(key_tot.at[pl.ds(0, 3)], send_sem.at[7])


def slots(sizes, tokens, cotangents, w_in, w_out, keys, scale):
    images, toks, width, experts, hidden, ny, nx, nz = sizes
    near = 2 * experts
    rows = near * images * 2
    half = near * images
    wide = min(256, width)
    parts = -(-width // wide)
    vmem = pltpu.VMEM
    dma = pltpu.SemaphoreType.DMA
    any_space = pl.BlockSpec(memory_space=pl.ANY)
    local = pl.BlockSpec(memory_space=pltpu.VMEM)
    flops = 2 * rows * width * hidden * 4
    return pl.pallas_call(
        functools.partial(slot_kernel, sizes),
        out_shape=(
            vmem((images, toks, width), BF16),
            vmem((1, width, hidden), BF16),
            vmem((1, hidden, width), BF16),
            vmem((1, width), F32),
        ),
        in_specs=[any_space] * 4 + [local, pl.BlockSpec(memory_space=pltpu.SMEM)],
        out_specs=(local,) * 4,
        scratch_shapes=[
            vmem((images * toks, width), BF16),
            vmem((images * toks, width), BF16),
            vmem((width, hidden), BF16),
            vmem((hidden, width), BF16),
            vmem((images, 2 * experts, toks), BF16),
            vmem((images, 2 * experts, width), BF16),
            vmem((images, 1, toks), F32),
            vmem((experts, width), F32),
            vmem((experts, width), BF16),
            vmem((toks, width), BF16),
            vmem((images, 1, toks), F32),
            vmem((images, experts, toks), F32),
            vmem((images, experts, toks), F32),
            vmem((images, experts, toks), F32),
            vmem((images * experts, images * toks), BF16),
            vmem((images * experts, images * toks), BF16),
            vmem((experts, images, width), BF16),
            vmem((experts, images, width), BF16),
            vmem((near, images, width), BF16),
            vmem((near, images, width), BF16),
            vmem((rows, width), BF16),
            vmem((rows, width), BF16),
            vmem((rows, hidden), BF16),
            vmem((rows, hidden), F32),
            vmem((rows, hidden), BF16),
            vmem((width, rows), BF16),
            vmem((hidden, rows), BF16),
            vmem((parts, half, wide), F32),
            vmem((parts, half, wide), F32),
            vmem((parts, half, wide), BF16),
            vmem((parts, half, wide), BF16),
            vmem((parts, half, wide), BF16),
            vmem((parts, half, wide), BF16),
            vmem((near, images, width), BF16),
            vmem((near, images, width), BF16),
            vmem((near, images, width), BF16),
            vmem((near, images, width), BF16),
            vmem((half, width), BF16),
            vmem((half, width), BF16),
            vmem((experts, 1, width), F32),
            vmem((experts, 1, width), F32),
            vmem((4, 1, width), F32),
            dma((3 * images + 2,)),
            dma((8,)),
            dma((8,)),
            dma((4, ny)),
            dma((2, ny)),
            dma((2, ny)),
        ],
        compiler_params=pltpu.CompilerParams(
            collective_id=0, has_side_effects=True, vmem_limit_bytes=44 * 1024 * 1024
        ),
        cost_estimate=pl.CostEstimate(
            flops=flops, bytes_accessed=4 * images * toks * width * 2, transcendentals=0
        ),
        name="slots",
    )(tokens, cotangents, w_in, w_out, keys, scale)


def store_kernel(gt, gi, go, gk, gt_h, gi_h, go_h, gk_h, sem):
    copies = []
    for src, dst in ((gi, gi_h), (go, go_h), (gt, gt_h), (gk, gk_h)):
        if len(src.shape) == 2:
            cuts = [(slice(None),)]
        elif src.shape[0] == 1:
            size = src.shape[1] // 4
            cuts = [(0, pl.ds(k * size, size)) for k in range(4)]
        else:
            cuts = [(k,) for k in range(src.shape[0])]
        for cut in cuts:
            copies.append(pltpu.make_async_copy(src.at[cut], dst.at[cut], sem.at[len(copies)]))
            copies[-1].start()
    for one in copies:
        one.wait()


def stored(*arrays):
    shape = jax.ShapeDtypeStruct
    return pl.pallas_call(
        store_kernel,
        out_shape=tuple(shape(one.shape, one.dtype) for one in arrays),
        in_specs=[pl.BlockSpec(memory_space=pltpu.VMEM)] * 4,
        out_specs=(pl.BlockSpec(memory_space=pl.ANY),) * 4,
        scratch_shapes=[pltpu.SemaphoreType.DMA((9 + arrays[0].shape[0],))],
        compiler_params=pltpu.CompilerParams(vmem_limit_bytes=4 * 1024 * 1024),
        cost_estimate=pl.CostEstimate(
            flops=0, bytes_accessed=2 * sum(one.size for one in arrays), transcendentals=0
        ),
        name="stored",
    )(*arrays)


def body(grid, tokens, slot_keys, logit_scale, w_in, w_out, grad_out):
    images, toks, width = tokens.shape
    sizes = (images, toks, width, slot_keys.shape[1], w_in.shape[2], *grid)
    gt, gi, go, gk = slots(sizes, tokens, grad_out, w_in, w_out, slot_keys.T, logit_scale)
    gt, gi, go, gk = stored(gt, gi, go, gk)
    return gt, gi, go, gk.reshape(width, 1)


def solution(mesh):
    experts = mesh.shape["expert"]
    nz = 2
    side = math.isqrt(experts // nz)
    grid = (experts // nz // side, side, nz)
    in_specs = (
        P(("dp", "expert"), None, None),
        P(),
        P(),
        P("expert", None, "dp"),
        P("expert", "dp", None),
        P(("dp", "expert"), None, None),
    )
    out_specs = (
        P(("dp", "expert"), None, None),
        P("expert", None, "dp"),
        P("expert", "dp", None),
        P(None, "expert"),
    )
    return jax.shard_map(
        functools.partial(body, grid),
        mesh=mesh,
        in_specs=in_specs,
        out_specs=out_specs,
        check_vma=False,
    )
```

```python
import functools
import math

import jax
import jax.numpy as jnp
from jax import lax
from jax.experimental import pallas as pl
from jax.experimental.pallas import tpu as pltpu
from jax.sharding import PartitionSpec as P

EPS = 1e-06
MESH = pl.DeviceIdType.MESH
F32 = jnp.float32
BF16 = jnp.bfloat16
NN = (((1,), (0,)), ((), ()))
NT = (((1,), (1,)), ((), ()))
TN = (((0,), (0,)), ((), ()))


def dot(a, b, dims=NN):
    return lax.dot_general(a, b, dims, preferred_element_type=F32)


def selector(rows, cols, stride, offset):
    i = lax.broadcasted_iota(jnp.int32, (rows, cols), 0)
    j = lax.broadcasted_iota(jnp.int32, (rows, cols), 1)
    return jnp.where(i == j * stride + offset, 1.0, 0.0).astype(BF16)


def wait_for(ref, sem):
    pltpu.make_async_copy(ref, ref, sem).wait()


def spread_offsets(dims):
    left = [
        (a, b, c) for a in range(dims[0]) for b in range(dims[1]) for c in range(dims[2])
    ][1:]
    share = {}
    for one in left:
        for kind in enumerate(one):
            share[kind] = share.get(kind, 0) + 1
    order, used, total = [(0, 0, 0)], dict.fromkeys(share, 0), len(left)
    while left:
        at = len(order)

        def uneven(one):
            taken = set(enumerate(one))
            return sum(
                (used[k] + (k in taken) - share[k] * at / total) ** 2 * (2 if k[1] else 1)
                for k in share
            )

        best = min(left, key=lambda one: (round(uneven(one), 9), one))
        left.remove(best)
        order.append(best)
        for kind in enumerate(best):
            used[kind] += 1
    near = lambda one: sum(min(d, n - d) for d, n in zip(one, dims))
    return order[:1] + sorted(order[1:], key=near, reverse=True)


def slot_kernel(
    sizes,
    tok_h, cot_h, w1_h, w2_h, keys_ref, scale_ref,
    gt_o, gi_o, go_o, gk_o,
    tok, cot, w1, w2, at, mix_b, mix_c,
    kt, keysn, normed, rinv_s, logit_s, disp_s, comb_s, mix_in, mix_grad,
    send_in, send_grad, recv_in, recv_grad,
    x, gs, act, slope, pg, xt, actt,
    own_out, own_back, pair_out, pair_back, pair_out_r, pair_back_r,
    send_out, send_bk, recv_out, recv_bk, rows_out, rows_bk,
    key_send, key_recv, key_tot,
    load_sem, send_sem, recv_sem, in_sem, twin_sem, part_sem,
):
    images, tokens, width, experts, hidden, ny, nx, nz = sizes
    layer = 2 * nx * nz
    near = ny * layer
    half = near * images
    scale = scale_ref[0]
    dp = lax.axis_index("dp")
    ex = lax.axis_index("expert")
    zh, core = dp // 2, dp % 2
    px, py = (ex // nz) % nx, ex // (nz * nx)
    pz = zh * nz + ex % nz
    twin = {"dp": zh * 2 + 1 - core, "expert": ex}

    zs = [(pz + d) % (2 * nz) for d in range(2 * nz)]
    xs = [(px + d) % nx for d in range(nx)]
    ys = [(py + d) % ny * nx for d in range(ny)]
    z_dp = [z // nz * 2 + core for z in zs]
    z_ex = [z % nz for z in zs]

    offsets = spread_offsets((ny, nx, 2 * nz))

    def device_at(dy, dx, dz):
        dz = dz % (2 * nz)
        ee = (ys[dy % ny] + xs[dx % nx]) * nz + z_ex[dz]
        return ee, {"dp": z_dp[dz], "expert": ee}

    def each_partner(body, sign=1):
        for p, (dy, dx, dz) in enumerate(offsets):
            if p:
                body(p, *device_at(sign * dy, sign * dx, sign * dz))

    def load(index, src, dst):
        return pltpu.make_async_copy(src, dst, load_sem.at[index])

    pieces = 2
    piece = tokens // pieces
    tok_loads = [
        load(
            b * pieces + p, tok_h.at[b, pl.ds(p * piece, piece)],
            tok.at[pl.ds(b * tokens + p * piece, piece)],
        )
        for b in range(images)
        for p in range(pieces)
    ]
    done = images * pieces
    cot_loads = [
        load(done + b, cot_h.at[b], cot.at[pl.ds(b * tokens, tokens)]) for b in range(images)
    ]
    done += images
    weight_loads = [load(done, w1_h.at[0], w1), load(done + 1, w2_h.at[0], w2)]
    barrier = pltpu.get_barrier_semaphore()

    def greet(p, ee, device):
        pl.semaphore_signal(barrier, inc=1, device_id=device, device_id_type=MESH)

    each_partner(greet)
    for far in (zh, 1 - zh):
        pl.semaphore_signal(
            barrier, inc=1, device_id={"dp": far * 2 + 1 - core, "expert": ex}, device_id_type=MESH
        )

    for one in tok_loads:
        one.start()

    key_rows = keys_ref[...].astype(F32)
    kt[...] = key_rows
    keysn[...] = (
        key_rows * lax.rsqrt(jnp.sum(key_rows * key_rows, axis=1, keepdims=True) + EPS)
    ).astype(BF16)

    for b in range(images):
        rows = pl.ds(b * tokens, tokens)
        for p in range(pieces):
            tok_loads[b * pieces + p].wait()
            if b == 0 and p == 0:
                for one in (*cot_loads, *weight_loads):
                    one.start()
            for i in range(p * piece // 128, (p + 1) * piece // 128):
                accs = []
                for r in range(i * 128, (i + 1) * 128, 32):
                    part = tok[b * tokens + r : b * tokens + r + 32, :].astype(F32)
                    square = part * part
                    acc = square[:, :128]
                    for j in range(1, width // 128):
                        acc = acc + square[:, j * 128 : (j + 1) * 128]
                    accs.append(acc)
                    down = lax.rsqrt(jnp.sum(acc, axis=1, keepdims=True) + EPS)
                    normed[r : r + 32, :] = (part * down).astype(BF16)
                acc = jnp.concatenate(accs, axis=0)
                rinv_s[b, :, i * 128 : (i + 1) * 128] = lax.rsqrt(
                    jnp.sum(acc.T, axis=0, keepdims=True) + EPS
                )
        logits = dot(keysn[...], normed[...], NT) * scale
        expo = jnp.exp(logits)
        disp = expo / jnp.sum(expo, axis=1, keepdims=True)
        comb = expo / jnp.sum(expo, axis=0, keepdims=True)
        logit_s[b] = logits
        disp_s[b] = disp
        comb_s[b] = comb
        disp_b = disp.astype(BF16)
        at[b, experts:, :] = disp_b
        spread = selector(images * experts, experts, images, b)
        mix_in[:, rows] = dot(spread, disp_b).astype(BF16)
        mix_grad[:, rows] = dot(spread, comb.astype(BF16)).astype(BF16)

    def remote(src, dst, send, recv, device):
        return pltpu.make_async_remote_copy(
            src_ref=src, dst_ref=dst, send_sem=send, recv_sem=recv,
            device_id=device, device_id_type=MESH,
        )

    def pack(rows_ref, start, blocks_ref, first, count):
        for i in range(count):
            rows_ref[start + i * images : start + (i + 1) * images, :] = blocks_ref[first + i]

    def out_of_experts(kind, out_ref, in_ref):
        def one(p, ee, device):
            remote(
                out_ref.at[ee], in_ref.at[p], send_sem.at[kind], in_sem.at[kind, p // layer], device
            ).start()

        each_partner(one)
        in_ref[0] = out_ref[ex]

    def unpack(blocks_ref, value):
        for i in range(experts):
            blocks_ref[i] = value[i * images : (i + 1) * images, :]

    unpack(send_in, dot(mix_in[...], tok[...]).astype(BF16))
    pl.semaphore_wait(barrier, near + 1)
    out_of_experts(0, send_in, recv_in)
    for one in cot_loads:
        one.wait()
    unpack(send_grad, dot(mix_grad[...], cot[...]).astype(BF16))

    def arrive(kind, in_ref, rows_ref):
        copies = []
        for group in range(ny):
            count = layer if group else layer - 1
            wait_for(in_ref.at[pl.ds(0, count)], in_sem.at[kind, group])
            pack(rows_ref, group * layer * images, in_ref, group * layer, layer)
            mine = pl.ds(group * layer * images, layer * images)
            theirs = pl.ds(half + group * layer * images, layer * images)
            copies.append(
                remote(
                    rows_ref.at[mine], rows_ref.at[theirs],
                    part_sem.at[kind, group], twin_sem.at[kind, group], twin,
                )
            )
            copies[-1].start()
        return copies

    copies_in = arrive(0, recv_in, x)
    out_of_experts(1, send_grad, recv_grad)
    for one in weight_loads:
        one.wait()
    for one in copies_in:
        one.wait_recv()

    step = min(256, hidden)

    def first(j, carry):
        cols = pl.ds(pl.multiple_of(j * step, step), step)
        pre = dot(x[...], w1[:, cols])
        cdf = 0.5 * (1.0 + lax.erf(pre * 0.7071067811865476))
        act[:, cols] = (pre * cdf).astype(BF16)
        slope[:, cols] = cdf + pre * jnp.exp(-0.5 * pre * pre) * 0.3989422804014327
        return carry

    lax.fori_loop(0, hidden // step, first, 0, unroll=2)

    wide = min(256, width)
    parts = -(-width // wide)

    def columns(j):
        return pl.ds(pl.multiple_of(jnp.minimum(j * wide, width - wide), 128), wide)

    def pair_copy(kind, j, src, dst):
        return remote(src.at[j], dst.at[j], send_sem.at[4 + kind], recv_sem.at[4 + kind], twin)

    def second(j, carry):
        res = dot(act[...], w2[:, columns(j)])
        pair_out[j] = res[half:].astype(BF16)
        pair_copy(0, j, pair_out, pair_out_r).start()
        own_out[j] = res[:half]
        return carry

    lax.fori_loop(0, parts, second, 0)

    def third(j, carry):
        cols = pl.ds(pl.multiple_of(j * step, step), step)
        pg[:, cols] = (dot(gs[...], w2[cols, :], NT) * slope[:, cols]).astype(BF16)
        return carry

    def chip_sums(kind, own, pair_r, rows_ref, out_ref, in_ref):
        wait_for(pair_r, recv_sem.at[4 + kind])
        for j in range(parts):
            start = min(j * wide, width - wide)
            rows_ref[:, start : start + wide] = (own[j] + pair_r[j].astype(F32)).astype(BF16)
        def one(p, ee, device):
            if p % layer == 1:
                for i in range(p, min(p + layer, near)):
                    out_ref[i] = rows_ref[i * images : (i + 1) * images, :]
            remote(
                out_ref.at[p], in_ref.at[p], send_sem.at[2 + kind], in_sem.at[2 + kind, p // layer],
                device,
            ).start()

        each_partner(one, -1)
        in_ref[0] = rows_ref[:images, :]

    chip_sums(0, own_out, pair_out_r, rows_out, send_out, recv_out)
    copies_grad = arrive(1, recv_grad, gs)
    for one in copies_grad:
        one.wait_recv()
    lax.fori_loop(0, hidden // step, third, 0, unroll=2)

    def fourth(j, carry):
        res = dot(pg[...], w1[columns(j), :], NT)
        pair_back[j] = res[half:].astype(BF16)
        pair_copy(1, j, pair_back, pair_back_r).start()
        own_back[j] = res[:half]
        return carry

    lax.fori_loop(0, parts, fourth, 0)
    chip_sums(1, own_back, pair_back_r, rows_bk, send_bk, recv_bk)

    def turn(src, dst, size):
        same = selector(wide, wide, 1, 0)

        def one(j, carry):
            cols = pl.ds(pl.multiple_of(jnp.minimum(j * wide, size - wide), 128), wide)
            dst[cols, :] = dot(same, src[:, cols], NT).astype(BF16)
            return carry

        lax.fori_loop(0, -(-size // wide), one, 0)

    def product(left, right, out, size):
        def one(j, carry):
            rows = pl.ds(pl.multiple_of(j * size, 16), size)
            out[0, rows, :] = dot(left[rows, :], right[...]).astype(BF16)
            return carry

        lax.fori_loop(0, left.shape[0] // size, one, 0)

    turn(act, actt, hidden)
    product(actt, gs, go_o, hidden // 4)
    def collect(kind, in_ref, rows_ref):
        for group in range(ny):
            count = layer if group else layer - 1
            wait_for(in_ref.at[pl.ds(0, count)], in_sem.at[2 + kind, group])
            pack(rows_ref, group * layer * images, in_ref, group * layer, layer)

    i = lax.broadcasted_iota(jnp.int32, (images * experts, half), 0)
    j = lax.broadcasted_iota(jnp.int32, (1, half), 1)
    place = jnp.full((1, half), ex, jnp.int32)
    for p, offset in enumerate(offsets):
        place = jnp.where(j // images == p, device_at(*offset)[0], place)
    wanted = i == place + j % images * experts
    gather = jnp.where(wanted, 1.0, 0.0).astype(BF16)

    def gathered(rows_ref):
        return dot(gather, rows_ref[...]).astype(BF16)

    collect(0, recv_out, rows_out)
    slot_out = gathered(rows_out)
    parts_lg = []
    for b in range(images):
        rows = pl.ds(b * tokens, tokens)
        comb_grad = dot(slot_out[b * experts : (b + 1) * experts], cot[rows, :], NT)
        comb = comb_s[b]
        parts_lg.append(comb * (comb_grad - jnp.sum(comb * comb_grad, axis=0, keepdims=True)))

    collect(1, recv_bk, rows_bk)
    slot_back = gathered(rows_bk)
    keys_grad = None
    for b in range(images):
        rows = pl.ds(b * tokens, tokens)
        back = slot_back[b * experts : (b + 1) * experts]
        mix_b[b, :experts, :] = keysn[...]
        mix_b[b, experts:, :] = back
        disp_grad = dot(back, tok[rows, :], NT)
        disp = disp_s[b]
        lg = parts_lg[b] + disp * (disp_grad - jnp.sum(disp * disp_grad, axis=1, keepdims=True))
        rinv = rinv_s[b]
        scaled = (lg * (scale * rinv)).astype(BF16)
        at[b, :experts, :] = scaled
        mix_c[b] = rinv * rinv * jnp.sum(lg * logit_s[b], axis=0, keepdims=True)
        term = dot(scaled, tok[rows, :])
        keys_grad = term if keys_grad is None else keys_grad + term

    for e in range(experts):
        key_send[e] = keys_grad[e : e + 1, :]

    for dy, dx, dz in spread_offsets((ny, nx, nz))[1:]:
        ee = (ys[dy] + xs[dx]) * nz + z_ex[dz]
        remote(
            key_send.at[ee], key_recv.at[ex], send_sem.at[6], recv_sem.at[6],
            {"dp": dp, "expert": ee},
        ).start()
    key_recv[ex] = key_send[ex]
    most = pl.ds(0, experts - 1)

    per = min(256, tokens)

    def token_grads(b):
        def one(j, carry):
            cut = pl.ds(pl.multiple_of(j * per, per), per)
            rows = pl.ds(pl.multiple_of(b * tokens + j * per, per), per)
            res = dot(at[b, :, cut], mix_b[b], TN)
            col = jnp.broadcast_to(mix_c[b, :, cut], (128, per)).T
            for k in range(width // 128):
                cols = slice(k * 128, (k + 1) * 128)
                gt_o[b, cut, cols] = (res[:, cols] - tok[rows, cols].astype(F32) * col).astype(BF16)
            return carry

        lax.fori_loop(0, tokens // per, one, 0)

    turn(x, xt, width)
    product(xt, pg, gi_o, width // 4)
    for b in range(images // 2):
        token_grads(b)
    wait_for(key_recv.at[most], recv_sem.at[6])
    total = key_recv[0]
    for e in range(1, experts):
        total = total + key_recv[e]
    key_tot[dp] = total
    for k in range(1, 4):
        remote(
            key_tot.at[dp], key_tot.at[dp], send_sem.at[7], recv_sem.at[7],
            {"dp": (dp + k) % 4, "expert": ex},
        ).start()
    for b in range(images // 2, images):
        token_grads(b)
    wait_for(key_tot.at[pl.ds(0, 3)], recv_sem.at[7])
    grad = (key_tot[0] + key_tot[1]) + (key_tot[2] + key_tot[3])
    own = kt[pl.ds(ex, 1), :]
    r = lax.rsqrt(jnp.sum(own * own, axis=1, keepdims=True) + EPS)
    gk_o[...] = grad * r - own * (r * r * r * jnp.sum(grad * own, axis=1, keepdims=True))

    some = pl.ds(0, near - 1)
    for kind, ref in enumerate((recv_in, recv_grad, recv_out, recv_bk)):
        wait_for(ref.at[some], send_sem.at[kind])
    wait_for(pair_out, send_sem.at[4])
    wait_for(pair_back, send_sem.at[5])
    for one in copies_in + copies_grad:
        one.wait_send()
    wait_for(key_recv.at[most], send_sem.at[6])
    wait_for(key_tot.at[pl.ds(0, 3)], send_sem.at[7])


def slots(sizes, tokens, cotangents, w_in, w_out, keys, scale):
    images, toks, width, experts, hidden, ny, nx, nz = sizes
    near = 2 * experts
    rows = near * images * 2
    half = near * images
    wide = min(256, width)
    parts = -(-width // wide)
    vmem = pltpu.VMEM
    dma = pltpu.SemaphoreType.DMA
    any_space = pl.BlockSpec(memory_space=pl.ANY)
    local = pl.BlockSpec(memory_space=pltpu.VMEM)
    flops = 2 * rows * width * hidden * 4
    return pl.pallas_call(
        functools.partial(slot_kernel, sizes),
        out_shape=(
            vmem((images, toks, width), BF16),
            vmem((1, width, hidden), BF16),
            vmem((1, hidden, width), BF16),
            vmem((1, width), F32),
        ),
        in_specs=[any_space] * 4 + [local, pl.BlockSpec(memory_space=pltpu.SMEM)],
        out_specs=(local,) * 4,
        scratch_shapes=[
            vmem((images * toks, width), BF16),
            vmem((images * toks, width), BF16),
            vmem((width, hidden), BF16),
            vmem((hidden, width), BF16),
            vmem((images, 2 * experts, toks), BF16),
            vmem((images, 2 * experts, width), BF16),
            vmem((images, 1, toks), F32),
            vmem((experts, width), F32),
            vmem((experts, width), BF16),
            vmem((toks, width), BF16),
            vmem((images, 1, toks), F32),
            vmem((images, experts, toks), F32),
            vmem((images, experts, toks), F32),
            vmem((images, experts, toks), F32),
            vmem((images * experts, images * toks), BF16),
            vmem((images * experts, images * toks), BF16),
            vmem((experts, images, width), BF16),
            vmem((experts, images, width), BF16),
            vmem((near, images, width), BF16),
            vmem((near, images, width), BF16),
            vmem((rows, width), BF16),
            vmem((rows, width), BF16),
            vmem((rows, hidden), BF16),
            vmem((rows, hidden), F32),
            vmem((rows, hidden), BF16),
            vmem((width, rows), BF16),
            vmem((hidden, rows), BF16),
            vmem((parts, half, wide), F32),
            vmem((parts, half, wide), F32),
            vmem((parts, half, wide), BF16),
            vmem((parts, half, wide), BF16),
            vmem((parts, half, wide), BF16),
            vmem((parts, half, wide), BF16),
            vmem((near, images, width), BF16),
            vmem((near, images, width), BF16),
            vmem((near, images, width), BF16),
            vmem((near, images, width), BF16),
            vmem((half, width), BF16),
            vmem((half, width), BF16),
            vmem((experts, 1, width), F32),
            vmem((experts, 1, width), F32),
            vmem((4, 1, width), F32),
            dma((3 * images + 2,)),
            dma((8,)),
            dma((8,)),
            dma((4, ny)),
            dma((2, ny)),
            dma((2, ny)),
        ],
        compiler_params=pltpu.CompilerParams(
            collective_id=0, has_side_effects=True, vmem_limit_bytes=44 * 1024 * 1024
        ),
        cost_estimate=pl.CostEstimate(
            flops=flops, bytes_accessed=4 * images * toks * width * 2, transcendentals=0
        ),
        name="slots",
    )(tokens, cotangents, w_in, w_out, keys, scale)


def store_kernel(gt, gi, go, gk, gt_h, gi_h, go_h, gk_h, sem):
    copies = []
    for src, dst in ((gi, gi_h), (go, go_h), (gt, gt_h), (gk, gk_h)):
        if len(src.shape) == 2:
            cuts = [(slice(None),)]
        elif src.shape[0] == 1:
            size = src.shape[1] // 4
            cuts = [(0, pl.ds(k * size, size)) for k in range(4)]
        else:
            cuts = [(k,) for k in range(src.shape[0])]
        for cut in cuts:
            copies.append(pltpu.make_async_copy(src.at[cut], dst.at[cut], sem.at[len(copies)]))
            copies[-1].start()
    for one in copies:
        one.wait()


def stored(*arrays):
    shape = jax.ShapeDtypeStruct
    return pl.pallas_call(
        store_kernel,
        out_shape=tuple(shape(one.shape, one.dtype) for one in arrays),
        in_specs=[pl.BlockSpec(memory_space=pltpu.VMEM)] * 4,
        out_specs=(pl.BlockSpec(memory_space=pl.ANY),) * 4,
        scratch_shapes=[pltpu.SemaphoreType.DMA((9 + arrays[0].shape[0],))],
        compiler_params=pltpu.CompilerParams(vmem_limit_bytes=4 * 1024 * 1024),
        cost_estimate=pl.CostEstimate(
            flops=0, bytes_accessed=2 * sum(one.size for one in arrays), transcendentals=0
        ),
        name="stored",
    )(*arrays)


def body(grid, tokens, slot_keys, logit_scale, w_in, w_out, grad_out):
    images, toks, width = tokens.shape
    sizes = (images, toks, width, slot_keys.shape[1], w_in.shape[2], *grid)
    gt, gi, go, gk = slots(sizes, tokens, grad_out, w_in, w_out, slot_keys.T, logit_scale)
    gt, gi, go, gk = stored(gt, gi, go, gk)
    return gt, gi, go, gk.reshape(width, 1)


def solution(mesh):
    experts = mesh.shape["expert"]
    nz = 2
    side = math.isqrt(experts // nz)
    grid = (experts // nz // side, side, nz)
    in_specs = (
        P(("dp", "expert"), None, None),
        P(),
        P(),
        P("expert", None, "dp"),
        P("expert", "dp", None),
        P(("dp", "expert"), None, None),
    )
    out_specs = (
        P(("dp", "expert"), None, None),
        P("expert", None, "dp"),
        P("expert", "dp", None),
        P(None, "expert"),
    )
    return jax.shard_map(
        functools.partial(body, grid),
        mesh=mesh,
        in_specs=in_specs,
        out_specs=out_specs,
        check_vma=False,
    )
```

```python
import functools
import math

import jax
import jax.numpy as jnp
from jax import lax
from jax.experimental import pallas as pl
from jax.experimental.pallas import tpu as pltpu
from jax.sharding import PartitionSpec as P

EPS = 1e-06
MESH = pl.DeviceIdType.MESH
F32 = jnp.float32
BF16 = jnp.bfloat16
NN = (((1,), (0,)), ((), ()))
NT = (((1,), (1,)), ((), ()))
TN = (((0,), (0,)), ((), ()))


def dot(a, b, dims=NN):
    return lax.dot_general(a, b, dims, preferred_element_type=F32)


def selector(rows, cols, stride, offset):
    i = lax.broadcasted_iota(jnp.int32, (rows, cols), 0)
    j = lax.broadcasted_iota(jnp.int32, (rows, cols), 1)
    return jnp.where(i == j * stride + offset, 1.0, 0.0).astype(BF16)


def wait_for(ref, sem):
    pltpu.make_async_copy(ref, ref, sem).wait()


def spread_offsets(dims):
    left = [
        (a, b, c) for a in range(dims[0]) for b in range(dims[1]) for c in range(dims[2])
    ][1:]
    share = {}
    for one in left:
        for kind in enumerate(one):
            share[kind] = share.get(kind, 0) + 1
    order, used, total = [(0, 0, 0)], dict.fromkeys(share, 0), len(left)
    while left:
        at = len(order)

        def uneven(one):
            taken = set(enumerate(one))
            return sum(
                (used[k] + (k in taken) - share[k] * at / total) ** 2 * (2 if k[1] else 1)
                for k in share
            )

        best = min(left, key=lambda one: (round(uneven(one), 9), one))
        left.remove(best)
        order.append(best)
        for kind in enumerate(best):
            used[kind] += 1
    near = lambda one: sum(min(d, n - d) for d, n in zip(one, dims))
    return order[:1] + sorted(order[1:], key=near, reverse=True)


def slot_kernel(
    sizes,
    tok_h, cot_h, w1_h, w2_h, keys_ref, scale_ref,
    gt_o, gi_o, go_o, gk_o,
    tok, cot, w1, w2, at, mix_b, mix_c,
    kt, keysn, normed, rinv_s, logit_s, disp_s, comb_s, mix_in, mix_grad,
    send_in, send_grad, recv_in, recv_grad,
    x, gs, act, slope, pg, xt, actt,
    own_out, own_back, pair_out, pair_back, pair_out_r, pair_back_r,
    send_out, send_bk, recv_out, recv_bk, rows_out, rows_bk,
    key_send, key_recv, key_tot,
    load_sem, send_sem, recv_sem, in_sem, twin_sem, part_sem,
):
    images, tokens, width, experts, hidden, ny, nx, nz = sizes
    layer = 2 * nx * nz
    near = ny * layer
    half = near * images
    scale = scale_ref[0]
    dp = lax.axis_index("dp")
    ex = lax.axis_index("expert")
    zh, core = dp // 2, dp % 2
    px, py = (ex // nz) % nx, ex // (nz * nx)
    pz = zh * nz + ex % nz
    twin = {"dp": zh * 2 + 1 - core, "expert": ex}

    zs = [(pz + d) % (2 * nz) for d in range(2 * nz)]
    xs = [(px + d) % nx for d in range(nx)]
    ys = [(py + d) % ny * nx for d in range(ny)]
    z_dp = [z // nz * 2 + core for z in zs]
    z_ex = [z % nz for z in zs]

    offsets = spread_offsets((ny, nx, 2 * nz))

    def device_at(dy, dx, dz):
        dz = dz % (2 * nz)
        ee = (ys[dy % ny] + xs[dx % nx]) * nz + z_ex[dz]
        return ee, {"dp": z_dp[dz], "expert": ee}

    def each_partner(body, sign=1):
        for p, (dy, dx, dz) in enumerate(offsets):
            if p:
                body(p, *device_at(sign * dy, sign * dx, sign * dz))

    def load(index, src, dst):
        return pltpu.make_async_copy(src, dst, load_sem.at[index])

    pieces = 2
    piece = tokens // pieces
    tok_loads = [
        load(
            b * pieces + p, tok_h.at[b, pl.ds(p * piece, piece)],
            tok.at[pl.ds(b * tokens + p * piece, piece)],
        )
        for b in range(images)
        for p in range(pieces)
    ]
    done = images * pieces
    cot_loads = [
        load(done + b, cot_h.at[b], cot.at[pl.ds(b * tokens, tokens)]) for b in range(images)
    ]
    done += images
    weight_loads = [load(done, w1_h.at[0], w1), load(done + 1, w2_h.at[0], w2)]
    barrier = pltpu.get_barrier_semaphore()

    def greet(p, ee, device):
        pl.semaphore_signal(barrier, inc=1, device_id=device, device_id_type=MESH)

    each_partner(greet)
    for far in (zh, 1 - zh):
        pl.semaphore_signal(
            barrier, inc=1, device_id={"dp": far * 2 + 1 - core, "expert": ex}, device_id_type=MESH
        )

    for one in tok_loads:
        one.start()

    key_rows = keys_ref[...].astype(F32)
    kt[...] = key_rows
    keysn[...] = (
        key_rows * lax.rsqrt(jnp.sum(key_rows * key_rows, axis=1, keepdims=True) + EPS)
    ).astype(BF16)

    for b in range(images):
        rows = pl.ds(b * tokens, tokens)
        for p in range(pieces):
            tok_loads[b * pieces + p].wait()
            if b == 0 and p == 0:
                for one in (*cot_loads, *weight_loads):
                    one.start()
            for i in range(p * piece // 128, (p + 1) * piece // 128):
                accs = []
                for r in range(i * 128, (i + 1) * 128, 32):
                    part = tok[b * tokens + r : b * tokens + r + 32, :].astype(F32)
                    square = part * part
                    acc = square[:, :128]
                    for j in range(1, width // 128):
                        acc = acc + square[:, j * 128 : (j + 1) * 128]
                    accs.append(acc)
                    down = lax.rsqrt(jnp.sum(acc, axis=1, keepdims=True) + EPS)
                    normed[r : r + 32, :] = (part * down).astype(BF16)
                acc = jnp.concatenate(accs, axis=0)
                rinv_s[b, :, i * 128 : (i + 1) * 128] = lax.rsqrt(
                    jnp.sum(acc.T, axis=0, keepdims=True) + EPS
                )
        logits = dot(keysn[...], normed[...], NT) * scale
        expo = jnp.exp(logits)
        disp = expo / jnp.sum(expo, axis=1, keepdims=True)
        comb = expo / jnp.sum(expo, axis=0, keepdims=True)
        logit_s[b] = logits
        disp_s[b] = disp
        comb_s[b] = comb
        disp_b = disp.astype(BF16)
        at[b, experts:, :] = disp_b
        spread = selector(images * experts, experts, images, b)
        mix_in[:, rows] = dot(spread, disp_b).astype(BF16)
        mix_grad[:, rows] = dot(spread, comb.astype(BF16)).astype(BF16)

    def remote(src, dst, send, recv, device):
        return pltpu.make_async_remote_copy(
            src_ref=src, dst_ref=dst, send_sem=send, recv_sem=recv,
            device_id=device, device_id_type=MESH,
        )

    def pack(rows_ref, start, blocks_ref, first, count):
        for i in range(count):
            rows_ref[start + i * images : start + (i + 1) * images, :] = blocks_ref[first + i]

    def out_of_experts(kind, out_ref, in_ref):
        def one(p, ee, device):
            remote(
                out_ref.at[ee], in_ref.at[p], send_sem.at[kind], in_sem.at[kind, p // layer], device
            ).start()

        each_partner(one)
        in_ref[0] = out_ref[ex]

    def unpack(blocks_ref, value):
        for i in range(experts):
            blocks_ref[i] = value[i * images : (i + 1) * images, :]

    unpack(send_in, dot(mix_in[...], tok[...]).astype(BF16))
    pl.semaphore_wait(barrier, near + 1)
    out_of_experts(0, send_in, recv_in)
    for one in cot_loads:
        one.wait()
    unpack(send_grad, dot(mix_grad[...], cot[...]).astype(BF16))
    out_of_experts(1, send_grad, recv_grad)

    def arrive(kind, in_ref, rows_ref):
        copies = []
        for group in reversed(range(ny)):
            count = layer if group else layer - 1
            wait_for(in_ref.at[pl.ds(0, count)], in_sem.at[kind, group])
            pack(rows_ref, group * layer * images, in_ref, group * layer, layer)
            mine = pl.ds(group * layer * images, layer * images)
            theirs = pl.ds(half + group * layer * images, layer * images)
            copies.append(
                remote(
                    rows_ref.at[mine], rows_ref.at[theirs],
                    part_sem.at[kind, group], twin_sem.at[kind, group], twin,
                )
            )
            copies[-1].start()
        return copies

    copies_in = arrive(0, recv_in, x)
    for one in weight_loads:
        one.wait()
    for one in copies_in:
        one.wait_recv()

    step = min(256, hidden)

    def first(j, carry):
        cols = pl.ds(pl.multiple_of(j * step, step), step)
        pre = dot(x[...], w1[:, cols])
        cdf = 0.5 * (1.0 + lax.erf(pre * 0.7071067811865476))
        act[:, cols] = (pre * cdf).astype(BF16)
        slope[:, cols] = cdf + pre * jnp.exp(-0.5 * pre * pre) * 0.3989422804014327
        return carry

    lax.fori_loop(0, hidden // step, first, 0, unroll=2)

    wide = min(256, width)
    parts = -(-width // wide)

    def columns(j):
        return pl.ds(pl.multiple_of(jnp.minimum(j * wide, width - wide), 128), wide)

    def pair_copy(kind, j, src, dst):
        return remote(src.at[j], dst.at[j], send_sem.at[4 + kind], recv_sem.at[4 + kind], twin)

    def second(j, carry):
        res = dot(act[...], w2[:, columns(j)])
        pair_out[j] = res[half:].astype(BF16)
        pair_copy(0, j, pair_out, pair_out_r).start()
        own_out[j] = res[:half]
        return carry

    lax.fori_loop(0, parts, second, 0)

    copies_grad = arrive(1, recv_grad, gs)

    def third(j, carry):
        cols = pl.ds(pl.multiple_of(j * step, step), step)
        pg[:, cols] = (dot(gs[...], w2[cols, :], NT) * slope[:, cols]).astype(BF16)
        return carry

    def chip_sums(kind, own, pair_r, rows_ref, out_ref, in_ref):
        wait_for(pair_r, recv_sem.at[4 + kind])
        for j in range(parts):
            start = min(j * wide, width - wide)
            rows_ref[:, start : start + wide] = (own[j] + pair_r[j].astype(F32)).astype(BF16)
        def one(p, ee, device):
            if p % layer == 1:
                for i in range(p, min(p + layer, near)):
                    out_ref[i] = rows_ref[i * images : (i + 1) * images, :]
            remote(
                out_ref.at[p], in_ref.at[p], send_sem.at[2 + kind], in_sem.at[2 + kind, p // layer],
                device,
            ).start()

        each_partner(one, -1)
        in_ref[0] = rows_ref[:images, :]

    chip_sums(0, own_out, pair_out_r, rows_out, send_out, recv_out)
    for one in copies_grad:
        one.wait_recv()
    lax.fori_loop(0, hidden // step, third, 0, unroll=2)

    def fourth(j, carry):
        res = dot(pg[...], w1[columns(j), :], NT)
        pair_back[j] = res[half:].astype(BF16)
        pair_copy(1, j, pair_back, pair_back_r).start()
        own_back[j] = res[:half]
        return carry

    lax.fori_loop(0, parts, fourth, 0)
    chip_sums(1, own_back, pair_back_r, rows_bk, send_bk, recv_bk)

    def turn(src, dst, size):
        same = selector(wide, wide, 1, 0)

        def one(j, carry):
            cols = pl.ds(pl.multiple_of(jnp.minimum(j * wide, size - wide), 128), wide)
            dst[cols, :] = dot(same, src[:, cols], NT).astype(BF16)
            return carry

        lax.fori_loop(0, -(-size // wide), one, 0)

    def product(left, right, out, size):
        def one(j, carry):
            rows = pl.ds(pl.multiple_of(j * size, 16), size)
            out[0, rows, :] = dot(left[rows, :], right[...]).astype(BF16)
            return carry

        lax.fori_loop(0, left.shape[0] // size, one, 0)

    turn(act, actt, hidden)
    product(actt, gs, go_o, hidden // 4)
    def collect(kind, in_ref, rows_ref):
        for group in reversed(range(ny)):
            count = layer if group else layer - 1
            wait_for(in_ref.at[pl.ds(0, count)], in_sem.at[2 + kind, group])
            pack(rows_ref, group * layer * images, in_ref, group * layer, layer)

    i = lax.broadcasted_iota(jnp.int32, (images * experts, half), 0)
    j = lax.broadcasted_iota(jnp.int32, (1, half), 1)
    place = jnp.full((1, half), ex, jnp.int32)
    for p, offset in enumerate(offsets):
        place = jnp.where(j // images == p, device_at(*offset)[0], place)
    wanted = i == place + j % images * experts
    gather = jnp.where(wanted, 1.0, 0.0).astype(BF16)

    def gathered(rows_ref):
        return dot(gather, rows_ref[...]).astype(BF16)

    collect(0, recv_out, rows_out)
    slot_out = gathered(rows_out)
    parts_lg = []
    for b in range(images):
        rows = pl.ds(b * tokens, tokens)
        comb_grad = dot(slot_out[b * experts : (b + 1) * experts], cot[rows, :], NT)
        comb = comb_s[b]
        parts_lg.append(comb * (comb_grad - jnp.sum(comb * comb_grad, axis=0, keepdims=True)))

    collect(1, recv_bk, rows_bk)
    slot_back = gathered(rows_bk)
    keys_grad = None
    for b in range(images):
        rows = pl.ds(b * tokens, tokens)
        back = slot_back[b * experts : (b + 1) * experts]
        mix_b[b, :experts, :] = keysn[...]
        mix_b[b, experts:, :] = back
        disp_grad = dot(back, tok[rows, :], NT)
        disp = disp_s[b]
        lg = parts_lg[b] + disp * (disp_grad - jnp.sum(disp * disp_grad, axis=1, keepdims=True))
        rinv = rinv_s[b]
        scaled = (lg * (scale * rinv)).astype(BF16)
        at[b, :experts, :] = scaled
        mix_c[b] = rinv * rinv * jnp.sum(lg * logit_s[b], axis=0, keepdims=True)
        term = dot(scaled, tok[rows, :])
        keys_grad = term if keys_grad is None else keys_grad + term

    for e in range(experts):
        key_send[e] = keys_grad[e : e + 1, :]

    for dy, dx, dz in spread_offsets((ny, nx, nz))[1:]:
        ee = (ys[dy] + xs[dx]) * nz + z_ex[dz]
        remote(
            key_send.at[ee], key_recv.at[ex], send_sem.at[6], recv_sem.at[6],
            {"dp": dp, "expert": ee},
        ).start()
    key_recv[ex] = key_send[ex]
    most = pl.ds(0, experts - 1)

    per = min(256, tokens)

    def token_grads(b):
        def one(j, carry):
            cut = pl.ds(pl.multiple_of(j * per, per), per)
            rows = pl.ds(pl.multiple_of(b * tokens + j * per, per), per)
            res = dot(at[b, :, cut], mix_b[b], TN)
            col = jnp.broadcast_to(mix_c[b, :, cut], (128, per)).T
            for k in range(width // 128):
                cols = slice(k * 128, (k + 1) * 128)
                gt_o[b, cut, cols] = (res[:, cols] - tok[rows, cols].astype(F32) * col).astype(BF16)
            return carry

        lax.fori_loop(0, tokens // per, one, 0)

    turn(x, xt, width)
    product(xt, pg, gi_o, width // 4)
    for b in range(images // 2):
        token_grads(b)
    wait_for(key_recv.at[most], recv_sem.at[6])
    total = key_recv[0]
    for e in range(1, experts):
        total = total + key_recv[e]
    key_tot[dp] = total
    for k in range(1, 4):
        remote(
            key_tot.at[dp], key_tot.at[dp], send_sem.at[7], recv_sem.at[7],
            {"dp": (dp + k) % 4, "expert": ex},
        ).start()
    for b in range(images // 2, images):
        token_grads(b)
    wait_for(key_tot.at[pl.ds(0, 3)], recv_sem.at[7])
    grad = (key_tot[0] + key_tot[1]) + (key_tot[2] + key_tot[3])
    own = kt[pl.ds(ex, 1), :]
    r = lax.rsqrt(jnp.sum(own * own, axis=1, keepdims=True) + EPS)
    gk_o[...] = grad * r - own * (r * r * r * jnp.sum(grad * own, axis=1, keepdims=True))

    some = pl.ds(0, near - 1)
    for kind, ref in enumerate((recv_in, recv_grad, recv_out, recv_bk)):
        wait_for(ref.at[some], send_sem.at[kind])
    wait_for(pair_out, send_sem.at[4])
    wait_for(pair_back, send_sem.at[5])
    for one in copies_in + copies_grad:
        one.wait_send()
    wait_for(key_recv.at[most], send_sem.at[6])
    wait_for(key_tot.at[pl.ds(0, 3)], send_sem.at[7])


def slots(sizes, tokens, cotangents, w_in, w_out, keys, scale):
    images, toks, width, experts, hidden, ny, nx, nz = sizes
    near = 2 * experts
    rows = near * images * 2
    half = near * images
    wide = min(256, width)
    parts = -(-width // wide)
    vmem = pltpu.VMEM
    dma = pltpu.SemaphoreType.DMA
    any_space = pl.BlockSpec(memory_space=pl.ANY)
    local = pl.BlockSpec(memory_space=pltpu.VMEM)
    flops = 2 * rows * width * hidden * 4
    return pl.pallas_call(
        functools.partial(slot_kernel, sizes),
        out_shape=(
            vmem((images, toks, width), BF16),
            vmem((1, width, hidden), BF16),
            vmem((1, hidden, width), BF16),
            vmem((1, width), F32),
        ),
        in_specs=[any_space] * 4 + [local, pl.BlockSpec(memory_space=pltpu.SMEM)],
        out_specs=(local,) * 4,
        scratch_shapes=[
            vmem((images * toks, width), BF16),
            vmem((images * toks, width), BF16),
            vmem((width, hidden), BF16),
            vmem((hidden, width), BF16),
            vmem((images, 2 * experts, toks), BF16),
            vmem((images, 2 * experts, width), BF16),
            vmem((images, 1, toks), F32),
            vmem((experts, width), F32),
            vmem((experts, width), BF16),
            vmem((toks, width), BF16),
            vmem((images, 1, toks), F32),
            vmem((images, experts, toks), F32),
            vmem((images, experts, toks), F32),
            vmem((images, experts, toks), F32),
            vmem((images * experts, images * toks), BF16),
            vmem((images * experts, images * toks), BF16),
            vmem((experts, images, width), BF16),
            vmem((experts, images, width), BF16),
            vmem((near, images, width), BF16),
            vmem((near, images, width), BF16),
            vmem((rows, width), BF16),
            vmem((rows, width), BF16),
            vmem((rows, hidden), BF16),
            vmem((rows, hidden), F32),
            vmem((rows, hidden), BF16),
            vmem((width, rows), BF16),
            vmem((hidden, rows), BF16),
            vmem((parts, half, wide), F32),
            vmem((parts, half, wide), F32),
            vmem((parts, half, wide), BF16),
            vmem((parts, half, wide), BF16),
            vmem((parts, half, wide), BF16),
            vmem((parts, half, wide), BF16),
            vmem((near, images, width), BF16),
            vmem((near, images, width), BF16),
            vmem((near, images, width), BF16),
            vmem((near, images, width), BF16),
            vmem((half, width), BF16),
            vmem((half, width), BF16),
            vmem((experts, 1, width), F32),
            vmem((experts, 1, width), F32),
            vmem((4, 1, width), F32),
            dma((3 * images + 2,)),
            dma((8,)),
            dma((8,)),
            dma((4, ny)),
            dma((2, ny)),
            dma((2, ny)),
        ],
        compiler_params=pltpu.CompilerParams(
            collective_id=0, has_side_effects=True, vmem_limit_bytes=44 * 1024 * 1024
        ),
        cost_estimate=pl.CostEstimate(
            flops=flops, bytes_accessed=4 * images * toks * width * 2, transcendentals=0
        ),
        name="slots",
    )(tokens, cotangents, w_in, w_out, keys, scale)


def store_kernel(gt, gi, go, gk, gt_h, gi_h, go_h, gk_h, sem):
    copies = []
    for src, dst in ((gi, gi_h), (go, go_h), (gt, gt_h), (gk, gk_h)):
        if len(src.shape) == 2:
            cuts = [(slice(None),)]
        elif src.shape[0] == 1:
            size = src.shape[1] // 4
            cuts = [(0, pl.ds(k * size, size)) for k in range(4)]
        else:
            cuts = [(k,) for k in range(src.shape[0])]
        for cut in cuts:
            copies.append(pltpu.make_async_copy(src.at[cut], dst.at[cut], sem.at[len(copies)]))
            copies[-1].start()
    for one in copies:
        one.wait()


def stored(*arrays):
    shape = jax.ShapeDtypeStruct
    return pl.pallas_call(
        store_kernel,
        out_shape=tuple(shape(one.shape, one.dtype) for one in arrays),
        in_specs=[pl.BlockSpec(memory_space=pltpu.VMEM)] * 4,
        out_specs=(pl.BlockSpec(memory_space=pl.ANY),) * 4,
        scratch_shapes=[pltpu.SemaphoreType.DMA((9 + arrays[0].shape[0],))],
        compiler_params=pltpu.CompilerParams(vmem_limit_bytes=4 * 1024 * 1024),
        cost_estimate=pl.CostEstimate(
            flops=0, bytes_accessed=2 * sum(one.size for one in arrays), transcendentals=0
        ),
        name="stored",
    )(*arrays)


def body(grid, tokens, slot_keys, logit_scale, w_in, w_out, grad_out):
    images, toks, width = tokens.shape
    sizes = (images, toks, width, slot_keys.shape[1], w_in.shape[2], *grid)
    gt, gi, go, gk = slots(sizes, tokens, grad_out, w_in, w_out, slot_keys.T, logit_scale)
    gt, gi, go, gk = stored(gt, gi, go, gk)
    return gt, gi, go, gk.reshape(width, 1)


def solution(mesh):
    experts = mesh.shape["expert"]
    nz = 2
    side = math.isqrt(experts // nz)
    grid = (experts // nz // side, side, nz)
    in_specs = (
        P(("dp", "expert"), None, None),
        P(),
        P(),
        P("expert", None, "dp"),
        P("expert", "dp", None),
        P(("dp", "expert"), None, None),
    )
    out_specs = (
        P(("dp", "expert"), None, None),
        P("expert", None, "dp"),
        P("expert", "dp", None),
        P(None, "expert"),
    )
    return jax.shard_map(
        functools.partial(body, grid),
        mesh=mesh,
        in_specs=in_specs,
        out_specs=out_specs,
        check_vma=False,
    )
```
